32 devices in a mesh: cube: 8 (over y, x, core), spec: 4 (over z).
Axes of the slice: x: 2, y: 2, z: 4, core: 2. Of those that a mesh axis runs over, the one named last changes fastest.
Arguments:
- tokens: bfloat16 [8, 1536, 768], P('cube', 'spec'), may hold values from -6 to 6
- cotangent: bfloat16 [8, 1536, 768], P('cube', 'spec'), may hold values from -24 to 24
- lengths: int32 [8], P('cube'), may hold values from 864 to 1536, as said below
- projection: bfloat16 [768, 2304], replicated, may hold values from -0.21875 to 0.21875
- query_bias: float32 [768], replicated, may hold values from -3 to 3
- value_bias: float32 [768], replicated, may hold values from -3 to 3
- output_weight: bfloat16 [768, 768], replicated, may hold values from -0.21875 to 0.21875
- output_bias: float32 [768], replicated, may hold values from -3 to 3
- up_weight: bfloat16 [768, 3072], replicated, may hold values from -0.21875 to 0.21875
- up_bias: float32 [3072], replicated, may hold values from -3 to 3
- down_weight: bfloat16 [3072, 768], replicated, may hold values from -0.109375 to 0.109375
- down_bias: float32 [768], replicated, may hold values from -3 to 3
- first_gain: float32 [768], replicated, may hold values from 0.1 to 1.9
- first_shift: float32 [768], replicated, may hold values from -3 to 3
- second_gain: float32 [768], replicated, may hold values from 0.1 to 1.9
- second_shift: float32 [768], replicated, may hold values from -3 to 3
Outputs:
- block_out: bfloat16 [8, 1536, 768], P('cube', 'spec')
- grad_tokens: float32 [8, 1536, 768], P('cube', 'spec')
- grad_projection: float32 [768, 2304], P('cube', 'spec')
- grad_query_bias: float32 [768], replicated
- grad_value_bias: float32 [768], replicated
- grad_output_weight: float32 [768, 768], P('cube', 'spec')
- grad_output_bias: float32 [768], replicated
- grad_up_weight: float32 [768, 3072], P('cube', 'spec')
- grad_up_bias: float32 [3072], replicated
- grad_down_weight: float32 [3072, 768], P('cube', 'spec')
- grad_down_bias: float32 [768], replicated
- grad_first_gain: float32 [768], replicated
- grad_first_shift: float32 [768], replicated
- grad_second_gain: float32 [768], replicated
- grad_second_shift: float32 [768], replicated
The draws below stay inside these ranges and needn't reach their ends.
Inputs may be any that keep to these rules, and one draw needn't show every extreme that they name: `lengths`: each cube's length is 1536 or 864, and both occur.
All inputs are finite; a program needn't handle non-finite values.
Results may differ from the reference program's by a relative error of at most 0.012.
Values may be sent and summed in bfloat16 or wider, within the bound.
No kernel may reach another device: no remote copies, remote signals or barrier semaphores. Data moves between devices by JAX's collectives and lax.ppermute only.
A program may use at most 192 MiB of HBM per device.

```python
import jax
import jax.numpy as jnp
from jax import lax

D = 768
HEADS = 12
HD = 64
FF = 3072
SEQ = 1536
CUBES = 8


def draw_lengths(key, part):
    picked = jax.random.randint(key, (CUBES,), 0, 128)
    position = jnp.arange(CUBES)
    longer = jnp.where(position == 0, True, jnp.where(position == 1, False, picked < 84))
    return jnp.where(longer, SEQ, 9 * SEQ // 16).astype(jnp.int32)


def draw_cotangent(key, part):
    first_key, second_key = jax.random.split(key)
    factor = jnp.exp(jax.random.uniform(first_key, (CUBES, 1, 1), jnp.float32, jnp.log(0.4), jnp.log(4.0)))
    basis = jnp.clip(jax.random.normal(second_key, (CUBES, SEQ, D), jnp.float32), -6.0, 6.0)
    return (basis * factor).astype(jnp.bfloat16)


def block_scale(key, dims, cuts, least, high):
    def one(dim, blocks):
        heights = jax.random.uniform(jax.random.fold_in(jax.random.fold_in(key, 6), dim), (blocks,), jnp.float32, least / len(cuts), high / len(cuts))
        return jnp.repeat(jnp.exp(heights), dims[dim] // blocks).reshape((-1,) + (1,) * (len(dims) - dim - 1))

    level = one(*cuts[0])
    for cut in cuts[1:]:
        level = level * one(*cut)
    return level


def scatter_about(stream_key, shape, spread, reach, pieces=(), dtype=jnp.bfloat16):
    values = jax.random.normal(stream_key, shape, jnp.float32) * spread
    if len(pieces) > 0:
        values = block_scale(stream_key, shape, pieces, -0.22, 0.18) * values
    return jnp.clip(values, min=-reach, max=reach).astype(dtype)


def setup_inputs(seed: int = 0) -> dict:
    seeds = jax.random.split(jax.random.key(seed), 17)
    return {
        "tokens": scatter_about(seeds[0], (CUBES, SEQ, D), 1.0, 6.0, ((0, 8), (1, 4))),
        "cotangent": draw_cotangent(jax.random.fold_in(seeds[16], 71), 0),
        "lengths": draw_lengths(jax.random.fold_in(seeds[16], 71), 0),
        "projection": scatter_about(seeds[3], (D, 3 * D), D ** -0.5, 0.21875),
        "query_bias": scatter_about(seeds[4], (D,), 0.5, 3.0, (), jnp.float32),
        "value_bias": scatter_about(seeds[5], (D,), 0.5, 3.0, (), jnp.float32),
        "output_weight": scatter_about(seeds[6], (D, D), D ** -0.5, 0.21875),
        "output_bias": scatter_about(seeds[7], (D,), 0.5, 3.0, (), jnp.float32),
        "up_weight": scatter_about(seeds[8], (D, FF), D ** -0.5, 0.21875),
        "up_bias": scatter_about(seeds[9], (FF,), 0.5, 3.0, (), jnp.float32),
        "down_weight": scatter_about(seeds[10], (FF, D), FF ** -0.5, 0.109375),
        "down_bias": scatter_about(seeds[11], (D,), 0.5, 3.0, (), jnp.float32),
        "first_gain": jnp.clip(1.0 + 0.18 * jax.random.normal(seeds[12], (D,), jnp.float32), 0.1, 1.9),
        "first_shift": scatter_about(seeds[13], (D,), 0.5, 3.0, (), jnp.float32),
        "second_gain": jnp.clip(1.0 + 0.18 * jax.random.normal(seeds[14], (D,), jnp.float32), 0.1, 1.9),
        "second_shift": scatter_about(seeds[15], (D,), 0.5, 3.0, (), jnp.float32),
    }


EPS = 1e-06
HIGH = lax.Precision.HIGHEST

@jax.custom_vjp
def low(v):
    return lax.optimization_barrier(v.astype(jnp.bfloat16)).astype(jnp.float32)

@jax.custom_vjp
def low_back(v):
    return v

def low_keep(v):
    return (low(v), None)

def low_pass(kept, grad):
    return (grad,)

def back_keep(v):
    return (v, None)

def back_low(kept, grad):
    return (low(grad),)
low.defvjp(low_keep, low_pass)
low_back.defvjp(back_keep, back_low)

def layer_norm(values, gain, shift):
    average = lax.optimization_barrier(jnp.mean(values, -1, keepdims=True))
    centred = values - average
    variance = lax.optimization_barrier(jnp.mean(centred * centred, -1, keepdims=True))
    return centred * lax.rsqrt(variance + EPS) * gain + shift

def matmul(left, right):
    return jnp.matmul(left, right, precision=HIGH)

def cube_layer(inputs, length, params):
    projection, query_bias, value_bias, output_weight, output_bias, up_weight, up_bias, down_weight, down_bias, first_gain, first_shift, second_gain, second_shift = params
    width = inputs.shape[-1]
    hidden_one = low(layer_norm(inputs, first_gain, first_shift))
    projected = matmul(hidden_one, projection)
    queries = low_back(low(projected[:, :width] + query_bias))
    all_keys = low_back(low(projected[:, width:2 * width]))
    values = low_back(low(projected[:, 2 * width:] + value_bias))
    positions = jnp.arange(inputs.shape[0])
    key_mask = positions < length
    scores = jnp.einsum('qhd,khd->hqk', queries.reshape(-1, HEADS, HD), all_keys.reshape(-1, HEADS, HD), precision=HIGH) * HD ** (-0.5)
    scores = jnp.where(key_mask[None, None, :], low_back(scores), -1e+30)
    softmaxed = low(jnp.exp(scores - jax.nn.logsumexp(scores, -1, keepdims=True)))
    attended = jnp.einsum('hqk,khd->qhd', softmaxed, values.reshape(-1, HEADS, HD), precision=HIGH).reshape(-1, width)
    attended = low_back(low(attended))
    middle = inputs + low_back(matmul(attended, output_weight) + output_bias)
    hidden_two = low(layer_norm(middle, second_gain, second_shift))
    before = low_back(matmul(hidden_two, up_weight) + up_bias)
    lifted = low(jax.nn.gelu(before, approximate=False))
    return middle + (matmul(lifted, down_weight) + down_bias)

def reference(tokens, cotangent, lengths, projection, query_bias, value_bias, output_weight, output_bias, up_weight, up_bias, down_weight, down_bias, first_gain, first_shift, second_gain, second_shift):
    params = tuple((argument.astype(jnp.float32) for argument in (projection, query_bias, value_bias, output_weight, output_bias, up_weight, up_bias, down_weight, down_bias, first_gain, first_shift, second_gain, second_shift)))
    inputs = tokens.astype(jnp.float32)

    def forward(layer_in, layer_params):

        def one_cube(members):
            return cube_layer(members[0], members[1], layer_params)
        return lax.map(jax.checkpoint(one_cube), (layer_in, lengths))
    result, pullback = jax.vjp(forward, inputs, params)
    grad_inputs, grads = pullback(cotangent.astype(jnp.float32))
    return (result.astype(jnp.bfloat16), grad_inputs, grads[0], grads[1], grads[2], grads[3], grads[4], grads[5], grads[6], grads[7], grads[8], grads[9], grads[10], grads[11], grads[12])
```

```python
import math
from functools import partial

import jax
import jax.numpy as jnp
import numpy as np
from jax import lax
from jax.experimental import pallas as pl
from jax.experimental.pallas import tpu as pltpu
from jax.sharding import PartitionSpec as P

HEADS = 12
HD = 64
PAIRS = HEADS // 2
EPS = 1e-06
SCALE = HD ** (-0.5)
TO_EXP2 = SCALE * math.log2(math.e)
MASKED = -1e30

BF = jnp.bfloat16
F32 = jnp.float32


def dot(left, right):
    return jnp.dot(left, right, preferred_element_type=F32)


def dot_nt(left, right):
    return lax.dot_general(left, right, (((1,), (1,)), ((), ())), preferred_element_type=F32)


def dot_tn(left, right):
    return lax.dot_general(left, right, (((0,), (0,)), ((), ())), preferred_element_type=F32)


def normalize(values):
    average = jnp.mean(values, -1, keepdims=True)
    centred = values - average
    inverse = lax.rsqrt(jnp.mean(centred * centred, -1, keepdims=True) + EPS)
    return centred * inverse, inverse


def transposed(values):
    return values.astype(F32).T


def params(megabytes):
    return pltpu.CompilerParams(vmem_limit_bytes=megabytes * 2**20)


def cost(flops, nbytes, trans=0):
    return pl.CostEstimate(flops=flops, bytes_accessed=nbytes, transcendentals=trans)


def extra_lanes(where_ref, rows, ones):
    slot = lax.broadcasted_iota(jnp.int32, (rows, 128), 0) + where_ref[0]
    lane = lax.broadcasted_iota(jnp.int32, (rows, 128), 1)
    masked = jnp.where(slot < where_ref[1], 0.0, MASKED)
    rest = jnp.where(lane <= ones, 1.0, 0.0)
    return jnp.where(lane == 0, masked, rest).astype(BF)


def two_heads(part, extra):
    n = part.shape[1]
    zero = jnp.zeros((HD, n), part.dtype)
    left = jnp.concatenate([part[:HD], zero], 0)
    right = jnp.concatenate([zero, part[HD:]], 0)
    return jnp.concatenate([jnp.concatenate([left, right], 1), extra], 0)


def pair_lanes(pair):
    return slice(pair * 2 * HD, (pair + 1) * 2 * HD)


def forward_kernel(first, last, *refs):
    if first:
        where_ref, tok_ref, gain_ref, shift_ref, w_ref, qb_ref, vb_ref = refs[:7]
        outs = refs[7:]
        h_out, k_out, v_out, m_out, l_out, acc_out, q_out, qt_out = outs
    else:
        where_ref, tok_ref, gain_ref, shift_ref, w_ref, vb_ref, qt_ref, m_ref, l_ref, acc_ref = refs[:10]
        h_out, k_out, v_out, m_out, l_out, acc_out = refs[10:]
    rows, width = tok_ref.shape
    normed, _ = normalize(tok_ref[...].astype(F32))
    hidden = (normed * gain_ref[...] + shift_ref[...]).astype(BF)
    h_out[...] = hidden
    k_out[...] = dot(hidden, w_ref[:, width : 2 * width]).astype(BF)
    values = dot(hidden, w_ref[:, 2 * width :]) + vb_ref[...]
    v_out[...] = values.astype(BF)
    values_t = v_out[...].astype(F32).T.astype(BF)
    if first:
        q_out[...] = (dot(hidden, w_ref[:, :width]) + qb_ref[...]).astype(BF)
        qt_out[...] = q_out[...].astype(F32).T.astype(BF)
        qt_ref = qt_out
    extra_keys = extra_lanes(where_ref, rows, 0)
    ones_row = (lax.broadcasted_iota(jnp.int32, (128, 2 * rows), 0) == 0).astype(BF)
    for pair in range(PAIRS):
        lanes = pair_lanes(pair)
        keys = jnp.concatenate([k_out[:, lanes], extra_keys], 1)
        scores = dot(keys, two_heads(qt_ref[lanes, :], ones_row))
        top = jnp.max(scores, 0, keepdims=True)
        if not first:
            before = m_ref[pair : pair + 1, :]
            top = jnp.maximum(top, before)
            fade = jnp.exp2((before - top) * TO_EXP2)
        weights = jnp.exp2((scores - top) * TO_EXP2)
        total = jnp.sum(weights, 0, keepdims=True)
        if not first:
            total = total + l_ref[pair : pair + 1, :] * fade
        both = dot(values_t[lanes, :], weights.astype(BF))
        for head in range(2):
            own = slice(lanes.start + head * HD, lanes.start + (head + 1) * HD)
            cols = slice(head * rows, (head + 1) * rows)
            part = both[head * HD : (head + 1) * HD, cols]
            if not first:
                part = part + acc_ref[own, :] * fade[:, cols]
            if last:
                part = part / total[:, cols]
            acc_out[own, :] = part
        if last:
            m_out[pair : pair + 1, :] = -(top + jnp.log2(total) * (1.0 / TO_EXP2))
        else:
            m_out[pair : pair + 1, :] = top
        l_out[pair : pair + 1, :] = total


def forward_step(first, last, where, tok, gain, shift, w, qb, vb, state):
    rows, width = tok.shape
    block = jax.ShapeDtypeStruct((rows, width), BF)
    outs = [
        block,
        block,
        block,
        jax.ShapeDtypeStruct((8, 2 * rows), F32),
        jax.ShapeDtypeStruct((8, 2 * rows), F32),
        jax.ShapeDtypeStruct((width, rows), F32),
    ]
    vmem = pl.BlockSpec(memory_space=pltpu.VMEM)
    smem = pl.BlockSpec(memory_space=pltpu.SMEM)
    if first:
        outs += [block, jax.ShapeDtypeStruct((width, rows), BF)]
        args = (where, tok, gain, shift, w, qb, vb)
    else:
        args = (where, tok, gain, shift, w, vb) + tuple(state)
    flops = 2 * rows * width * width * (3 if first else 2) + 4 * rows * rows * width * 4
    return pl.pallas_call(
        partial(forward_kernel, first, last),
        out_shape=outs,
        in_specs=[smem] + [vmem] * (len(args) - 1),
        out_specs=[vmem] * len(outs),
        compiler_params=params(32),
        cost_estimate=cost(flops, 12 * 2**20, HEADS * rows * rows),
        name="attend_first" if first else ("attend_last" if last else "attend_next"),
    )(*args)


def middle_kernel(
    order_ref,
    tok_ref,
    cot_ref,
    attt_ref,
    wo_ref,
    ob_ref,
    gain_ref,
    shift_ref,
    up_ref,
    ub_ref,
    down_ref,
    db_ref,
    perm_ref,
    block_out,
    down_keep,
    down_send,
    up_keep,
    up_send,
    out_keep,
    out_send,
    da_out,
    dat_out,
    negd_out,
    gmid_out,
    vec_out,
    ubg_out,
    mid_ref,
    norm_ref,
    inv_ref,
    h2_ref,
    h2t_ref,
    att_ref,
    res_ref,
    gh_ref,
):
    step = pl.program_id(0)
    steps = pl.num_programs(0)
    rows, width = tok_ref.shape

    @pl.when(step == 0)
    def _():
        att_ref[...] = attt_ref[...].T.astype(BF)
        middle = tok_ref[...].astype(F32) + (dot(att_ref[...], wo_ref[...]) + ob_ref[...])
        mid_ref[...] = middle
        normed, inverse = normalize(middle)
        norm_ref[...] = normed
        inv_ref[...] = jnp.broadcast_to(inverse, inv_ref.shape)
        h2_ref[...] = (normed * gain_ref[...] + shift_ref[...]).astype(BF)
        h2t_ref[...] = dot_nt(perm_ref[...], h2_ref[...]).astype(BF)
        res_ref[...] = jnp.zeros_like(res_ref)
        gh_ref[...] = jnp.zeros_like(gh_ref)

    before = dot(h2_ref[...], up_ref[...]) + ub_ref[...]
    cdf = 0.5 * (1.0 + lax.erf(before * math.sqrt(0.5)))
    slope = cdf + before * (jnp.exp(-0.5 * before * before) * (1.0 / math.sqrt(2.0 * math.pi)))
    lifted = (before * cdf).astype(BF)
    res_ref[...] += dot(lifted, down_ref[...])
    grad_down = dot_tn(lifted, cot_ref[...]).astype(BF)

    @pl.when(step < steps // 2)
    def _():
        down_send[...] = grad_down

    @pl.when(step >= steps // 2)
    def _():
        down_keep[...] = grad_down

    grad_lifted = dot_nt(cot_ref[...], down_ref[...])
    grad_before = (grad_lifted * slope).astype(BF)
    ubg_out[...] = jnp.sum(grad_before.astype(F32), 0, keepdims=True)
    grad_up = dot(h2t_ref[...], grad_before).astype(BF)
    half = width // 2
    up_keep[...] = grad_up[:half]
    up_send[...] = grad_up[half:]
    gh_ref[...] += dot_nt(grad_before, up_ref[...])

    @pl.when(step == steps - 1)
    def _():
        block_out[...] = (mid_ref[...] + (res_ref[...] + db_ref[...])).astype(BF)
        cot = cot_ref[...].astype(F32)
        grad = gh_ref[...]
        normed = norm_ref[...]
        vec_out[0:1, :] = jnp.sum(cot, 0, keepdims=True)
        vec_out[1:2, :] = jnp.sum(grad * normed, 0, keepdims=True)
        vec_out[2:3, :] = jnp.sum(grad, 0, keepdims=True)
        scaled = grad * gain_ref[...]
        grad_middle = cot + inv_ref[:, :1] * (
            scaled
            - jnp.mean(scaled, -1, keepdims=True)
            - normed * jnp.mean(scaled * normed, -1, keepdims=True)
        )
        gmid_out[...] = grad_middle
        branch = grad_middle.astype(BF)
        vec_out[3:4, :] = jnp.sum(branch.astype(F32), 0, keepdims=True)
        att_t = dot_nt(perm_ref[...], att_ref[...]).astype(BF)
        grad_out = dot(att_t, branch).astype(BF)
        out_keep[...] = grad_out[:half]
        out_send[...] = grad_out[half:]
        grad_att = dot_nt(branch, wo_ref[...]).astype(BF)
        da_out[...] = grad_att
        grad_att_t = grad_att.astype(F32).T
        dat_out[...] = grad_att_t.astype(BF)
        product = grad_att_t * attt_ref[...]
        for head in range(HEADS):
            spread = jnp.sum(product[head * HD : (head + 1) * HD], 0, keepdims=True)
            place = slice((head % 2) * rows, (head % 2 + 1) * rows)
            negd_out[head // 2 : head // 2 + 1, place] = -spread


def middle_step(order, tok, cot, attt, wo, ob, gain, shift, up, ub, down, db, perm):
    rows, width = tok.shape
    hidden = up.shape[1]
    steps = 8
    chunk = hidden // steps
    half = steps // 2

    def whole(shape):
        return pl.BlockSpec(shape, lambda i, order: (0,) * len(shape))

    in_specs = [
        whole((rows, width)),
        whole((rows, width)),
        whole((width, rows)),
        whole((width, width)),
        whole((1, width)),
        whole((1, width)),
        whole((1, width)),
        pl.BlockSpec((width, chunk), lambda i, order: (0, order[i])),
        pl.BlockSpec((1, chunk), lambda i, order: (0, order[i])),
        pl.BlockSpec((chunk, width), lambda i, order: (order[i], 0)),
        whole((1, width)),
        whole((width, width)),
    ]
    out_shape = [
        jax.ShapeDtypeStruct((rows, width), BF),
        jax.ShapeDtypeStruct((hidden // 2, width), BF),
        jax.ShapeDtypeStruct((hidden // 2, width), BF),
        jax.ShapeDtypeStruct((width // 2, hidden), BF),
        jax.ShapeDtypeStruct((width // 2, hidden), BF),
        jax.ShapeDtypeStruct((width // 2, width), BF),
        jax.ShapeDtypeStruct((width // 2, width), BF),
        jax.ShapeDtypeStruct((rows, width), BF),
        jax.ShapeDtypeStruct((width, rows), BF),
        jax.ShapeDtypeStruct((8, 2 * rows), F32),
        jax.ShapeDtypeStruct((rows, width), F32),
        jax.ShapeDtypeStruct((8, width), F32),
        jax.ShapeDtypeStruct((1, hidden), F32),
    ]
    out_specs = [
        whole((rows, width)),
        pl.BlockSpec((chunk, width), lambda i, order: (jnp.maximum(i - half, 0), 0)),
        pl.BlockSpec((chunk, width), lambda i, order: (jnp.minimum(i, half - 1), 0)),
        pl.BlockSpec((width // 2, chunk), lambda i, order: (0, order[i])),
        pl.BlockSpec((width // 2, chunk), lambda i, order: (0, order[i])),
        whole((width // 2, width)),
        whole((width // 2, width)),
        whole((rows, width)),
        whole((width, rows)),
        whole((8, 2 * rows)),
        whole((rows, width)),
        whole((8, width)),
        pl.BlockSpec((1, chunk), lambda i, order: (0, order[i])),
    ]
    return pl.pallas_call(
        middle_kernel,
        out_shape=out_shape,
        grid_spec=pltpu.PrefetchScalarGridSpec(
            num_scalar_prefetch=1,
            grid=(steps,),
            in_specs=in_specs,
            out_specs=out_specs,
            scratch_shapes=[
                pltpu.VMEM((rows, width), F32),
                pltpu.VMEM((rows, width), F32),
                pltpu.VMEM((rows, 128), F32),
                pltpu.VMEM((rows, width), BF),
                pltpu.VMEM((width, rows), BF),
                pltpu.VMEM((rows, width), BF),
                pltpu.VMEM((rows, width), F32),
                pltpu.VMEM((rows, width), F32),
            ],
        ),
        compiler_params=params(48),
        cost_estimate=cost(12 * rows * width * hidden + 6 * rows * width * width, 30 * 2**20, 0),
        name="middle",
    )(order, tok, cot, attt, wo, ob, gain, shift, up, ub, down, db, perm)


def three_parts(row):
    high = row.astype(BF)
    rest = row - high.astype(F32)
    mid = rest.astype(BF)
    low = (rest - mid.astype(F32)).astype(BF)
    return high.astype(F32), mid.astype(F32), low.astype(F32)


def extra_rows(row, with_mask):
    n = row.shape[1]
    high, mid, low = three_parts(row)
    place = lax.broadcasted_iota(jnp.int32, (128, n), 0)
    out = jnp.where(place == 0, 1.0 if with_mask else 0.0, 0.0)
    out = jnp.where(place == 1, high, out)
    out = jnp.where(place == 2, mid, out)
    out = jnp.where(place == 3, low, out)
    return out.astype(BF)


def backward_kernel(first, last, *refs):
    (where_ref, q_ref, qt_ref, da_ref, dat_ref, negl_ref, negd_ref, k_ref, v_ref, tok_ref, w_ref) = refs[:11]
    refs = refs[11:]
    if not first:
        dqt_ref, vec_ref = refs[:2]
        refs = refs[2:]
    if last:
        dkv_out, g_out, vec_out, dq_out = refs[:4]
        (dqt_out,) = refs[4:]
    else:
        dkv_out, g_out, vec_out, dqt_out = refs
    rows, width = q_ref.shape
    extra_keys = extra_lanes(where_ref, rows, 3)
    keys_t = k_ref[...].astype(F32).T.astype(BF)
    lane = lax.broadcasted_iota(jnp.int32, (rows, 128), 1)
    for pair in range(PAIRS):
        lanes = pair_lanes(pair)
        keys = jnp.concatenate([k_ref[:, lanes], extra_keys], 1)
        scores = dot(keys, two_heads(qt_ref[lanes, :], extra_rows(negl_ref[pair : pair + 1, :], True)))
        softmaxed = jnp.exp2(scores * TO_EXP2)
        values = jnp.concatenate([v_ref[:, lanes], extra_keys], 1)
        centred = dot(values, two_heads(dat_ref[lanes, :], extra_rows(negd_ref[pair : pair + 1, :], False)))
        grad_scores = (softmaxed * centred).astype(BF)
        weights = softmaxed.astype(BF)
        zero = jnp.zeros((rows, 128), BF)
        q_pair = q_ref[:, lanes]
        da_pair = da_ref[:, lanes]
        q_both = jnp.concatenate([jnp.where(lane < HD, q_pair, zero), jnp.where(lane < HD, zero, q_pair)], 0)
        da_both = jnp.concatenate([jnp.where(lane < HD, da_pair, zero), jnp.where(lane < HD, zero, da_pair)], 0)
        dkv_out[:, lanes] = (dot(grad_scores, q_both) * SCALE).astype(BF)
        dkv_out[:, slice(width + lanes.start, width + lanes.stop)] = dot(weights, da_both).astype(BF)
        both = dot(keys_t[lanes, :], grad_scores)
        for head in range(2):
            own = slice(lanes.start + head * HD, lanes.start + (head + 1) * HD)
            part = both[head * HD : (head + 1) * HD, head * rows : (head + 1) * rows]
            if not first:
                part = part + dqt_ref[own, :]
            dqt_out[own, :] = part
    grad = dot_nt(dkv_out[...], w_ref[:, width:])
    query_bias = jnp.zeros((1, width), F32)
    if last:
        dq = (dqt_out[...].T * SCALE).astype(BF)
        dq_out[...] = dq
        query_bias = jnp.sum(dq.astype(F32), 0, keepdims=True)
        grad = grad + dot_nt(dq, w_ref[:, :width])
    g_out[...] = grad.astype(g_out.dtype)
    normed, _ = normalize(tok_ref[...].astype(F32))
    value_bias = jnp.sum(dkv_out[:, width:].astype(F32), 0, keepdims=True)
    gain = jnp.sum(grad * normed, 0, keepdims=True)
    shift = jnp.sum(grad, 0, keepdims=True)
    if not first:
        value_bias = value_bias + vec_ref[1:2, :]
        gain = gain + vec_ref[2:3, :]
        shift = shift + vec_ref[3:4, :]
    vec_out[0:1, :] = query_bias
    vec_out[1:2, :] = value_bias
    vec_out[2:3, :] = gain
    vec_out[3:4, :] = shift
    vec_out[4:8, :] = jnp.zeros((4, width), F32)


def backward_step(first, last, where, q, qt, da, dat, negl, negd, k, v, tok, w, state):
    rows, width = q.shape
    vmem = pl.BlockSpec(memory_space=pltpu.VMEM)
    smem = pl.BlockSpec(memory_space=pltpu.SMEM)
    args = (where, q, qt, da, dat, negl, negd, k, v, tok, w) + (() if first else tuple(state))
    outs = [
        jax.ShapeDtypeStruct((rows, 2 * width), BF),
        jax.ShapeDtypeStruct((rows, width), F32 if last else BF),
        jax.ShapeDtypeStruct((8, width), F32),
    ]
    if last:
        outs.append(jax.ShapeDtypeStruct((rows, width), BF))
        scratch = [pltpu.VMEM((width, rows), F32)]
    else:
        outs.append(jax.ShapeDtypeStruct((width, rows), F32))
        scratch = []
    flops = 2 * rows * width * width * (3 if last else 2) + 10 * rows * rows * width * 4
    return pl.pallas_call(
        partial(backward_kernel, first, last),
        out_shape=outs,
        in_specs=[smem] + [vmem] * (len(args) - 1),
        out_specs=[vmem] * len(outs),
        scratch_shapes=scratch,
        compiler_params=params(40),
        cost_estimate=cost(flops, 16 * 2**20, HEADS * rows * rows),
        name="attend_back",
    )(*args)


def projection_kernel(*refs):
    count = (len(refs) - 5) // 2
    perm_ref, dq_ref = refs[:2]
    hiddens = refs[2 : 2 + count]
    dkvs = refs[2 + count : 2 + 2 * count]
    keep_ref, send_ref, ht_ref = refs[2 + 2 * count :]
    step = pl.program_id(0)
    rows = hiddens[0].shape[0]
    half = keep_ref.shape[0]

    @pl.when(step == 0)
    def _():
        for i, hidden in enumerate(hiddens):
            ht_ref[:, i * rows : (i + 1) * rows] = dot_nt(perm_ref[...], hidden[...]).astype(BF)

    @pl.when(step < 2)
    def _():
        grad = dot(ht_ref[:, :rows], dq_ref[...])
        keep_ref[...] = grad[:half].astype(BF)
        send_ref[...] = grad[half:].astype(BF)

    @pl.when(step >= 2)
    def _():
        right = jnp.concatenate([dkv[...] for dkv in dkvs], 0)
        grad = dot(ht_ref[...], right)
        keep_ref[...] = grad[:half].astype(BF)
        send_ref[...] = grad[half:].astype(BF)


def projection_step(perm, dq, hiddens, dkvs):
    rows, width = dq.shape
    chunk = width // 2
    count = len(hiddens)

    def whole(shape):
        return pl.BlockSpec(shape, lambda i: (0,) * len(shape))

    out = jax.ShapeDtypeStruct((width // 2, 3 * width), BF)
    return pl.pallas_call(
        projection_kernel,
        out_shape=[out, out],
        grid=(6,),
        in_specs=[whole((width, width)), pl.BlockSpec((rows, chunk), lambda i: (0, jnp.minimum(i, 1)))]
        + [whole((rows, width))] * count
        + [pl.BlockSpec((rows, chunk), lambda i: (0, jnp.maximum(i - 2, 0)))] * count,
        out_specs=[pl.BlockSpec((width // 2, chunk), lambda i: (0, i))] * 2,
        scratch_shapes=[pltpu.VMEM((width, count * rows), BF)],
        compiler_params=params(32),
        cost_estimate=cost(2 * rows * width * width * (1 + 2 * count), 12 * 2**20, 0),
        name="projection_grad",
    )(perm, dq, *hiddens, *dkvs)


def final_kernel(tok_ref, gain_ref, g_ref, recv_ref, gmid_ref, out_ref):
    normed, inverse = normalize(tok_ref[...].astype(F32))
    scaled = (g_ref[...] + recv_ref[...].astype(F32)) * gain_ref[...]
    out_ref[...] = gmid_ref[...] + inverse * (
        scaled
        - jnp.mean(scaled, -1, keepdims=True)
        - normed * jnp.mean(scaled * normed, -1, keepdims=True)
    )


def final_step(tok, gain, g, recv, gmid):
    vmem = pl.BlockSpec(memory_space=pltpu.VMEM)
    return pl.pallas_call(
        final_kernel,
        out_shape=jax.ShapeDtypeStruct(tok.shape, F32),
        in_specs=[vmem] * 5,
        out_specs=vmem,
        compiler_params=params(16),
        cost_estimate=cost(20 * tok.size, 10 * tok.size, 0),
        name="norm_back",
    )(tok, gain, g, recv, gmid)


def flip(count, distance):
    return [(i, i ^ distance) for i in range(count)]


def tree_place(bits):
    n = len(bits)
    return np.array([sum(((p >> (n - 1 - i)) & 1) << bit for i, bit in enumerate(bits)) for p in range(1 << n)])


def tree_sum(keep, recv, bits, cubes):
    for bit in bits:
        half = keep.shape[0] // 2
        send = (keep[half:].astype(F32) + recv[half:].astype(F32)).astype(BF)
        moved = lax.ppermute(send, "cube", flip(cubes, 1 << bit))
        keep = (keep[:half].astype(F32) + recv[:half].astype(F32)).astype(BF)
        recv = moved
    return keep.astype(F32) + recv.astype(F32)


def spec_sum(part, me, count):
    cols = part.shape[1] // count

    def mine(distance):
        return lax.dynamic_slice_in_dim(part, (me ^ distance) * cols, cols, 1)

    got = [lax.ppermute(mine(d).astype(BF), "spec", flip(count, d)) for d in range(1, count)]
    total = mine(0)
    for piece in got:
        total = total + piece.astype(F32)
    return total


def vector_sum(vectors, cubes, count):
    done = 1
    while done < cubes:
        group = min(8, cubes // done)
        got = [lax.ppermute(vectors, "cube", flip(cubes, d * done)) for d in range(1, group)]
        vectors = sum(got, vectors)
        done *= group
    got = [lax.ppermute(vectors, "spec", flip(count, d)) for d in range(1, count)]
    return sum(got, vectors)


def local(
    tokens,
    cotangent,
    lengths,
    projection,
    query_bias,
    value_bias,
    output_weight,
    output_bias,
    up_weight,
    up_bias,
    down_weight,
    down_bias,
    first_gain,
    first_shift,
    second_gain,
    second_shift,
):
    _, rows, width = tokens.shape
    hidden = up_weight.shape[1]
    cubes, count = lax.axis_size("cube"), lax.axis_size("spec")
    cube, spec = lax.axis_index("cube"), lax.axis_index("spec")
    tok = tokens.reshape(rows, width)
    cot = cotangent.reshape(rows, width)

    def row(vector):
        return vector.reshape(1, -1)

    ring = [(i, (i + 1) % count) for i in range(count)]
    blocks = [tok]
    for _ in range(count - 1):
        blocks.append(lax.ppermute(blocks[-1], "spec", ring))
    wheres = [
        jnp.stack([((spec - s) % count).astype(jnp.int32) * rows, lengths[0].astype(jnp.int32)])
        for s in range(count)
    ]

    bits = cubes.bit_length() - 1
    order_a = list(range(bits))
    order_b = [0] + list(range(bits - 1, 0, -1))
    place_a, place_b = tree_place(order_a), tree_place(order_b)
    split = cubes // 2

    def source_rows(place, offset, size, block):
        start = (jnp.asarray(place, jnp.int32) ^ cube) * block + offset
        return (start[:, None] + jnp.arange(size, dtype=jnp.int32)[None, :]).reshape(-1)

    def one_hot(source):
        return (source[:, None] == jnp.arange(width, dtype=jnp.int32)[None, :]).astype(BF)

    block = width // cubes
    part = block // 2
    perm_b = one_hot(source_rows(place_b, 0, block, block))
    perm_mixed = one_hot(
        jnp.concatenate(
            [
                source_rows(place_a[:split], 0, part, block),
                source_rows(place_b[:split], part, part, block),
                source_rows(place_a[split:], 0, part, block),
                source_rows(place_b[split:], part, part, block),
            ]
        )
    )
    chunks = 8
    if cubes == chunks:
        order = jnp.asarray(np.roll(place_a, -split), jnp.int32) ^ cube
    else:
        order = jnp.roll(jnp.arange(chunks, dtype=jnp.int32), -(chunks // 2))

    hiddens, keys, values = [], [], []
    state = None
    for s in range(count):
        first, last = s == 0, s == count - 1
        made = forward_step(
            first,
            last,
            wheres[s],
            blocks[s],
            row(first_gain),
            row(first_shift),
            projection,
            row(query_bias),
            row(value_bias),
            state,
        )
        hiddens.append(made[0])
        keys.append(made[1])
        values.append(made[2])
        if first:
            q, qt = made[6:]
        state = (qt,) + tuple(made[3:6])
    negl, attt = state[1], state[3]

    (
        block_out,
        down_keep,
        down_send,
        up_keep,
        up_send,
        out_keep,
        out_send,
        da,
        dat,
        negd,
        gmid,
        vec_mid,
        grad_up_bias,
    ) = middle_step(
        order,
        tok,
        cot,
        attt,
        output_weight,
        row(output_bias),
        row(second_gain),
        row(second_shift),
        up_weight,
        row(up_bias),
        down_weight,
        row(down_bias),
        perm_b,
    )
    if cubes != chunks:
        whole = jnp.concatenate([down_keep, down_send], 0).reshape(cubes, hidden // cubes, width)
        whole = jnp.take(whole, jnp.asarray(place_a, jnp.int32) ^ cube, axis=0)
        down_keep = whole[:split].reshape(hidden // 2, width)
        down_send = whole[split:].reshape(hidden // 2, width)

    pair = flip(cubes, 1)
    down_recv = lax.ppermute(down_send, "cube", pair)
    up_recv = lax.ppermute(up_send, "cube", pair)
    out_recv = lax.ppermute(out_send, "cube", pair)
    grad_down = tree_sum(down_keep, down_recv, order_a[1:], cubes)
    grad_up = tree_sum(up_keep, up_recv, order_b[1:], cubes)
    grad_out = tree_sum(out_keep, out_recv, order_b[1:], cubes)

    dkvs = [None] * count
    back_state = None
    travelling = None
    for step in range(count):
        s = (step + 1) % count
        first, last = step == 0, step == count - 1
        made = backward_step(
            first,
            last,
            wheres[s],
            q,
            qt,
            da,
            dat,
            negl,
            negd,
            keys[s],
            values[s],
            blocks[s],
            projection,
            back_state,
        )
        dkvs[s] = made[0]
        back_state = (made[3], made[2])
        if last:
            g_own, vec_back, dq = made[1:]
        else:
            g = made[1]
            if not first:
                g = (g.astype(F32) + travelling.astype(F32)).astype(BF)
            travelling = lax.ppermute(g, "spec", ring)

    proj_keep, proj_send = projection_step(perm_mixed, dq, hiddens, dkvs)
    proj_recv = lax.ppermute(proj_send, "cube", pair)
    mid = proj_keep.shape[0] // 2
    proj_a = tree_sum(proj_keep[:mid], proj_recv[:mid], order_a[1:], cubes)
    proj_b = tree_sum(proj_keep[mid:], proj_recv[mid:], order_b[1:], cubes)
    grad_proj = jnp.concatenate([proj_a, proj_b], 0)

    vectors = jnp.concatenate([vec_mid[:4], vec_back[:4], grad_up_bias.reshape(-1, width)], 0)
    vectors = vector_sum(vectors, cubes, count)

    grad_tokens = final_step(tok, row(first_gain), g_own, travelling, gmid)

    return (
        block_out.reshape(tokens.shape),
        grad_tokens.reshape(tokens.shape),
        spec_sum(grad_proj, spec, count),
        vectors[4],
        vectors[5],
        spec_sum(grad_out, spec, count),
        vectors[3],
        spec_sum(grad_up, spec, count),
        vectors[8:].reshape(-1),
        spec_sum(grad_down, spec, count),
        vectors[0],
        vectors[6],
        vectors[7],
        vectors[1],
        vectors[2],
    )


def solution(mesh):
    return jax.shard_map(
        local,
        mesh=mesh,
        in_specs=(
            P("cube", "spec", None),
            P("cube", "spec", None),
            P("cube"),
        )
        + (P(),) * 13,
        out_specs=(
            P("cube", "spec", None),
            P("cube", "spec", None),
            P("cube", "spec"),
            P(),
            P(),
            P("cube", "spec"),
            P(),
            P("cube", "spec"),
            P(),
            P("cube", "spec"),
            P(),
            P(),
            P(),
            P(),
            P(),
        ),
        check_vma=False,
    )
```

```python
import math
from functools import partial

import jax
import jax.numpy as jnp
import numpy as np
from jax import lax
from jax.experimental import pallas as pl
from jax.experimental.pallas import tpu as pltpu
from jax.sharding import PartitionSpec as P

HEADS = 12
HD = 64
PAIRS = HEADS // 2
EPS = 1e-06
SCALE = HD ** (-0.5)
TO_EXP2 = SCALE * math.log2(math.e)
MASKED = -1e30

BF = jnp.bfloat16
F32 = jnp.float32


def dot(left, right):
    return jnp.dot(left, right, preferred_element_type=F32)


def dot_nt(left, right):
    return lax.dot_general(left, right, (((1,), (1,)), ((), ())), preferred_element_type=F32)


def dot_tn(left, right):
    return lax.dot_general(left, right, (((0,), (0,)), ((), ())), preferred_element_type=F32)


def normalize(values):
    average = jnp.mean(values, -1, keepdims=True)
    centred = values - average
    inverse = lax.rsqrt(jnp.mean(centred * centred, -1, keepdims=True) + EPS)
    return centred * inverse, inverse


def params(megabytes=60):
    return pltpu.CompilerParams(vmem_limit_bytes=megabytes * 2**20)


def cost(flops, nbytes, trans=0):
    return pl.CostEstimate(flops=flops // 1000, bytes_accessed=nbytes // 1000, transcendentals=trans // 1000)


def extra_lanes(where_ref, rows, ones):
    slot = lax.broadcasted_iota(jnp.int32, (rows, 128), 0) + where_ref[0]
    lane = lax.broadcasted_iota(jnp.int32, (rows, 128), 1)
    masked = jnp.where(slot < where_ref[1], 0.0, MASKED)
    rest = jnp.where(lane <= ones, 1.0, 0.0)
    return jnp.where(lane == 0, masked, rest).astype(BF)


def two_heads(part, extra):
    n = part.shape[1]
    zero = jnp.zeros((HD, n), part.dtype)
    left = jnp.concatenate([part[:HD], zero], 0)
    right = jnp.concatenate([zero, part[HD:]], 0)
    return jnp.concatenate([jnp.concatenate([left, right], 1), extra], 0)


def as_row(ref):
    return ref[...].reshape(1, -1)


def pair_lanes(pair):
    return slice(pair * 2 * HD, (pair + 1) * 2 * HD)


ANY = pl.BlockSpec(memory_space=pl.ANY)
SMEM = pl.BlockSpec(memory_space=pltpu.SMEM)


def staged(body, name, scalars, ins, outs, estimate, scratch=(), deps=()):
    parts = [x if isinstance(x, tuple) else (x, slice(0, x.shape[0]), slice(0, x.shape[-1])) for x in ins]
    shapes = []
    for x, rows, cols in parts:
        shapes.append((rows.stop - rows.start,) if x.ndim == 1 else (rows.stop - rows.start, cols.stop - cols.start))
    arrays = []
    for x, _, _ in parts:
        if not any(x is y for y in arrays):
            arrays.append(x)
    index = [[i for i, y in enumerate(arrays) if y is x][0] for x, _, _ in parts]
    n_s, n_a, n_i, n_o, n_x = len(scalars), len(arrays), len(ins), len(outs), len(scratch)

    def kernel(*refs):
        at = 0
        groups = []
        for n in (n_s, n_a, len(deps), n_o, n_x, n_i, n_o):
            groups.append(refs[at : at + n])
            at += n
        s_refs, a_ref, _, o_to, x_refs, i_ref, o_ref = groups
        i_sem, o_sem = refs[at:]
        loads = []
        for i, (x, rows, cols) in enumerate(parts):
            source = a_ref[index[i]]
            if shapes[i] != x.shape:
                source = source.at[rows, cols]
            loads.append(pltpu.make_async_copy(source, i_ref[i], i_sem.at[i]))
        stores = [pltpu.make_async_copy(o_ref[i], o_to[i], o_sem.at[i]) for i in range(n_o)]
        for load in loads:
            load.start()
        waited = set()
        sent = set()

        def get(i):
            if i not in waited:
                waited.add(i)
                loads[i].wait()
            return i_ref[i]

        def put(i, *where):
            sent.add(i)
            if where:
                pltpu.make_async_copy(o_ref[i].at[where], o_to[i].at[where], o_sem.at[i]).start()
            else:
                stores[i].start()

        body(s_refs, get, o_ref, put, x_refs)
        for i in range(n_i):
            get(i)
        for i in range(n_o):
            if i not in sent:
                put(i)
        for store in stores:
            store.wait()

    return pl.pallas_call(
        kernel,
        out_shape=list(outs),
        in_specs=[SMEM] * n_s + [ANY] * (n_a + len(deps)),
        out_specs=[ANY] * n_o,
        scratch_shapes=list(scratch)
        + [pltpu.VMEM(shape, x.dtype) for shape, (x, _, _) in zip(shapes, parts)]
        + [pltpu.VMEM(x.shape, x.dtype) for x in outs]
        + [pltpu.SemaphoreType.DMA((n_i,)), pltpu.SemaphoreType.DMA((n_o,))],
        compiler_params=params(),
        cost_estimate=estimate,
        name=name,
    )(*scalars, *arrays, *deps)


def shaped(shape, dtype=BF):
    return jax.ShapeDtypeStruct(shape, dtype)


def forward_step(last, wheres, toks, gain, shift, w, qb, vb, state, through, deps=()):
    first = state is None
    count = len(toks)
    rows, width = toks[0].shape
    block = shaped((rows, width))
    outs = [shaped((8, 2 * rows), F32), shaped((8, 2 * rows), F32), shaped((width, rows), F32)]
    outs += [block, block, block] * count
    full = slice(0, width)
    ins = [toks[0], gain, shift, vb, (w, full, slice(width, 2 * width)), (w, full, slice(2 * width, 3 * width))]
    if first:
        ins += [(w, full, full), qb]
        outs += [block, shaped((width, rows)), block]
    else:
        ins += list(state)
    at_tok = len(ins) - 1
    ins += toks[1:]
    if first:
        ins.append(through)

    def body(scalars, get, out, put, scratch):
        m_out, l_out, acc_out = out[:3]
        ones_row = (lax.broadcasted_iota(jnp.int32, (128, 2 * rows), 0) == 0).astype(BF)
        for i in range(count):
            h_out, k_out, v_out = out[3 + 3 * i : 6 + 3 * i]
            normed, _ = normalize(get(at_tok + i if i > 0 else 0)[...].astype(F32))
            hidden = (normed * as_row(get(1)) + as_row(get(2))).astype(BF)
            h_out[...] = hidden
            put(3 + 3 * i)
            k_out[...] = dot(hidden, get(4)[...]).astype(BF)
            put(4 + 3 * i)
            values = dot(hidden, get(5)[...]) + as_row(get(3))
            v_out[...] = values.astype(BF)
            put(5 + 3 * i)
            values_t = v_out[...].astype(F32).T.astype(BF)
            if first:
                at = 3 + 3 * count
                q_out, qt_out, through_out = out[at:]
                if i == 0:
                    q_out[...] = (dot(hidden, get(6)[...]) + as_row(get(7))).astype(BF)
                    put(at)
                    qt_out[...] = q_out[...].astype(F32).T.astype(BF)
                    put(at + 1)
                if i == count - 1:
                    through_out[...] = get(len(ins) - 1)[...]
                    put(at + 2)
                qt_ref = qt_out
            else:
                qt_ref = get(6)
            extra_keys = extra_lanes(scalars[i], rows, 0)
            start = first and i == 0
            end = last and i == count - 1
            for pair in range(PAIRS):
                lanes = pair_lanes(pair)
                this = slice(pair, pair + 1)
                keys = jnp.concatenate([k_out[:, lanes], extra_keys], 1)
                scores = dot(keys, two_heads(qt_ref[lanes, :], ones_row))
                top = jnp.max(scores, 0, keepdims=True)
                if not start:
                    m_ref, l_ref, acc_ref = (get(7 + j) for j in range(3)) if i == 0 else (m_out, l_out, acc_out)
                    before = m_ref[this, :]
                    top = jnp.maximum(top, before)
                    fade = jnp.exp2((before - top) * TO_EXP2)
                weights = jnp.exp2((scores - top) * TO_EXP2)
                total = jnp.sum(weights, 0, keepdims=True)
                if not start:
                    total = total + l_ref[this, :] * fade
                both = dot(values_t[lanes, :], weights.astype(BF))
                for head in range(2):
                    own = slice(lanes.start + head * HD, lanes.start + (head + 1) * HD)
                    cols = slice(head * rows, (head + 1) * rows)
                    part = both[head * HD : (head + 1) * HD, cols]
                    if not start:
                        part = part + acc_ref[own, :] * fade[:, cols]
                    if end:
                        part = part / total[:, cols]
                    acc_out[own, :] = part
                m_out[this, :] = -(top + jnp.log2(total) * (1.0 / TO_EXP2)) if end else top
                l_out[this, :] = total
                if i == count - 1:
                    put(2, lanes)

    estimate = pl.CostEstimate(flops=count * 10**10, bytes_accessed=24 * 2**20, transcendentals=0)
    return staged(body, "attend", wheres, ins, outs, estimate, deps=deps)


def middle_step(order, tok, cot, attt, wo, ob, gain, shift, up, ub, down, db, perm):
    rows, width = tok.shape
    hidden = up.shape[1]
    chunks = 8
    chunk = hidden // chunks
    half = width // 2
    ins = [attt, wo, ob, tok, gain, shift, perm, up, ub, cot, down, db]
    outs = [
        shaped((rows, width)),
        shaped((hidden // 2, width)),
        shaped((hidden // 2, width)),
        shaped((half, hidden + width)),
        shaped((half, hidden + width)),
        shaped((rows, width)),
        shaped((width, rows)),
        shaped((8, 2 * rows), F32),
        shaped((rows, width), F32),
        shaped((8, width), F32),
        shaped((8, chunk), F32),
    ]
    scratch = [
        pltpu.VMEM((rows, width), F32),
        pltpu.VMEM((rows, width), F32),
        pltpu.VMEM((rows, width), BF),
        pltpu.VMEM((width, rows), BF),
        pltpu.VMEM((rows, width), BF),
        pltpu.VMEM((rows, width), F32),
        pltpu.VMEM((rows, width), F32),
    ]

    def body(scalars, get, out, put, scratch):
        (order_ref,) = scalars
        block_out, down_keep, down_send, up_keep, up_send, da_out, dat_out, negd_out, gmid_out, vec_out, ubg_out = out
        mid_ref, norm_ref, h2_ref, h2t_ref, att_ref, res_ref, gh_ref = scratch
        attt_ref = get(0)
        att_ref[...] = attt_ref[...].T.astype(BF)
        projected = dot(att_ref[...], get(1)[...]) + as_row(get(2))
        middle = get(3)[...].astype(F32) + projected
        mid_ref[...] = middle
        normed, inverse = normalize(middle)
        norm_ref[...] = normed
        h2_ref[...] = (normed * as_row(get(4)) + as_row(get(5))).astype(BF)
        h2t_ref[...] = dot_nt(get(6)[...], h2_ref[...]).astype(BF)
        up_ref, ub_ref, cot_ref, down_ref = get(7), get(8), get(9), get(10)
        for turn in range(chunks // 2):
            p = (2 * turn + chunks // 2) % chunks
            places = [order_ref[p], order_ref[p + 1]]
            at = [pl.ds(pl.multiple_of(place * chunk, 128), chunk) for place in places]
            up_c = jnp.concatenate([up_ref[:, a] for a in at], 1)
            down_c = jnp.concatenate([down_ref[a, :] for a in at], 0)
            bias = jnp.concatenate([ub_ref[pl.ds(place, 1), :] for place in places], 1)
            before = dot(h2_ref[...], up_c) + bias
            cdf = 0.5 * (1.0 + lax.erf(before * math.sqrt(0.5)))
            slope = cdf + before * (jnp.exp(-0.5 * before * before) * (1.0 / math.sqrt(2.0 * math.pi)))
            lifted = (before * cdf).astype(BF)
            grad_lifted = dot_nt(cot_ref[...], down_c)
            grad_down = dot_tn(lifted, cot_ref[...]).astype(BF)
            to, first = (down_keep, p) if p < chunks // 2 else (down_send, p - chunks // 2)
            rows_to = pl.ds(first * chunk, 2 * chunk)
            to[rows_to, :] = grad_down
            put(1 if p < chunks // 2 else 2, rows_to)
            grad_before = (grad_lifted * slope).astype(BF)
            bias_grad = jnp.sum(grad_before.astype(F32), 0, keepdims=True)
            for i, place in enumerate(places):
                ubg_out[pl.ds(place, 1), :] = bias_grad[:, i * chunk : (i + 1) * chunk]
            grad_up = dot(h2t_ref[...], grad_before).astype(BF)
            for i, a in enumerate(at):
                cols = slice(i * chunk, (i + 1) * chunk)
                up_keep[:, a] = grad_up[:half, cols]
                up_send[:, a] = grad_up[half:, cols]
                put(3, slice(None), a)
                put(4, slice(None), a)
            part = dot(lifted, down_c)
            back = dot_nt(grad_before, up_c)
            if turn == 0:
                res_ref[...] = part
                gh_ref[...] = back
            else:
                res_ref[...] += part
                gh_ref[...] += back
        block_out[...] = (mid_ref[...] + (res_ref[...] + as_row(get(11)))).astype(BF)
        put(0)
        cot32 = cot_ref[...].astype(F32)
        grad = gh_ref[...]
        normed = norm_ref[...]
        vec_out[0:1, :] = jnp.sum(cot32, 0, keepdims=True)
        vec_out[1:2, :] = jnp.sum(grad * normed, 0, keepdims=True)
        vec_out[2:3, :] = jnp.sum(grad, 0, keepdims=True)
        scaled = grad * as_row(get(4))
        grad_middle = cot32 + inverse * (
            scaled
            - jnp.mean(scaled, -1, keepdims=True)
            - normed * jnp.mean(scaled * normed, -1, keepdims=True)
        )
        gmid_out[...] = grad_middle
        put(8)
        branch = grad_middle.astype(BF)
        vec_out[3:4, :] = jnp.sum(branch.astype(F32), 0, keepdims=True)
        vec_out[4:8, :] = jnp.zeros((4, width), F32)
        att_t = dot_nt(get(6)[...], att_ref[...]).astype(BF)
        grad_out = dot(att_t, branch).astype(BF)
        cols = pl.ds(hidden, width)
        up_keep[:, cols] = grad_out[:half]
        up_send[:, cols] = grad_out[half:]
        put(3, slice(None), cols)
        put(4, slice(None), cols)
        grad_att = dot_nt(branch, get(1)[...]).astype(BF)
        da_out[...] = grad_att
        put(5)
        grad_att_t = grad_att.astype(F32).T
        dat_out[...] = grad_att_t.astype(BF)
        put(6)
        product = grad_att_t * attt_ref[...]
        for head in range(HEADS):
            spread = jnp.sum(product[head * HD : (head + 1) * HD], 0, keepdims=True)
            place = slice((head % 2) * rows, (head % 2 + 1) * rows)
            negd_out[head // 2 : head // 2 + 1, place] = -spread

    estimate = cost(12 * rows * width * hidden + 6 * rows * width * width, 30 * 2**20, 0)
    return staged(body, "middle", [order], ins, outs, estimate, scratch)


def three_parts(row):
    high = row.astype(BF)
    rest = row - high.astype(F32)
    mid = rest.astype(BF)
    low = (rest - mid.astype(F32)).astype(BF)
    return high.astype(F32), mid.astype(F32), low.astype(F32)


def extra_rows(row, with_mask):
    n = row.shape[1]
    high, mid, low = three_parts(row)
    place = lax.broadcasted_iota(jnp.int32, (128, n), 0)
    out = jnp.where(place == 0, 1.0 if with_mask else 0.0, 0.0)
    out = jnp.where(place == 1, high, out)
    out = jnp.where(place == 2, mid, out)
    out = jnp.where(place == 3, low, out)
    return out.astype(BF)


def backward_step(wheres, q, qt, da, dat, negl, negd, keys, values, toks, w, state, last, deps):
    rows, width = q.shape
    blocks = len(keys)
    first = state is None
    ins = [qt, negl, dat, negd, q, da]
    for k, v in zip(keys, values):
        ins += [k, v]
    base_w = len(ins)
    ins += [w, *toks]
    base_state = len(ins)
    if not first:
        ins += list(state)
    outs = []
    for i in range(blocks):
        outs += [shaped((rows, 2 * width)), shaped((rows, width), F32 if last and i == blocks - 1 else BF)]
    outs += [shaped((8, width), F32), shaped((rows, width)) if last else shaped((width, rows), F32)]

    def body(scalars, get, out, put, scratch):
        (dqt,) = scratch
        vec_out, end_out = out[2 * blocks :]
        lane = lax.broadcasted_iota(jnp.int32, (rows, 128), 1)
        zero = jnp.zeros((rows, 128), BF)
        value_bias = gain = shift = jnp.zeros((1, width), F32)
        query_bias = jnp.zeros((1, width), F32)
        for i in range(blocks):
            dkv_out, g_out = out[2 * i], out[2 * i + 1]
            extra_keys = extra_lanes(scalars[i], rows, 3)
            qt_ref, negl_ref, dat_ref, negd_ref = get(0), get(1), get(2), get(3)
            k_ref, v_ref = get(6 + 2 * i), get(7 + 2 * i)
            keys_t = k_ref[...].astype(F32).T.astype(BF)
            for pair in range(PAIRS):
                lanes = pair_lanes(pair)
                key = jnp.concatenate([k_ref[:, lanes], extra_keys], 1)
                scores = dot(key, two_heads(qt_ref[lanes, :], extra_rows(negl_ref[pair : pair + 1, :], True)))
                softmaxed = jnp.exp2(scores * TO_EXP2)
                value = jnp.concatenate([v_ref[:, lanes], extra_keys], 1)
                centred = dot(value, two_heads(dat_ref[lanes, :], extra_rows(negd_ref[pair : pair + 1, :], False)))
                grad_scores = (softmaxed * centred).astype(BF)
                weights = softmaxed.astype(BF)
                q_pair = get(4)[:, lanes]
                da_pair = get(5)[:, lanes]
                q_both = jnp.concatenate([jnp.where(lane < HD, q_pair, zero), jnp.where(lane < HD, zero, q_pair)], 0)
                da_both = jnp.concatenate([jnp.where(lane < HD, da_pair, zero), jnp.where(lane < HD, zero, da_pair)], 0)
                dkv_out[:, lanes] = (dot(grad_scores, q_both) * SCALE).astype(BF)
                dkv_out[:, slice(width + lanes.start, width + lanes.stop)] = dot(weights, da_both).astype(BF)
                both = dot(keys_t[lanes, :], grad_scores)
                for head in range(2):
                    own = slice(lanes.start + head * HD, lanes.start + (head + 1) * HD)
                    part = both[head * HD : (head + 1) * HD, head * rows : (head + 1) * rows]
                    if i > 0:
                        part = part + dqt[own, :]
                    elif not first:
                        part = part + get(base_state)[own, :]
                    dqt[own, :] = part
            put(2 * i)
            w_ref = get(base_w)
            grad = dot_nt(dkv_out[...], w_ref[:, width:])
            if last and i == blocks - 1:
                dq = (dqt[...].T * SCALE).astype(BF)
                end_out[...] = dq
                put(2 * blocks + 1)
                query_bias = jnp.sum(dq.astype(F32), 0, keepdims=True)
                grad = grad + dot_nt(dq, w_ref[:, :width])
            g_out[...] = grad.astype(g_out.dtype)
            put(2 * i + 1)
            normed, _ = normalize(get(base_w + 1 + i)[...].astype(F32))
            value_bias = value_bias + jnp.sum(dkv_out[:, width:].astype(F32), 0, keepdims=True)
            gain = gain + jnp.sum(grad * normed, 0, keepdims=True)
            shift = shift + jnp.sum(grad, 0, keepdims=True)
        if not last:
            end_out[...] = dqt[...]
        if not first:
            vec_ref = get(base_state + 1)
            value_bias = value_bias + vec_ref[1:2, :]
            gain = gain + vec_ref[2:3, :]
            shift = shift + vec_ref[3:4, :]
        vec_out[0:1, :] = query_bias
        vec_out[1:2, :] = value_bias
        vec_out[2:3, :] = gain
        vec_out[3:4, :] = shift
        vec_out[4:8, :] = jnp.zeros((4, width), F32)

    flops = blocks * (2 * rows * width * width * 3 + 10 * rows * rows * width * 4)
    estimate = cost(flops, 20 * 2**20, blocks * HEADS * rows * rows)
    return staged(
        body, "attend_back", wheres, ins, outs, estimate, [pltpu.VMEM((width, rows), F32)], deps
    )


def projection_step(perm, dq, hiddens, dkvs, vec_mid, vec_up, vec_back, deps):
    rows, width = dq.shape
    count = len(hiddens)
    part = width // 4
    ins = [perm, *hiddens, dq, vec_mid, vec_up, vec_back, *dkvs]
    outs = [shaped((n, 3 * width)) for n in (part, part, part + 16, part)] + [shaped((8, 3 * width), F32)]
    at = 1 + count

    def body(scalars, get, out, put, scratch):
        (ht_ref,) = scratch
        keep_a, keep_b, send_a, send_b, vec_ref = out
        for i in range(count):
            ht_ref[:, i * rows : (i + 1) * rows] = dot_nt(get(0)[...], get(1 + i)[...]).astype(BF)
        vec_ref[0:4, :width] = get(at + 1)[0:4, :]
        vec_ref[0:4, width : 2 * width] = get(at + 3)[0:4, :]
        up = jnp.concatenate([get(at + 2)[i : i + 1, :] for i in range(get(at + 2).shape[0])], 1)
        for i in range(4):
            vec_ref[i : i + 1, 2 * width :] = up[:, i * width : (i + 1) * width]
        vec_ref[4:8, :] = jnp.zeros((4, 3 * width), F32)
        send_a[part:, :] = split_high(vec_ref[...])
        put(4)
        for third in range(3):
            if third == 0:
                grad = dot(ht_ref[:, :rows], get(at)[...])
            else:
                own = slice((third - 1) * width, third * width)
                grad = dot(ht_ref[...], jnp.concatenate([get(at + 4 + i)[:, own] for i in range(count)], 0))
            grad = grad.astype(BF)
            cols = pl.ds(third * width, width)
            send_a[:part, cols] = grad[2 * part : 3 * part]
            put(2, slice(None), cols)
            send_b[:, cols] = grad[3 * part :]
            put(3, slice(None), cols)
            keep_a[:, cols] = grad[:part]
            put(0, slice(None), cols)
            keep_b[:, cols] = grad[part : 2 * part]
            put(1, slice(None), cols)

    estimate = cost(2 * rows * width * width * (1 + 2 * count), 12 * 2**20, 0)
    return staged(
        body, "projection_grad", [], ins, outs, estimate, [pltpu.VMEM((width, count * rows), BF)], deps
    )


def final_step(tok, gain, gmid, g, pieces, deps=()):
    def body(scalars, get, out, put, scratch):
        normed, inverse = normalize(get(0)[...].astype(F32))
        total = get(3)[...]
        for i in range(len(pieces)):
            total = total + get(4 + i)[...].astype(F32)
        scaled = total * as_row(get(1))
        out[0][...] = (
            get(2)[...]
            + inverse
            * (
                scaled
                - jnp.mean(scaled, -1, keepdims=True)
                - normed * jnp.mean(scaled * normed, -1, keepdims=True)
            )
        ).astype(BF)

    estimate = cost(20 * tok.size, 12 * tok.size, 0)
    ins = [tok, gain, gmid, g, *pieces]
    return staged(body, "norm_back", [], ins, [shaped(tok.shape)], estimate, deps=deps)[0]


def flip(count, distance):
    return [(i, i ^ distance) for i in range(count)]


def tree_place(bits):
    n = len(bits)
    return np.array([sum(((p >> (n - 1 - i)) & 1) << bit for i, bit in enumerate(bits)) for p in range(1 << n)])


def split_high(values):
    high = values.astype(BF)
    return jnp.concatenate([high.astype(F32), values - high.astype(F32)], 0).astype(BF)


def joined(both):
    both = both.astype(F32)
    return both[:8] + both[8:]


class Part:
    def __init__(self, keep, recv):
        self.terms, self.rows, self.cols = [keep, recv], keep.shape[0], keep.shape[1]

    def inputs(self, start):
        return [(x, slice(start, self.rows), slice(0, self.cols)) for x in self.terms]

    def total(self):
        return sum(x[: self.rows].astype(F32) for x in self.terms)


def add_up(refs):
    total = refs[0][...].astype(F32)
    for ref in refs[1:]:
        total = total + ref[...].astype(F32)
    return total


def halve(parts, name, vectors=None, deps=()):
    halves = [p.rows // 2 for p in parts]
    if any(h % 16 for h in halves):
        sends = [p.total()[h:].astype(BF) for p, h in zip(parts, halves)]
        if vectors is not None:
            vectors = vectors + joined(parts[0].terms[-1][parts[0].rows :])
            sends[0] = jnp.concatenate([sends[0], split_high(vectors)], 0)
    else:
        ins, counts = [], []
        for p, h in zip(parts, halves):
            ins += p.inputs(h)
            counts.append(len(p.terms))
        outs = [shaped((h, p.cols)) for p, h in zip(parts, halves)]
        if vectors is not None:
            sent, rows = parts[0].terms[-1], parts[0].rows
            ins += [vectors, (sent, slice(rows, rows + 16), slice(0, parts[0].cols))]
            outs[0] = shaped((halves[0] + 16, parts[0].cols))
            outs.append(shaped(vectors.shape, F32))

        def body(scalars, get, out, put, scratch):
            at = 0
            for i, (n, h) in enumerate(zip(counts, halves)):
                out[i][:h, :] = add_up([get(at + j) for j in range(n)]).astype(BF)
                at += n
                if vectors is not None and i == 0:
                    total = get(len(ins) - 2)[...] + joined(get(len(ins) - 1)[...])
                    out[len(outs) - 1][...] = total
                    out[0][h:, :] = split_high(total)
                put(i)

        size = sum(h * p.cols for p, h in zip(parts, halves))
        made = staged(body, name, [], ins, outs, cost(size, 6 * size), deps=deps)
        sends = made[: len(parts)]
        vectors = made[-1] if vectors is not None else None
    for p, h in zip(parts, halves):
        p.rows = h
    return sends, vectors


def pack(me, parts, columns, count, name, vectors=None, deps=()):
    rows = min(p.rows for p in parts)
    widths = [c[2] // count for c in columns]
    ahead = 0 if vectors is None else 16 * vectors.shape[1] // rows
    wide = ahead + sum(parts[c[0]].rows // rows * w for c, w in zip(columns, widths))
    ins, counts = [], []
    for p in parts:
        ins += p.inputs(0)
        counts.append(len(p.terms))
    outs = [shaped((2 * rows, wide)), shaped((2 * rows, wide), F32)]
    if vectors is not None:
        sent = parts[0].terms[-1]
        ins += [vectors, (sent, slice(parts[0].rows, parts[0].rows + 16), slice(0, parts[0].cols))]
        outs.append(shaped(vectors.shape, F32))

    def body(scalars, get, out, put, scratch):
        (me_ref,) = scalars
        sums, at = [], 0
        for n in counts:
            sums.append(add_up([get(at + j) for j in range(n)]))
            at += n
        if vectors is not None:
            vec = get(len(ins) - 2)[...] + joined(get(len(ins) - 1)[...])
            out[2][...] = vec
            put(2)
            store_vectors(out[0], vec, rows, ahead)
        for place, (ref, turn) in enumerate([(out[0], 0), (out[0], 1), (out[1], 0), (out[1], 1)]):
            distance = (1, 3, 0, 2)[place]
            for owner in range(count):

                @pl.when((me_ref[0] ^ distance) == owner)
                def _(ref=ref, owner=owner, turn=turn):
                    at = ahead
                    for (which, start, _), w in zip(columns, widths):
                        piece = sums[which][:, start + owner * w : start + (owner + 1) * w].astype(ref.dtype)
                        for j in range(piece.shape[0] // rows):
                            ref[turn * rows : (turn + 1) * rows, at : at + w] = piece[j * rows : (j + 1) * rows]
                            at += w

            if turn == 1:
                put(place // 2)

    size = sum(p.rows * p.cols for p in parts)
    return staged(body, name, [me], ins, outs, cost(2 * size, 6 * size), deps=deps)


def store_vectors(ref, vec, rows, ahead):
    both = split_high(vec)
    for i in range(rows // 16):
        ref[16 * i : 16 * (i + 1), :ahead] = both[:, i * ahead : (i + 1) * ahead]


def load_vectors(ref, rows, ahead):
    return joined(jnp.concatenate([ref[16 * i : 16 * (i + 1), :ahead] for i in range(rows // 16)], 1))


def pack_far(own, recv, name, vectors=None, deps=()):
    rows, wide = own.shape[0] // 2, own.shape[1]
    ahead = 0 if vectors is None else 16 * vectors.shape[1] // rows
    far = slice(rows, 2 * rows)
    ins = [(own, far, slice(0, wide)), (recv, far, slice(0, wide))]
    outs = [shaped((rows, wide))]
    if vectors is not None:
        ins += [vectors, (recv, slice(0, rows), slice(0, ahead))]
        outs.append(shaped(vectors.shape, F32))

    def body(scalars, get, out, put, scratch):
        out[0][:, ahead:] = (get(0)[:, ahead:] + get(1)[:, ahead:].astype(F32)).astype(BF)
        if vectors is not None:
            vec = get(2)[...] + load_vectors(get(3), rows, ahead)
            out[1][...] = vec
            store_vectors(out[0], vec, rows, ahead)

    size = rows * wide
    return staged(body, name, [], ins, outs, cost(size, 10 * size), deps=deps)


def unpack(own, near, far, shapes, name, vectors=None, deps=()):
    rows, wide = far.shape
    this, all_cols = slice(0, rows), slice(0, wide)
    ins = [(own, this, all_cols), (near, this, all_cols), far]
    outs = [shaped(shape, F32) for shape in shapes]
    ahead = 0
    if vectors is not None:
        ahead = 16 * vectors.shape[1] // rows
        width = vectors.shape[1] // 3
        ins.append(vectors)
        outs += [shaped((width,), F32)] * 8 + [shaped((4 * width,), F32)]

    def body(scalars, get, out, put, scratch):
        total = get(0)[:, ahead:] + get(1)[:, ahead:].astype(F32) + get(2)[:, ahead:].astype(F32)
        at = 0
        for i, (height, width) in enumerate(shapes):
            for j in range(height // rows):
                out[i][j * rows : (j + 1) * rows, :] = total[:, at : at + width]
                at += width
            put(i)
        if vectors is not None:
            vec = get(3)[...] + load_vectors(get(2), rows, ahead)
            wide = vec.shape[1] // 3
            base = len(shapes)
            for i in range(2):
                for j in range(4):
                    out[base + 4 * i + j][...] = vec[j : j + 1, i * wide : (i + 1) * wide].reshape(wide)
            for j in range(4):
                out[base + 8][j * wide : (j + 1) * wide] = vec[j : j + 1, 2 * wide :].reshape(wide)

    size = rows * wide
    return staged(body, name, [], ins, outs, cost(size, 12 * size), deps=deps)


def spec_sum(part, me, count):
    cols = part.shape[1] // count

    def mine(distance):
        return lax.dynamic_slice_in_dim(part, (me ^ distance) * cols, cols, 1)

    got = [lax.ppermute(mine(d).astype(BF), "spec", flip(count, d)) for d in range(1, count)]
    total = mine(0)
    for piece in got:
        total = total + piece.astype(F32)
    return total


def local(
    tokens,
    cotangent,
    lengths,
    projection,
    query_bias,
    value_bias,
    output_weight,
    output_bias,
    up_weight,
    up_bias,
    down_weight,
    down_bias,
    first_gain,
    first_shift,
    second_gain,
    second_shift,
):
    _, rows, width = tokens.shape
    hidden = up_weight.shape[1]
    cubes, count = lax.axis_size("cube"), lax.axis_size("spec")
    cube, spec = lax.axis_index("cube"), lax.axis_index("spec")
    tok = tokens.reshape(rows, width)
    cot = cotangent.reshape(rows, width)

    assert count == 4
    half_way = count // 2

    def partner(c, s):
        return (c ^ 1, s ^ half_way) if (c & 1) != (s // half_way) else (c, s)

    places = [(c, s) for c in range(cubes) for s in range(count)]

    def both_axes(move):
        return [(c * count + s, move(c, s)[0] * count + move(c, s)[1]) for c, s in places]

    exchange = both_axes(partner)
    diagonal = both_axes(lambda c, s: (c ^ 1, s ^ 1))
    pair = flip(cubes, 1)
    near = flip(count, 1)
    axes = ("cube", "spec")

    own_tok = tok
    tok = lax.ppermute(own_tok, axes, exchange)
    away = (cube & 1) != (spec // half_way)
    length = jnp.where(away, lax.ppermute(lengths, "cube", pair), lengths)[0].astype(jnp.int32)
    my_block = jnp.where(away, spec ^ half_way, spec).astype(jnp.int32)
    next_tok = lax.ppermute(tok, "spec", near)
    blocks = [tok, lax.ppermute(tok, "cube", pair), next_tok, lax.ppermute(next_tok, "cube", pair)]
    distances = [0, half_way, 1, half_way + 1]
    wheres = [jnp.stack([(my_block ^ d) * rows, length]) for d in distances]

    bits = cubes.bit_length() - 1
    order_a = list(range(bits))
    order_b = [0] + list(range(bits - 1, 0, -1))
    place_a, place_b = tree_place(order_a), tree_place(order_b)
    split = cubes // 2

    def source_rows(place, offset, size, block):
        start = (jnp.asarray(place, jnp.int32) ^ cube) * block + offset
        return (start[:, None] + jnp.arange(size, dtype=jnp.int32)[None, :]).reshape(-1)

    def one_hot(source):
        return (source[:, None] == jnp.arange(width, dtype=jnp.int32)[None, :]).astype(BF)

    block = width // cubes
    part = block // 2
    perm_b = one_hot(source_rows(place_b, 0, block, block))
    perm_mixed = one_hot(
        jnp.concatenate(
            [
                source_rows(place_a[:split], 0, part, block),
                source_rows(place_b[:split], part, part, block),
                source_rows(place_a[split:], 0, part, block),
                source_rows(place_b[split:], part, part, block),
            ]
        )
    )
    chunks = 8
    if cubes == chunks:
        order = jnp.asarray(place_a, jnp.int32) ^ cube
    else:
        order = jnp.arange(chunks, dtype=jnp.int32)

    up_bias_row = up_bias.reshape(chunks, -1)
    hiddens, keys, values = [], [], []
    state = None
    for which in ((0, 1), (2,), (3,)):
        made = forward_step(
            which[-1] == count - 1,
            [wheres[i] for i in which],
            [blocks[i] for i in which],
            first_gain,
            first_shift,
            projection,
            query_bias,
            value_bias,
            state,
            cot,
            (perm_b, perm_mixed, order, up_bias_row) if state is None else (),
        )
        for i in range(len(which)):
            hiddens.append(made[3 + 3 * i])
            keys.append(made[4 + 3 * i])
            values.append(made[5 + 3 * i])
        if state is None:
            q, qt, cot = made[3 + 3 * len(which) :]
            cot = lax.ppermute(cot, axes, exchange)
        state = (qt,) + tuple(made[:3])
    negl, attt = state[1], state[3]

    (
        block_out,
        down_keep,
        down_send,
        up_keep,
        up_send,
        da,
        dat,
        negd,
        gmid,
        vec_mid,
        grad_up_bias,
    ) = middle_step(
        order,
        tok,
        cot,
        attt,
        output_weight,
        output_bias,
        second_gain,
        second_shift,
        up_weight,
        up_bias_row,
        down_weight,
        down_bias,
        perm_b,
    )
    if cubes != chunks:
        whole = jnp.concatenate([down_keep, down_send], 0).reshape(cubes, hidden // cubes, width)
        whole = jnp.take(whole, jnp.asarray(place_a, jnp.int32) ^ cube, axis=0)
        down_keep = whole[:split].reshape(hidden // 2, width)
        down_send = whole[split:].reshape(hidden // 2, width)

    block_out = lax.ppermute(block_out, axes, exchange)
    down_recv = lax.ppermute(down_send, "cube", pair)
    up_recv = lax.ppermute(up_send, "cube", pair)

    common = (q, qt, da, dat, negl, negd)

    def back(which, state, last, deps):
        def pick(things):
            return [things[i] for i in which]

        return backward_step(
            pick(wheres), *common, pick(keys), pick(values), pick(blocks), projection, state, last, deps
        )

    dkv_3, g_3, dkv_2, g_2, vec_back, dqt = back((3, 2), None, False, ())
    g_3 = lax.ppermute(g_3, axes, diagonal)
    g_2 = lax.ppermute(g_2, "spec", near)

    def hop(parts, sends, level):
        for p, send, order in zip(parts, sends, (order_a, order_b)):
            p.terms.append(lax.ppermute(send, "cube", flip(cubes, 1 << order[level])))

    levels = len(order_a)
    me = spec.astype(jnp.int32).reshape(1)
    ff = [Part(down_keep, down_recv), Part(up_keep, up_recv)]
    last = dqt
    if levels > 1:
        sends, _ = halve(ff, "sum_ff", None, (last, block_out))
        last = sends[0]
        hop(ff, sends, 1)
    dkv_1, g_1, dkv_0, g_0, vec_back, dq = back((1, 0), (dqt, vec_back), True, (last,))
    g_1 = lax.ppermute(g_1, "cube", pair)

    proj_a, proj_b, send_a, send_b, vectors = projection_step(
        perm_mixed, dq, hiddens, [dkv_0, dkv_1, dkv_2, dkv_3], vec_mid, grad_up_bias, vec_back, (g_2, g_3)
    )
    proj = [
        Part(proj_a, lax.ppermute(send_a, "cube", pair)),
        Part(proj_b, lax.ppermute(send_b, "cube", pair)),
    ]
    last = vectors
    for level in range(2, levels):
        sends, _ = halve(ff, "sum_ff", None, (last,))
        last = sends[0]
        hop(ff, sends, level)
    grad_tokens = final_step(tok, first_gain, gmid, g_0, [g_1, g_2, g_3], (last,))
    last = grad_tokens
    grad_tokens = lax.ppermute(grad_tokens, axes, exchange)
    aligned = width // cubes % 32 == 0
    far = flip(count, 2)
    for level in range(1, levels):
        sends, vectors = halve(proj, "sum_proj", vectors, (last,))
        last = sends[0]
        hop(proj, sends, level)
        if level == 1 and aligned:
            columns = [(1, 0, hidden), (1, hidden, width), (0, 0, width)]
            ff_send, ff_own = pack(me, ff, columns, count, "pack_ff", None, (last,))
            last = ff_own
            ff_near = lax.ppermute(ff_send, "spec", near)
    if aligned:
        (ff_send,) = pack_far(ff_own, ff_near, "pack_ff_far", None, (last,))
        ff_far = lax.ppermute(ff_send, "spec", far)
        pr_send, pr_own, vectors = pack(
            me, proj, [(0, 0, 3 * width), (1, 0, 3 * width)], count, "pack_proj", vectors, (ff_send, grad_tokens)
        )
        pr_near = lax.ppermute(pr_send, "spec", near)
        grad_up, grad_out, grad_down = unpack(
            ff_own,
            ff_near,
            ff_far,
            [(width // cubes, hidden // count), (width // cubes, width // count), (hidden // cubes, width // count)],
            "unpack_ff",
            None,
            (pr_own,),
        )
        pr_send, vectors = pack_far(pr_own, pr_near, "pack_proj_far", vectors, (grad_out,))
        pr_far = lax.ppermute(pr_send, "spec", far)
        shapes = [(width // cubes, 3 * width // count)]
        grad_proj, *vectors = unpack(pr_own, pr_near, pr_far, shapes, "unpack_proj", vectors)
    else:
        vectors = vectors + joined(proj[0].terms[-1][-16:])
        vectors = sum([lax.ppermute(vectors, "spec", flip(count, d)) for d in range(1, count)], vectors)
        grad_up_out = ff[1].total()
        grad_up = spec_sum(grad_up_out[:, :hidden], spec, count)
        grad_out = spec_sum(grad_up_out[:, hidden:], spec, count)
        grad_down = spec_sum(ff[0].total(), spec, count)
        grad_proj = spec_sum(jnp.concatenate([p.total() for p in proj], 0), spec, count)
        vectors = [vectors[j, i * width : (i + 1) * width] for i in range(2) for j in range(4)] + [
            vectors[:4, 2 * width :].reshape(-1)
        ]

    grad_tokens = grad_tokens.astype(F32)

    return (
        block_out.reshape(tokens.shape),
        grad_tokens.reshape(tokens.shape),
        grad_proj,
        vectors[4],
        vectors[5],
        grad_out,
        vectors[3],
        grad_up,
        vectors[8],
        grad_down,
        vectors[0],
        vectors[6],
        vectors[7],
        vectors[1],
        vectors[2],
    )


def solution(mesh):
    return jax.shard_map(
        local,
        mesh=mesh,
        in_specs=(
            P("cube", "spec", None),
            P("cube", "spec", None),
            P("cube"),
        )
        + (P(),) * 13,
        out_specs=(
            P("cube", "spec", None),
            P("cube", "spec", None),
            P("cube", "spec"),
            P(),
            P(),
            P("cube", "spec"),
            P(),
            P("cube", "spec"),
            P(),
            P("cube", "spec"),
            P(),
            P(),
            P(),
            P(),
            P(),
        ),
        check_vma=False,
    )
```

```python
import math
from functools import partial

import jax
import jax.numpy as jnp
import numpy as np
from jax import lax
from jax.experimental import pallas as pl
from jax.experimental.pallas import tpu as pltpu
from jax.sharding import PartitionSpec as P

HEADS = 12
HD = 64
PAIRS = HEADS // 2
EPS = 1e-06
SCALE = HD ** (-0.5)
TO_EXP2 = SCALE * math.log2(math.e)
MASKED = -1e30

BF = jnp.bfloat16
F32 = jnp.float32


def dot(left, right):
    return jnp.dot(left, right, preferred_element_type=F32)


def dot_nt(left, right):
    return lax.dot_general(left, right, (((1,), (1,)), ((), ())), preferred_element_type=F32)


def dot_tn(left, right):
    return lax.dot_general(left, right, (((0,), (0,)), ((), ())), preferred_element_type=F32)


def normalize(values):
    average = jnp.mean(values, -1, keepdims=True)
    centred = values - average
    inverse = lax.rsqrt(jnp.mean(centred * centred, -1, keepdims=True) + EPS)
    return centred * inverse, inverse


def params(megabytes=64):
    return pltpu.CompilerParams(vmem_limit_bytes=megabytes * 2**20)


def cost(flops, nbytes, trans=0):
    return pl.CostEstimate(flops=flops // 1000, bytes_accessed=nbytes // 1000, transcendentals=trans // 1000)


def extra_lanes(ids_ref, distance, rows, ones):
    slot = lax.broadcasted_iota(jnp.int32, (rows, 128), 0) + (ids_ref[1] ^ distance) * rows
    lane = lax.broadcasted_iota(jnp.int32, (rows, 128), 1)
    masked = jnp.where(slot < ids_ref[2], 0.0, MASKED)
    rest = jnp.where(lane <= ones, 1.0, 0.0)
    return jnp.where(lane == 0, masked, rest).astype(BF)


def two_heads(part, extra):
    n = part.shape[1]
    zero = jnp.zeros((HD, n), part.dtype)
    left = jnp.concatenate([part[:HD], zero], 0)
    right = jnp.concatenate([zero, part[HD:]], 0)
    return jnp.concatenate([jnp.concatenate([left, right], 1), extra], 0)


def as_row(ref):
    return ref[...].reshape(1, -1)


def pair_lanes(pair):
    return slice(pair * 2 * HD, (pair + 1) * 2 * HD)


ANY = pl.BlockSpec(memory_space=pl.ANY)
SMEM = pl.BlockSpec(memory_space=pltpu.SMEM)


def staged(body, name, scalars, ins, outs, estimate, scratch=(), deps=()):
    parts = [x if isinstance(x, tuple) else (x, slice(0, x.shape[0]), slice(0, x.shape[-1])) for x in ins]
    shapes = []
    for x, rows, cols in parts:
        shapes.append((rows.stop - rows.start,) if x.ndim == 1 else (rows.stop - rows.start, cols.stop - cols.start))
    arrays = []
    for x, _, _ in parts:
        if not any(x is y for y in arrays):
            arrays.append(x)
    index = [[i for i, y in enumerate(arrays) if y is x][0] for x, _, _ in parts]
    n_s, n_a, n_i, n_o, n_x = len(scalars), len(arrays), len(ins), len(outs), len(scratch)

    def kernel(*refs):
        at = 0
        groups = []
        for n in (n_s, n_a, len(deps), n_o, n_x, n_i, n_o):
            groups.append(refs[at : at + n])
            at += n
        s_refs, a_ref, _, o_to, x_refs, i_ref, o_ref = groups
        i_sem, o_sem = refs[at:]
        loads = []
        for i, (x, rows, cols) in enumerate(parts):
            source = a_ref[index[i]]
            if shapes[i] != x.shape:
                source = source.at[rows, cols]
            loads.append(pltpu.make_async_copy(source, i_ref[i], i_sem.at[i]))
        stores = [pltpu.make_async_copy(o_ref[i], o_to[i], o_sem.at[i]) for i in range(n_o)]
        for load in loads:
            load.start()
        waited = set()
        sent = set()

        def get(i):
            if i not in waited:
                waited.add(i)
                loads[i].wait()
            return i_ref[i]

        def put(i, *where):
            sent.add(i)
            if where:
                pltpu.make_async_copy(o_ref[i].at[where], o_to[i].at[where], o_sem.at[i]).start()
            else:
                stores[i].start()

        body(s_refs, get, o_ref, put, x_refs)
        for i in range(n_i):
            get(i)
        for i in range(n_o):
            if i not in sent:
                put(i)
        for store in stores:
            store.wait()

    return pl.pallas_call(
        kernel,
        out_shape=list(outs),
        in_specs=[SMEM] * n_s + [ANY] * (n_a + len(deps)),
        out_specs=[ANY] * n_o,
        scratch_shapes=list(scratch)
        + [pltpu.VMEM(shape, x.dtype) for shape, (x, _, _) in zip(shapes, parts)]
        + [pltpu.VMEM(x.shape, x.dtype) for x in outs]
        + [pltpu.SemaphoreType.DMA((n_i,)), pltpu.SemaphoreType.DMA((n_o,))],
        compiler_params=params(),
        cost_estimate=estimate,
        name=name,
    )(*scalars, *arrays, *deps)


def shaped(shape, dtype=BF):
    return jax.ShapeDtypeStruct(shape, dtype)


def forward_step(last, ids, distances, toks, gain, shift, w, qb, vb, state, through, deps=()):
    first = state is None
    count = len(toks)
    rows, width = toks[0].shape
    block = shaped((rows, width))
    outs = [shaped((8, 2 * rows), F32), shaped((8, 2 * rows), F32), shaped((width, rows), F32)]
    outs += [block, block, block] * count
    full = slice(0, width)
    ins = [toks[0], gain, shift, vb, (w, full, slice(width, 2 * width)), (w, full, slice(2 * width, 3 * width))]
    if first:
        ins += [(w, full, full), qb]
        outs += [block, shaped((width, rows)), block]
    else:
        ins += list(state)
    at_tok = len(ins) - 1
    ins += toks[1:]
    if first:
        ins.append(through)

    def body(scalars, get, out, put, scratch):
        m_out, l_out, acc_out = out[:3]
        ones_row = (lax.broadcasted_iota(jnp.int32, (128, 2 * rows), 0) == 0).astype(BF)
        for i in range(count):
            h_out, k_out, v_out = out[3 + 3 * i : 6 + 3 * i]
            normed, _ = normalize(get(at_tok + i if i > 0 else 0)[...].astype(F32))
            hidden = (normed * as_row(get(1)) + as_row(get(2))).astype(BF)
            h_out[...] = hidden
            put(3 + 3 * i)
            k_out[...] = dot(hidden, get(4)[...]).astype(BF)
            put(4 + 3 * i)
            values = dot(hidden, get(5)[...]) + as_row(get(3))
            v_out[...] = values.astype(BF)
            put(5 + 3 * i)
            values_t = v_out[...].astype(F32).T.astype(BF)
            if first:
                at = 3 + 3 * count
                q_out, qt_out, through_out = out[at:]
                if i == 0:
                    q_out[...] = (dot(hidden, get(6)[...]) + as_row(get(7))).astype(BF)
                    put(at)
                    qt_out[...] = q_out[...].astype(F32).T.astype(BF)
                    put(at + 1)
                if i == count - 1:
                    through_out[...] = get(len(ins) - 1)[...]
                    put(at + 2)
                qt_ref = qt_out
            else:
                qt_ref = get(6)
            extra_keys = extra_lanes(scalars[0], distances[i], rows, 0)
            start = first and i == 0
            end = last and i == count - 1
            for pair in range(PAIRS):
                lanes = pair_lanes(pair)
                this = slice(pair, pair + 1)
                keys = jnp.concatenate([k_out[:, lanes], extra_keys], 1)
                scores = dot(keys, two_heads(qt_ref[lanes, :], ones_row))
                top = jnp.max(scores, 0, keepdims=True)
                if not start:
                    m_ref, l_ref, acc_ref = (get(7 + j) for j in range(3)) if i == 0 else (m_out, l_out, acc_out)
                    before = m_ref[this, :]
                    top = jnp.maximum(top, before)
                    fade = jnp.exp2((before - top) * TO_EXP2)
                weights = jnp.exp2((scores - top) * TO_EXP2)
                total = jnp.sum(weights, 0, keepdims=True)
                if not start:
                    total = total + l_ref[this, :] * fade
                both = dot(values_t[lanes, :], weights.astype(BF))
                for head in range(2):
                    own = slice(lanes.start + head * HD, lanes.start + (head + 1) * HD)
                    cols = slice(head * rows, (head + 1) * rows)
                    part = both[head * HD : (head + 1) * HD, cols]
                    if not start:
                        part = part + acc_ref[own, :] * fade[:, cols]
                    if end:
                        part = part / total[:, cols]
                    acc_out[own, :] = part
                m_out[this, :] = -(top + jnp.log2(total) * (1.0 / TO_EXP2)) if end else top
                l_out[this, :] = total
                if i == count - 1:
                    put(2, lanes)

    estimate = pl.CostEstimate(flops=count * 10**10, bytes_accessed=24 * 2**20, transcendentals=0)
    return staged(body, "attend", [ids], ins, outs, estimate, deps=deps)


def make_perm(ref, me, blocks, firsts, size, block):
    here = lax.broadcasted_iota(jnp.int32, (size, ref.shape[1]), 0)
    there = lax.broadcasted_iota(jnp.int32, (size, ref.shape[1]), 1)
    for i, (relative, first) in enumerate(zip(blocks, firsts)):
        start = (me ^ relative) * block + first
        ref[i * size : (i + 1) * size, :] = (here + start == there).astype(F32).astype(BF)


def middle_step(ids, places, tok, cot, attt, wo, ob, gain, shift, up, ub, down, db, perm):
    rows, width = tok.shape
    hidden = up.shape[1]
    chunks = 8
    chunk = hidden // chunks
    half = width // 2
    given = not isinstance(perm, tuple)
    ins = [attt, wo, ob, tok, gain, shift, up, ub, cot, down, db] + ([perm] if given else [])
    outs = [
        shaped((rows, width)),
        shaped((hidden // 2, width)),
        shaped((hidden // 2, width)),
        shaped((half, hidden + width)),
        shaped((half, hidden + width)),
        shaped((rows, width)),
        shaped((width, rows)),
        shaped((8, 2 * rows), F32),
        shaped((rows, width), F32),
        shaped((8, width), F32),
        shaped((8, chunk), F32),
    ]
    scratch = [
        pltpu.VMEM((rows, width), F32),
        pltpu.VMEM((rows, width), F32),
        pltpu.VMEM((rows, width), BF),
        pltpu.VMEM((width, rows), BF),
        pltpu.VMEM((rows, width), BF),
        pltpu.VMEM((rows, width), F32),
        pltpu.VMEM((rows, width), F32),
        pltpu.VMEM((width, width), BF),
    ]

    def body(scalars, get, out, put, scratch):
        (ids_ref,) = scalars
        block_out, down_keep, down_send, up_keep, up_send, da_out, dat_out, negd_out, gmid_out, vec_out, ubg_out = out
        mid_ref, norm_ref, h2_ref, h2t_ref, att_ref, res_ref, gh_ref, perm_ref = scratch
        if given:
            perm_ref[...] = get(11)[...]
        else:
            make_perm(perm_ref, ids_ref[0], *perm)
        attt_ref = get(0)
        att_ref[...] = attt_ref[...].T.astype(BF)
        projected = dot(att_ref[...], get(1)[...]) + as_row(get(2))
        middle = get(3)[...].astype(F32) + projected
        mid_ref[...] = middle
        normed, inverse = normalize(middle)
        norm_ref[...] = normed
        h2_ref[...] = (normed * as_row(get(4)) + as_row(get(5))).astype(BF)
        h2t_ref[...] = dot_nt(perm_ref[...], h2_ref[...]).astype(BF)
        up_ref, ub_ref, cot_ref, down_ref = get(6), get(7), get(8), get(9)
        for turn in range(chunks // 2):
            p = (2 * turn + chunks // 2) % chunks
            own = [p, p + 1] if places is None else [places[p] ^ ids_ref[0], places[p + 1] ^ ids_ref[0]]
            at = [pl.ds(pl.multiple_of(place * chunk, 128), chunk) for place in own]
            up_c = jnp.concatenate([up_ref[:, a] for a in at], 1)
            down_c = jnp.concatenate([down_ref[a, :] for a in at], 0)
            bias = jnp.concatenate([ub_ref[pl.ds(place, 1), :] for place in own], 1)
            before = dot(h2_ref[...], up_c) + bias
            cdf = 0.5 * (1.0 + lax.erf(before * math.sqrt(0.5)))
            slope = cdf + before * (jnp.exp(-0.5 * before * before) * (1.0 / math.sqrt(2.0 * math.pi)))
            lifted = (before * cdf).astype(BF)
            grad_lifted = dot_nt(cot_ref[...], down_c)
            grad_down = dot_tn(lifted, cot_ref[...]).astype(BF)
            to, first = (down_keep, p) if p < chunks // 2 else (down_send, p - chunks // 2)
            rows_to = pl.ds(first * chunk, 2 * chunk)
            to[rows_to, :] = grad_down
            put(1 if p < chunks // 2 else 2, rows_to)
            grad_before = (grad_lifted * slope).astype(BF)
            bias_grad = jnp.sum(grad_before.astype(F32), 0, keepdims=True)
            for i, place in enumerate(own):
                ubg_out[pl.ds(place, 1), :] = bias_grad[:, i * chunk : (i + 1) * chunk]
            grad_up = dot(h2t_ref[...], grad_before).astype(BF)
            for i, a in enumerate(at):
                cols = slice(i * chunk, (i + 1) * chunk)
                up_keep[:, a] = grad_up[:half, cols]
                up_send[:, a] = grad_up[half:, cols]
                put(3, slice(None), a)
                put(4, slice(None), a)
            part = dot(lifted, down_c)
            back = dot_nt(grad_before, up_c)
            if turn == 0:
                res_ref[...] = part
                gh_ref[...] = back
            else:
                res_ref[...] += part
                gh_ref[...] += back
        block_out[...] = (mid_ref[...] + (res_ref[...] + as_row(get(10)))).astype(BF)
        put(0)
        cot32 = cot_ref[...].astype(F32)
        grad = gh_ref[...]
        normed = norm_ref[...]
        vec_out[0:1, :] = jnp.sum(cot32, 0, keepdims=True)
        vec_out[1:2, :] = jnp.sum(grad * normed, 0, keepdims=True)
        vec_out[2:3, :] = jnp.sum(grad, 0, keepdims=True)
        scaled = grad * as_row(get(4))
        grad_middle = cot32 + inverse * (
            scaled
            - jnp.mean(scaled, -1, keepdims=True)
            - normed * jnp.mean(scaled * normed, -1, keepdims=True)
        )
        gmid_out[...] = grad_middle
        put(8)
        branch = grad_middle.astype(BF)
        vec_out[3:4, :] = jnp.sum(branch.astype(F32), 0, keepdims=True)
        vec_out[4:8, :] = jnp.zeros((4, width), F32)
        att_t = dot_nt(perm_ref[...], att_ref[...]).astype(BF)
        grad_out = dot(att_t, branch).astype(BF)
        cols = pl.ds(hidden, width)
        up_keep[:, cols] = grad_out[:half]
        up_send[:, cols] = grad_out[half:]
        put(3, slice(None), cols)
        put(4, slice(None), cols)
        grad_att = dot_nt(branch, get(1)[...]).astype(BF)
        da_out[...] = grad_att
        put(5)
        grad_att_t = grad_att.astype(F32).T
        dat_out[...] = grad_att_t.astype(BF)
        put(6)
        product = grad_att_t * attt_ref[...]
        for head in range(HEADS):
            spread = jnp.sum(product[head * HD : (head + 1) * HD], 0, keepdims=True)
            place = slice((head % 2) * rows, (head % 2 + 1) * rows)
            negd_out[head // 2 : head // 2 + 1, place] = -spread

    estimate = cost(12 * rows * width * hidden + 6 * rows * width * width, 30 * 2**20, 0)
    return staged(body, "middle", [ids], ins, outs, estimate, scratch)


def three_parts(row):
    high = row.astype(BF)
    rest = row - high.astype(F32)
    mid = rest.astype(BF)
    low = (rest - mid.astype(F32)).astype(BF)
    return high.astype(F32), mid.astype(F32), low.astype(F32)


def extra_rows(row, with_mask):
    n = row.shape[1]
    high, mid, low = three_parts(row)
    place = lax.broadcasted_iota(jnp.int32, (128, n), 0)
    out = jnp.where(place == 0, 1.0 if with_mask else 0.0, 0.0)
    out = jnp.where(place == 1, high, out)
    out = jnp.where(place == 2, mid, out)
    out = jnp.where(place == 3, low, out)
    return out.astype(BF)


def backward_step(ids, distances, q, qt, da, dat, negl, negd, keys, values, toks, w, state, last, deps, arrived=None, through=None):
    rows, width = q.shape
    blocks = len(keys)
    first = state is None
    ins = [qt, negl, dat, negd, q, da]
    for k, v in zip(keys, values):
        ins += [k, v]
    base_w = len(ins)
    ins += [w, *toks]
    base_state = len(ins)
    if not first:
        ins += list(state)
    at_extra = len(ins)
    ins += [x for x in (arrived, through) if x is not None]
    outs = []
    for i in range(blocks):
        outs += [shaped((rows, 2 * width)), shaped((rows, width), F32 if last and i == blocks - 1 else BF)]
    outs += [shaped((8, width), F32), shaped((rows, width)) if last else shaped((width, rows), F32)]
    if through is not None:
        outs.append(shaped(through.shape, through.dtype))

    def body(scalars, get, out, put, scratch):
        (dqt,) = scratch
        vec_out, end_out = out[2 * blocks : 2 * blocks + 2]
        lane = lax.broadcasted_iota(jnp.int32, (rows, 128), 1)
        zero = jnp.zeros((rows, 128), BF)
        value_bias = gain = shift = jnp.zeros((1, width), F32)
        query_bias = jnp.zeros((1, width), F32)
        for i in range(blocks):
            dkv_out, g_out = out[2 * i], out[2 * i + 1]
            extra_keys = extra_lanes(scalars[0], distances[i], rows, 3)
            qt_ref, negl_ref, dat_ref, negd_ref = get(0), get(1), get(2), get(3)
            k_ref, v_ref = get(6 + 2 * i), get(7 + 2 * i)
            keys_t = k_ref[...].astype(F32).T.astype(BF)
            for pair in range(PAIRS):
                lanes = pair_lanes(pair)
                key = jnp.concatenate([k_ref[:, lanes], extra_keys], 1)
                scores = dot(key, two_heads(qt_ref[lanes, :], extra_rows(negl_ref[pair : pair + 1, :], True)))
                softmaxed = jnp.exp2(scores * TO_EXP2)
                value = jnp.concatenate([v_ref[:, lanes], extra_keys], 1)
                centred = dot(value, two_heads(dat_ref[lanes, :], extra_rows(negd_ref[pair : pair + 1, :], False)))
                grad_scores = (softmaxed * centred).astype(BF)
                weights = softmaxed.astype(BF)
                q_pair = get(4)[:, lanes]
                da_pair = get(5)[:, lanes]
                q_both = jnp.concatenate([jnp.where(lane < HD, q_pair, zero), jnp.where(lane < HD, zero, q_pair)], 0)
                da_both = jnp.concatenate([jnp.where(lane < HD, da_pair, zero), jnp.where(lane < HD, zero, da_pair)], 0)
                dkv_out[:, lanes] = (dot(grad_scores, q_both) * SCALE).astype(BF)
                dkv_out[:, slice(width + lanes.start, width + lanes.stop)] = dot(weights, da_both).astype(BF)
                both = dot(keys_t[lanes, :], grad_scores)
                for head in range(2):
                    own = slice(lanes.start + head * HD, lanes.start + (head + 1) * HD)
                    part = both[head * HD : (head + 1) * HD, head * rows : (head + 1) * rows]
                    if i > 0:
                        part = part + dqt[own, :]
                    elif not first:
                        part = part + get(base_state)[own, :]
                    dqt[own, :] = part
            put(2 * i)
            w_ref = get(base_w)
            grad = dot_nt(dkv_out[...], w_ref[:, width:])
            if last and i == blocks - 1:
                dq = (dqt[...].T * SCALE).astype(BF)
                end_out[...] = dq
                put(2 * blocks + 1)
                query_bias = jnp.sum(dq.astype(F32), 0, keepdims=True)
                grad = grad + dot_nt(dq, w_ref[:, :width])
            if arrived is not None and i == 0:
                g_out[...] = (grad + get(at_extra)[...].astype(F32)).astype(g_out.dtype)
            else:
                g_out[...] = grad.astype(g_out.dtype)
            put(2 * i + 1)
            normed, _ = normalize(get(base_w + 1 + i)[...].astype(F32))
            value_bias = value_bias + jnp.sum(dkv_out[:, width:].astype(F32), 0, keepdims=True)
            gain = gain + jnp.sum(grad * normed, 0, keepdims=True)
            shift = shift + jnp.sum(grad, 0, keepdims=True)
        if not last:
            end_out[...] = dqt[...]
        if through is not None:
            out[2 * blocks + 2][...] = get(len(ins) - 1)[...]
        if not first:
            vec_ref = get(base_state + 1)
            value_bias = value_bias + vec_ref[1:2, :]
            gain = gain + vec_ref[2:3, :]
            shift = shift + vec_ref[3:4, :]
        vec_out[0:1, :] = query_bias
        vec_out[1:2, :] = value_bias
        vec_out[2:3, :] = gain
        vec_out[3:4, :] = shift
        vec_out[4:8, :] = jnp.zeros((4, width), F32)

    flops = blocks * (2 * rows * width * width * 3 + 10 * rows * rows * width * 4)
    estimate = cost(flops, 20 * 2**20, blocks * HEADS * rows * rows)
    return staged(
        body, "attend_back", [ids], ins, outs, estimate, [pltpu.VMEM((width, rows), F32)], deps
    )


def projection_step(ids, perm, dq, hiddens, dkvs, vec_mid, vec_up, vec_back, deps):
    rows, width = dq.shape
    count = len(hiddens)
    part = width // 4
    given = not isinstance(perm, tuple)
    ins = [*hiddens, dq, vec_mid, vec_up, vec_back, *dkvs] + ([perm] if given else [])
    outs = [shaped((n, 3 * width)) for n in (part, part, part + 16, part)] + [shaped((8, 3 * width), F32)]
    at = count

    def body(scalars, get, out, put, scratch):
        ht_ref, perm_ref = scratch
        if given:
            perm_ref[...] = get(len(ins) - 1)[...]
        else:
            make_perm(perm_ref, scalars[0][0], *perm)
        keep_a, keep_b, send_a, send_b, vec_ref = out
        for i in range(count):
            ht_ref[:, i * rows : (i + 1) * rows] = dot_nt(perm_ref[...], get(i)[...]).astype(BF)
        vec_ref[0:4, :width] = get(at + 1)[0:4, :]
        vec_ref[0:4, width : 2 * width] = get(at + 3)[0:4, :]
        up = jnp.concatenate([get(at + 2)[i : i + 1, :] for i in range(get(at + 2).shape[0])], 1)
        for i in range(4):
            vec_ref[i : i + 1, 2 * width :] = up[:, i * width : (i + 1) * width]
        vec_ref[4:8, :] = jnp.zeros((4, 3 * width), F32)
        send_a[part:, :] = split_high(vec_ref[...])
        put(4)
        for third in range(3):
            if third == 0:
                grad = dot(ht_ref[:, :rows], get(at)[...])
            else:
                own = slice((third - 1) * width, third * width)
                grad = dot(ht_ref[...], jnp.concatenate([get(at + 4 + i)[:, own] for i in range(count)], 0))
            grad = grad.astype(BF)
            cols = pl.ds(third * width, width)
            send_a[:part, cols] = grad[2 * part : 3 * part]
            put(2, slice(None), cols)
            send_b[:, cols] = grad[3 * part :]
            put(3, slice(None), cols)
            keep_a[:, cols] = grad[:part]
            put(0, slice(None), cols)
            keep_b[:, cols] = grad[part : 2 * part]
            put(1, slice(None), cols)

    estimate = cost(2 * rows * width * width * (1 + 2 * count), 12 * 2**20, 0)
    return staged(
        body,
        "projection_grad",
        [ids],
        ins,
        outs,
        estimate,
        [pltpu.VMEM((width, count * rows), BF), pltpu.VMEM((width, width), BF)],
        deps,
    )


def final_step(tok, gain, gmid, g, pieces, block_out, deps=()):
    def body(scalars, get, out, put, scratch):
        normed, inverse = normalize(get(0)[...].astype(F32))
        total = get(3)[...]
        for i in range(len(pieces)):
            total = total + get(4 + i)[...].astype(F32)
        scaled = total * as_row(get(1))
        out[0][...] = (
            get(2)[...]
            + inverse
            * (
                scaled
                - jnp.mean(scaled, -1, keepdims=True)
                - normed * jnp.mean(scaled * normed, -1, keepdims=True)
            )
        ).astype(BF)
        put(0)
        out[1][...] = get(len(ins) - 1)[...]

    estimate = cost(20 * tok.size, 12 * tok.size, 0)
    ins = [tok, gain, gmid, g, *pieces, block_out]
    return staged(body, "norm_back", [], ins, [shaped(tok.shape)] * 2, estimate, deps=deps)


def flip(count, distance):
    return [(i, i ^ distance) for i in range(count)]


def tree_place(bits):
    n = len(bits)
    return np.array([sum(((p >> (n - 1 - i)) & 1) << bit for i, bit in enumerate(bits)) for p in range(1 << n)])


def split_high(values):
    high = values.astype(BF)
    return jnp.concatenate([high.astype(F32), values - high.astype(F32)], 0).astype(BF)


def joined(both):
    both = both.astype(F32)
    return both[:8] + both[8:]


class Part:
    def __init__(self, keep, recv):
        self.terms, self.rows, self.cols = [keep, recv], keep.shape[0], keep.shape[1]

    def inputs(self, start):
        return [(x, slice(start, self.rows), slice(0, self.cols)) for x in self.terms]

    def total(self):
        return sum(x[: self.rows].astype(F32) for x in self.terms)


def add_up(refs):
    total = refs[0][...].astype(F32)
    for ref in refs[1:]:
        total = total + ref[...].astype(F32)
    return total


def halve(parts, name, vectors=None, deps=(), through=None):
    halves = [p.rows // 2 for p in parts]
    if any(h % 16 for h in halves):
        sends = [p.total()[h:].astype(BF) for p, h in zip(parts, halves)]
        if vectors is not None:
            vectors = vectors + joined(parts[0].terms[-1][parts[0].rows :])
            sends[0] = jnp.concatenate([sends[0], split_high(vectors)], 0)
        vectors = through if vectors is None else vectors
    else:
        ins, counts = [], []
        for p, h in zip(parts, halves):
            ins += p.inputs(h)
            counts.append(len(p.terms))
        outs = [shaped((h, p.cols)) for p, h in zip(parts, halves)]
        if vectors is not None:
            sent, rows = parts[0].terms[-1], parts[0].rows
            ins += [vectors, (sent, slice(rows, rows + 16), slice(0, parts[0].cols))]
            outs[0] = shaped((halves[0] + 16, parts[0].cols))
            outs.append(shaped(vectors.shape, F32))
        if through is not None:
            ins.append(through)
            outs.append(shaped(through.shape, through.dtype))

        def body(scalars, get, out, put, scratch):
            at = 0
            for i, (n, h) in enumerate(zip(counts, halves)):
                out[i][:h, :] = add_up([get(at + j) for j in range(n)]).astype(BF)
                at += n
                if vectors is not None and i == 0:
                    total = get(len(ins) - 2)[...] + joined(get(len(ins) - 1)[...])
                    out[len(outs) - 1][...] = total
                    out[0][h:, :] = split_high(total)
                put(i)
            if through is not None:
                out[len(outs) - 1][...] = get(len(ins) - 1)[...]

        size = sum(h * p.cols for p, h in zip(parts, halves))
        made = staged(body, name, [], ins, outs, cost(size, 6 * size), deps=deps)
        sends = made[: len(parts)]
        vectors = made[-1] if len(made) > len(parts) else None
    for p, h in zip(parts, halves):
        p.rows = h
    return sends, vectors


def pack(me, parts, columns, count, name, vectors=None, deps=()):
    rows = min(p.rows for p in parts)
    widths = [c[2] // count for c in columns]
    ahead = 0 if vectors is None else 16 * vectors.shape[1] // rows
    wide = ahead + sum(parts[c[0]].rows // rows * w for c, w in zip(columns, widths))
    ins, counts = [], []
    for p in parts:
        ins += p.inputs(0)
        counts.append(len(p.terms))
    outs = [shaped((2 * rows, wide)), shaped((2 * rows, wide), F32)]
    if vectors is not None:
        sent = parts[0].terms[-1]
        ins += [vectors, (sent, slice(parts[0].rows, parts[0].rows + 16), slice(0, parts[0].cols))]
        outs.append(shaped(vectors.shape, F32))

    def body(scalars, get, out, put, scratch):
        (me_ref,) = scalars
        sums, at = [], 0
        for n in counts:
            sums.append(add_up([get(at + j) for j in range(n)]))
            at += n
        if vectors is not None:
            vec = get(len(ins) - 2)[...] + joined(get(len(ins) - 1)[...])
            out[2][...] = vec
            put(2)
            store_vectors(out[0], vec, rows, ahead)
        for place, (ref, turn) in enumerate([(out[0], 0), (out[0], 1), (out[1], 0), (out[1], 1)]):
            distance = (1, 3, 0, 2)[place]
            for owner in range(count):

                @pl.when((me_ref[0] ^ distance) == owner)
                def _(ref=ref, owner=owner, turn=turn):
                    at = ahead
                    for (which, start, _), w in zip(columns, widths):
                        piece = sums[which][:, start + owner * w : start + (owner + 1) * w].astype(ref.dtype)
                        for j in range(piece.shape[0] // rows):
                            ref[turn * rows : (turn + 1) * rows, at : at + w] = piece[j * rows : (j + 1) * rows]
                            at += w

            if turn == 1:
                put(place // 2)

    size = sum(p.rows * p.cols for p in parts)
    long = pl.CostEstimate(flops=10**11, transcendentals=0, bytes_accessed=10**8)
    estimate = cost(2 * size, 6 * size) if vectors is not None else long
    return staged(body, name, [me], ins, outs, estimate, deps=deps)


def store_vectors(ref, vec, rows, ahead):
    both = split_high(vec)
    for i in range(rows // 16):
        ref[16 * i : 16 * (i + 1), :ahead] = both[:, i * ahead : (i + 1) * ahead]


def load_vectors(ref, rows, ahead):
    return joined(jnp.concatenate([ref[16 * i : 16 * (i + 1), :ahead] for i in range(rows // 16)], 1))


def pack_far(own, recv, name, vectors=None, deps=()):
    rows, wide = own.shape[0] // 2, own.shape[1]
    ahead = 0 if vectors is None else 16 * vectors.shape[1] // rows
    far = slice(rows, 2 * rows)
    ins = [(own, far, slice(0, wide)), (recv, far, slice(0, wide))]
    outs = [shaped((rows, wide))]
    if vectors is not None:
        ins += [vectors, (recv, slice(0, rows), slice(0, ahead))]
        outs.append(shaped(vectors.shape, F32))

    def body(scalars, get, out, put, scratch):
        out[0][:, ahead:] = (get(0)[:, ahead:] + get(1)[:, ahead:].astype(F32)).astype(BF)
        if vectors is not None:
            vec = get(2)[...] + load_vectors(get(3), rows, ahead)
            out[1][...] = vec
            store_vectors(out[0], vec, rows, ahead)

    size = rows * wide
    return staged(body, name, [], ins, outs, cost(size, 10 * size), deps=deps)


def unpack(own, near, far, shapes, name, vectors=None, deps=(), tall=None, through=None):
    rows, wide = far.shape
    this, all_cols = slice(0, rows), slice(0, wide)
    ins = [(own, this, all_cols), (near, this, all_cols), far]
    outs = [shaped(shape[::-1] if i == tall else shape, F32) for i, shape in enumerate(shapes)]
    ahead = 0
    if through is not None:
        ins.append(through)
        outs.append(shaped(through.shape, F32))
    if vectors is not None:
        ahead = 16 * vectors.shape[1] // rows
        width = vectors.shape[1] // 3
        ins.append(vectors)
        outs += [shaped((width,), F32)] * 8 + [shaped((4 * width,), F32)]

    def body(scalars, get, out, put, scratch):
        total = get(0)[:, ahead:] + get(1)[:, ahead:].astype(F32) + get(2)[:, ahead:].astype(F32)
        at = 0
        for i, (height, width) in enumerate(shapes):
            if i == tall:
                turns = range(height // rows)
                whole = jnp.concatenate([total[:, at + j * width : at + (j + 1) * width] for j in turns], 0)
                out[i][...] = whole.T
                at += len(turns) * width
            else:
                for j in range(height // rows):
                    out[i][j * rows : (j + 1) * rows, :] = total[:, at : at + width]
                    at += width
            put(i)
        if through is not None:
            out[len(shapes)][...] = get(3)[...].astype(F32)
        if vectors is not None:
            vec = get(3)[...] + load_vectors(get(2), rows, ahead)
            wide = vec.shape[1] // 3
            base = len(shapes)
            for i in range(2):
                for j in range(4):
                    out[base + 4 * i + j][...] = vec[j : j + 1, i * wide : (i + 1) * wide].reshape(wide)
            for j in range(4):
                out[base + 8][j * wide : (j + 1) * wide] = vec[j : j + 1, 2 * wide :].reshape(wide)

    size = rows * wide
    return staged(body, name, [], ins, outs, cost(size, 12 * size), deps=deps)


def spec_sum(part, me, count):
    cols = part.shape[1] // count

    def mine(distance):
        return lax.dynamic_slice_in_dim(part, (me ^ distance) * cols, cols, 1)

    got = [lax.ppermute(mine(d).astype(BF), "spec", flip(count, d)) for d in range(1, count)]
    total = mine(0)
    for piece in got:
        total = total + piece.astype(F32)
    return total


def local(
    tokens,
    cotangent,
    lengths,
    projection,
    query_bias,
    value_bias,
    output_weight,
    output_bias,
    up_weight,
    up_bias,
    down_weight,
    down_bias,
    first_gain,
    first_shift,
    second_gain,
    second_shift,
):
    _, rows, width = tokens.shape
    hidden = up_weight.shape[1]
    cubes, count = lax.axis_size("cube"), lax.axis_size("spec")
    cube, spec = lax.axis_index("cube"), lax.axis_index("spec")
    tok = tokens.reshape(rows, width)
    cot = cotangent.reshape(rows, width)

    assert count == 4
    half_way = count // 2

    def partner(c, s):
        return (c ^ 1, s ^ half_way) if (c & 1) != (s // half_way) else (c, s)

    places = [(c, s) for c in range(cubes) for s in range(count)]

    def both_axes(move):
        return [(c * count + s, move(c, s)[0] * count + move(c, s)[1]) for c, s in places]

    exchange = both_axes(partner)
    pair = flip(cubes, 1)
    near = flip(count, 1)
    axes = ("cube", "spec")

    own_tok = tok
    tok = lax.ppermute(own_tok, axes, exchange)
    away = (cube & 1) != (spec // half_way)
    length = jnp.where(away, lax.ppermute(lengths, "cube", pair), lengths)[0].astype(jnp.int32)
    my_block = jnp.where(away, spec ^ half_way, spec).astype(jnp.int32)
    next_tok = lax.ppermute(tok, "spec", near)
    blocks = [tok, lax.ppermute(tok, "cube", pair), next_tok, lax.ppermute(next_tok, "cube", pair)]
    distances = [0, half_way, 1, half_way + 1]
    ids = jnp.stack([cube.astype(jnp.int32), my_block, length])

    bits = cubes.bit_length() - 1
    order_a = list(range(bits))
    order_b = [0] + list(range(bits - 1, 0, -1))
    place_a, place_b = tree_place(order_a), tree_place(order_b)
    split = cubes // 2

    def source_rows(place, offset, size, block):
        start = (jnp.asarray(place, jnp.int32) ^ cube) * block + offset
        return (start[:, None] + jnp.arange(size, dtype=jnp.int32)[None, :]).reshape(-1)

    def one_hot(source):
        return (source[:, None] == jnp.arange(width, dtype=jnp.int32)[None, :]).astype(BF)

    block = width // cubes
    part = block // 2
    chunks = 8
    lists = [list(map(int, place)) for place in (place_a, place_b)]
    perm_b = (lists[1], [0] * cubes, block, block)
    perm_mixed = (
        lists[0][:split] + lists[1][:split] + lists[0][split:] + lists[1][split:],
        ([0] * split + [part] * split) * 2,
        part,
        block,
    )
    if part % 16:
        perm_b, perm_mixed = (
            one_hot(jnp.concatenate([source_rows([r], f, size, block) for r, f in zip(relative, first)]))
            for relative, first, size, _ in (perm_b, perm_mixed)
        )
    places = lists[0] if cubes == chunks else None

    up_bias_row = up_bias.reshape(chunks, -1)
    hiddens, keys, values = [], [], []
    state = None
    for which in ((0, 1), (2,), (3,)):
        made = forward_step(
            which[-1] == count - 1,
            ids,
            [distances[i] for i in which],
            [blocks[i] for i in which],
            first_gain,
            first_shift,
            projection,
            query_bias,
            value_bias,
            state,
            cot,
            (up_bias_row,) if state is None else (),
        )
        for i in range(len(which)):
            hiddens.append(made[3 + 3 * i])
            keys.append(made[4 + 3 * i])
            values.append(made[5 + 3 * i])
        if state is None:
            q, qt, cot = made[3 + 3 * len(which) :]
            cot = lax.ppermute(cot, axes, exchange)
        state = (qt,) + tuple(made[:3])
    negl, attt = state[1], state[3]

    (
        block_out,
        down_keep,
        down_send,
        up_keep,
        up_send,
        da,
        dat,
        negd,
        gmid,
        vec_mid,
        grad_up_bias,
    ) = middle_step(
        ids,
        places,
        tok,
        cot,
        attt,
        output_weight,
        output_bias,
        second_gain,
        second_shift,
        up_weight,
        up_bias_row,
        down_weight,
        down_bias,
        perm_b,
    )
    if cubes != chunks:
        whole = jnp.concatenate([down_keep, down_send], 0).reshape(cubes, hidden // cubes, width)
        whole = jnp.take(whole, jnp.asarray(place_a, jnp.int32) ^ cube, axis=0)
        down_keep = whole[:split].reshape(hidden // 2, width)
        down_send = whole[split:].reshape(hidden // 2, width)

    down_recv = lax.ppermute(down_send, "cube", pair)
    up_recv = lax.ppermute(up_send, "cube", pair)

    common = (q, qt, da, dat, negl, negd)

    def back(which, state, last, deps, arrived=None, through=None):
        def pick(things):
            return [things[i] for i in which]

        some = (pick(keys), pick(values), pick(blocks))
        return backward_step(
            ids, pick(distances), *common, *some, projection, state, last, deps, arrived, through
        )

    dkv_3, g_3, vec_back, dqt, block_out = back((3,), None, False, (), None, block_out)
    block_out = lax.ppermute(block_out, axes, exchange)
    g_3 = lax.ppermute(g_3, "cube", pair)

    def hop(parts, sends, level):
        for p, send, order in zip(parts, sends, (order_a, order_b)):
            p.terms.append(lax.ppermute(send, "cube", flip(cubes, 1 << order[level])))

    levels = len(order_a)
    me = spec.astype(jnp.int32).reshape(1)
    ff = [Part(down_keep, down_recv), Part(up_keep, up_recv)]
    last = dqt
    if levels > 1:
        sends, _ = halve(ff, "sum_ff", None, (last, g_3))
        last = sends[0]
        hop(ff, sends, 1)
    dkv_2, g_2, dkv_1, g_1, dkv_0, g_0, vec_back, dq = back((2, 1, 0), (dqt, vec_back), True, (last,), g_3)
    g_2 = lax.ppermute(g_2, "spec", near)
    g_1 = lax.ppermute(g_1, "cube", pair)
    last = dq
    for level in range(2, levels):
        sends, _ = halve(ff, "sum_ff", None, (last, block_out))
        last = sends[0]
        hop(ff, sends, level)

    proj_a, proj_b, send_a, send_b, vectors = projection_step(
        ids, perm_mixed, dq, hiddens, [dkv_0, dkv_1, dkv_2, dkv_3], vec_mid, grad_up_bias, vec_back, (g_1, last)
    )
    proj = [
        Part(proj_a, lax.ppermute(send_a, "cube", pair)),
        Part(proj_b, lax.ppermute(send_b, "cube", pair)),
    ]
    aligned = width // cubes % 32 == 0
    far = flip(count, 2)
    last = vectors
    if aligned:
        columns = [(1, 0, hidden), (1, hidden, width), (0, 0, width)]
        ff_send, ff_own = pack(me, ff, columns, count, "pack_ff", None, (last,))
        last = ff_own
        ff_near = lax.ppermute(ff_send, "spec", near)
    for level in range(1, levels):
        sends, vectors = halve(proj, "sum_proj", vectors, (last, ff_near) if level == 2 and aligned else (last,))
        last = sends[0]
        hop(proj, sends, level)
        if level == 1:
            grad_tokens, block_out = final_step(tok, first_gain, gmid, g_0, [g_1, g_2], block_out, (last,))
            last = grad_tokens
            grad_tokens = lax.ppermute(grad_tokens, axes, exchange)
    if aligned:
        pr_send, pr_own, vectors = pack(
            me, proj, [(0, 0, 3 * width), (1, 0, 3 * width)], count, "pack_proj", vectors, (last, grad_tokens)
        )
        pr_near = lax.ppermute(pr_send, "spec", near)
        (ff_send,) = pack_far(ff_own, ff_near, "pack_ff_far", None, (pr_own,))
        ff_far = lax.ppermute(ff_send, "spec", far)
        pr_send, vectors = pack_far(pr_own, pr_near, "pack_proj_far", vectors, (ff_send,))
        pr_far = lax.ppermute(pr_send, "spec", far)
        grad_up, grad_out, grad_down, grad_tokens = unpack(
            ff_own,
            ff_near,
            ff_far,
            [(width // cubes, hidden // count), (width // cubes, width // count), (hidden // cubes, width // count)],
            "unpack_ff",
            None,
            (pr_send,),
            2,
            grad_tokens,
        )
        grad_down = grad_down.T
        shapes = [(width // cubes, 3 * width // count)]
        grad_proj, *vectors = unpack(pr_own, pr_near, pr_far, shapes, "unpack_proj", vectors, (grad_out,))
    else:
        grad_tokens = grad_tokens.astype(F32)
        vectors = vectors + joined(proj[0].terms[-1][-16:])
        vectors = sum([lax.ppermute(vectors, "spec", flip(count, d)) for d in range(1, count)], vectors)
        grad_up_out = ff[1].total()
        grad_up = spec_sum(grad_up_out[:, :hidden], spec, count)
        grad_out = spec_sum(grad_up_out[:, hidden:], spec, count)
        grad_down = spec_sum(ff[0].total(), spec, count)
        grad_proj = spec_sum(jnp.concatenate([p.total() for p in proj], 0), spec, count)
        vectors = [vectors[j, i * width : (i + 1) * width] for i in range(2) for j in range(4)] + [
            vectors[:4, 2 * width :].reshape(-1)
        ]

    return (
        block_out.reshape(tokens.shape),
        grad_tokens.reshape(tokens.shape),
        grad_proj,
        vectors[4],
        vectors[5],
        grad_out,
        vectors[3],
        grad_up,
        vectors[8],
        grad_down,
        vectors[0],
        vectors[6],
        vectors[7],
        vectors[1],
        vectors[2],
    )


def solution(mesh):
    return jax.shard_map(
        local,
        mesh=mesh,
        in_specs=(
            P("cube", "spec", None),
            P("cube", "spec", None),
            P("cube"),
        )
        + (P(),) * 13,
        out_specs=(
            P("cube", "spec", None),
            P("cube", "spec", None),
            P("cube", "spec"),
            P(),
            P(),
            P("cube", "spec"),
            P(),
            P("cube", "spec"),
            P(),
            P("cube", "spec"),
            P(),
            P(),
            P(),
            P(),
            P(),
        ),
        check_vma=False,
    )
```

```python
import math
from functools import partial

import jax
import jax.numpy as jnp
import numpy as np
from jax import lax
from jax.experimental import pallas as pl
from jax.experimental.pallas import tpu as pltpu
from jax.sharding import PartitionSpec as P

HEADS = 12
HD = 64
PAIRS = HEADS // 2
EPS = 1e-06
SCALE = HD ** (-0.5)
TO_EXP2 = SCALE * math.log2(math.e)
MASKED = -1e30

BF = jnp.bfloat16
F32 = jnp.float32


def dot(left, right):
    return jnp.dot(left, right, preferred_element_type=F32)


def dot_nt(left, right):
    return lax.dot_general(left, right, (((1,), (1,)), ((), ())), preferred_element_type=F32)


def dot_tn(left, right):
    return lax.dot_general(left, right, (((0,), (0,)), ((), ())), preferred_element_type=F32)


def normalize(values):
    average = jnp.mean(values, -1, keepdims=True)
    centred = values - average
    inverse = lax.rsqrt(jnp.mean(centred * centred, -1, keepdims=True) + EPS)
    return centred * inverse, inverse


def params(megabytes=64):
    return pltpu.CompilerParams(vmem_limit_bytes=megabytes * 2**20)


def cost(flops, nbytes, trans=0):
    return pl.CostEstimate(flops=flops // 1000, bytes_accessed=nbytes // 1000, transcendentals=trans // 1000)


def extra_lanes(ids_ref, distance, rows, ones):
    slot = lax.broadcasted_iota(jnp.int32, (rows, 128), 0) + (ids_ref[1] ^ distance) * rows
    lane = lax.broadcasted_iota(jnp.int32, (rows, 128), 1)
    masked = jnp.where(slot < ids_ref[2], 0.0, MASKED)
    rest = jnp.where(lane <= ones, 1.0, 0.0)
    return jnp.where(lane == 0, masked, rest).astype(BF)


def two_heads(part, extra):
    n = part.shape[1]
    zero = jnp.zeros((HD, n), part.dtype)
    left = jnp.concatenate([part[:HD], zero], 0)
    right = jnp.concatenate([zero, part[HD:]], 0)
    return jnp.concatenate([jnp.concatenate([left, right], 1), extra], 0)


def as_row(ref):
    return ref[...].reshape(1, -1)


def pair_lanes(pair):
    return slice(pair * 2 * HD, (pair + 1) * 2 * HD)


ANY = pl.BlockSpec(memory_space=pl.ANY)
SMEM = pl.BlockSpec(memory_space=pltpu.SMEM)


def staged(body, name, scalars, ins, outs, estimate, scratch=(), deps=()):
    parts = [x if isinstance(x, tuple) else (x, slice(0, x.shape[0]), slice(0, x.shape[-1])) for x in ins]
    shapes = []
    for x, rows, cols in parts:
        shapes.append((rows.stop - rows.start,) if x.ndim == 1 else (rows.stop - rows.start, cols.stop - cols.start))
    arrays = []
    for x, _, _ in parts:
        if not any(x is y for y in arrays):
            arrays.append(x)
    index = [[i for i, y in enumerate(arrays) if y is x][0] for x, _, _ in parts]
    n_s, n_a, n_i, n_o, n_x = len(scalars), len(arrays), len(ins), len(outs), len(scratch)

    def kernel(*refs):
        at = 0
        groups = []
        for n in (n_s, n_a, len(deps), n_o, n_x, n_i, n_o):
            groups.append(refs[at : at + n])
            at += n
        s_refs, a_ref, _, o_to, x_refs, i_ref, o_ref = groups
        i_sem, o_sem = refs[at:]
        loads = []
        for i, (x, rows, cols) in enumerate(parts):
            source = a_ref[index[i]]
            if shapes[i] != x.shape:
                source = source.at[rows, cols]
            loads.append(pltpu.make_async_copy(source, i_ref[i], i_sem.at[i]))
        stores = [pltpu.make_async_copy(o_ref[i], o_to[i], o_sem.at[i]) for i in range(n_o)]
        for load in loads:
            load.start()
        waited = set()
        sent = set()

        def get(i):
            if i not in waited:
                waited.add(i)
                loads[i].wait()
            return i_ref[i]

        def put(i, *where):
            sent.add(i)
            if where:
                pltpu.make_async_copy(o_ref[i].at[where], o_to[i].at[where], o_sem.at[i]).start()
            else:
                stores[i].start()

        body(s_refs, get, o_ref, put, x_refs)
        for i in range(n_i):
            get(i)
        for i in range(n_o):
            if i not in sent:
                put(i)
        for store in stores:
            store.wait()

    return pl.pallas_call(
        kernel,
        out_shape=list(outs),
        in_specs=[SMEM] * n_s + [ANY] * (n_a + len(deps)),
        out_specs=[ANY] * n_o,
        scratch_shapes=list(scratch)
        + [pltpu.VMEM(shape, x.dtype) for shape, (x, _, _) in zip(shapes, parts)]
        + [pltpu.VMEM(x.shape, x.dtype) for x in outs]
        + [pltpu.SemaphoreType.DMA((n_i,)), pltpu.SemaphoreType.DMA((n_o,))],
        compiler_params=params(),
        cost_estimate=estimate,
        name=name,
    )(*scalars, *arrays, *deps)


def shaped(shape, dtype=BF):
    return jax.ShapeDtypeStruct(shape, dtype)


def forward_step(last, ids, distances, toks, gain, shift, w, qb, vb, state, through, deps=()):
    first = state is None
    count = len(toks)
    rows, width = toks[0].shape
    block = shaped((rows, width))
    outs = [shaped((8, 2 * rows), F32), shaped((8, 2 * rows), F32), shaped((width, rows), F32)]
    outs += [block, block, block] * count
    full = slice(0, width)
    ins = [toks[0], gain, shift, vb, (w, full, slice(width, 2 * width)), (w, full, slice(2 * width, 3 * width))]
    if first:
        ins += [(w, full, full), qb]
        outs += [block, shaped((width, rows)), block]
    else:
        ins += list(state)
    at_tok = len(ins) - 1
    ins += toks[1:]
    if first:
        ins.append(through)

    def body(scalars, get, out, put, scratch):
        m_out, l_out, acc_out = out[:3]
        ones_row = (lax.broadcasted_iota(jnp.int32, (128, 2 * rows), 0) == 0).astype(BF)
        for i in range(count):
            h_out, k_out, v_out = out[3 + 3 * i : 6 + 3 * i]
            normed, _ = normalize(get(at_tok + i if i > 0 else 0)[...].astype(F32))
            hidden = (normed * as_row(get(1)) + as_row(get(2))).astype(BF)
            h_out[...] = hidden
            put(3 + 3 * i)
            k_out[...] = dot(hidden, get(4)[...]).astype(BF)
            put(4 + 3 * i)
            values = dot(hidden, get(5)[...]) + as_row(get(3))
            v_out[...] = values.astype(BF)
            put(5 + 3 * i)
            values_t = v_out[...].astype(F32).T.astype(BF)
            if first:
                at = 3 + 3 * count
                q_out, qt_out, through_out = out[at:]
                if i == 0:
                    q_out[...] = (dot(hidden, get(6)[...]) + as_row(get(7))).astype(BF)
                    put(at)
                    qt_out[...] = q_out[...].astype(F32).T.astype(BF)
                    put(at + 1)
                if i == count - 1:
                    through_out[...] = get(len(ins) - 1)[...]
                    put(at + 2)
                qt_ref = qt_out
            else:
                qt_ref = get(6)
            extra_keys = extra_lanes(scalars[0], distances[i], rows, 0)
            start = first and i == 0
            end = last and i == count - 1
            for pair in range(PAIRS):
                lanes = pair_lanes(pair)
                this = slice(pair, pair + 1)
                keys = jnp.concatenate([k_out[:, lanes], extra_keys], 1)
                scores = dot(keys, two_heads(qt_ref[lanes, :], ones_row))
                top = jnp.max(scores, 0, keepdims=True)
                if not start:
                    m_ref, l_ref, acc_ref = (get(7 + j) for j in range(3)) if i == 0 else (m_out, l_out, acc_out)
                    before = m_ref[this, :]
                    top = jnp.maximum(top, before)
                    fade = jnp.exp2((before - top) * TO_EXP2)
                weights = jnp.exp2((scores - top) * TO_EXP2)
                total = jnp.sum(weights, 0, keepdims=True)
                if not start:
                    total = total + l_ref[this, :] * fade
                both = dot(values_t[lanes, :], weights.astype(BF))
                for head in range(2):
                    own = slice(lanes.start + head * HD, lanes.start + (head + 1) * HD)
                    cols = slice(head * rows, (head + 1) * rows)
                    part = both[head * HD : (head + 1) * HD, cols]
                    if not start:
                        part = part + acc_ref[own, :] * fade[:, cols]
                    if end:
                        part = part / total[:, cols]
                    acc_out[own, :] = part
                m_out[this, :] = -(top + jnp.log2(total) * (1.0 / TO_EXP2)) if end else top
                l_out[this, :] = total
                if i == count - 1:
                    put(2, lanes)

    estimate = pl.CostEstimate(flops=count * 10**10, bytes_accessed=24 * 2**20, transcendentals=0)
    return staged(body, "attend", [ids], ins, outs, estimate, deps=deps)


def make_perm(ref, me, blocks, firsts, size, block):
    here = lax.broadcasted_iota(jnp.int32, (size, ref.shape[1]), 0)
    there = lax.broadcasted_iota(jnp.int32, (size, ref.shape[1]), 1)
    for i, (relative, first) in enumerate(zip(blocks, firsts)):
        start = (me ^ relative) * block + first
        ref[i * size : (i + 1) * size, :] = (here + start == there).astype(F32).astype(BF)


def middle_step(ids, places, tok, cot, attt, wo, ob, gain, shift, up, ub, down, db, perm):
    rows, width = tok.shape
    hidden = up.shape[1]
    chunks = 8
    chunk = hidden // chunks
    half = width // 2
    given = not isinstance(perm, tuple)
    ins = [attt, wo, ob, tok, gain, shift, up, ub, cot, down, db] + ([perm] if given else [])
    outs = [
        shaped((rows, width)),
        shaped((hidden // 2, width)),
        shaped((hidden // 2, width)),
        shaped((half, hidden + width)),
        shaped((half, hidden + width)),
        shaped((rows, width)),
        shaped((width, rows)),
        shaped((8, 2 * rows), F32),
        shaped((rows, width), F32),
        shaped((8, width), F32),
        shaped((8, chunk), F32),
    ]
    scratch = [
        pltpu.VMEM((rows, width), F32),
        pltpu.VMEM((rows, width), F32),
        pltpu.VMEM((rows, width), BF),
        pltpu.VMEM((width, rows), BF),
        pltpu.VMEM((rows, width), BF),
        pltpu.VMEM((rows, width), F32),
        pltpu.VMEM((rows, width), F32),
        pltpu.VMEM((width, width), BF),
    ]

    def body(scalars, get, out, put, scratch):
        (ids_ref,) = scalars
        block_out, down_keep, down_send, up_keep, up_send, da_out, dat_out, negd_out, gmid_out, vec_out, ubg_out = out
        mid_ref, norm_ref, h2_ref, h2t_ref, att_ref, res_ref, gh_ref, perm_ref = scratch
        if given:
            perm_ref[...] = get(11)[...]
        else:
            make_perm(perm_ref, ids_ref[0], *perm)
        attt_ref = get(0)
        att_ref[...] = attt_ref[...].T.astype(BF)
        projected = dot(att_ref[...], get(1)[...]) + as_row(get(2))
        middle = get(3)[...].astype(F32) + projected
        mid_ref[...] = middle
        normed, inverse = normalize(middle)
        norm_ref[...] = normed
        h2_ref[...] = (normed * as_row(get(4)) + as_row(get(5))).astype(BF)
        h2t_ref[...] = dot_nt(perm_ref[...], h2_ref[...]).astype(BF)
        up_ref, ub_ref, cot_ref, down_ref = get(6), get(7), get(8), get(9)
        for turn in range(chunks // 2):
            p = (2 * turn + chunks // 2) % chunks
            own = [p, p + 1] if places is None else [places[p] ^ ids_ref[0], places[p + 1] ^ ids_ref[0]]
            at = [pl.ds(pl.multiple_of(place * chunk, 128), chunk) for place in own]
            up_c = jnp.concatenate([up_ref[:, a] for a in at], 1)
            down_c = jnp.concatenate([down_ref[a, :] for a in at], 0)
            bias = jnp.concatenate([ub_ref[pl.ds(place, 1), :] for place in own], 1)
            before = dot(h2_ref[...], up_c) + bias
            cdf = 0.5 * (1.0 + lax.erf(before * math.sqrt(0.5)))
            slope = cdf + before * (jnp.exp(-0.5 * before * before) * (1.0 / math.sqrt(2.0 * math.pi)))
            lifted = (before * cdf).astype(BF)
            grad_lifted = dot_nt(cot_ref[...], down_c)
            grad_down = dot_tn(lifted, cot_ref[...]).astype(BF)
            to, first = (down_keep, p) if p < chunks // 2 else (down_send, p - chunks // 2)
            rows_to = pl.ds(first * chunk, 2 * chunk)
            to[rows_to, :] = grad_down
            put(1 if p < chunks // 2 else 2, rows_to)
            grad_before = (grad_lifted * slope).astype(BF)
            bias_grad = jnp.sum(grad_before.astype(F32), 0, keepdims=True)
            for i, place in enumerate(own):
                ubg_out[pl.ds(place, 1), :] = bias_grad[:, i * chunk : (i + 1) * chunk]
            grad_up = dot(h2t_ref[...], grad_before).astype(BF)
            for i, a in enumerate(at):
                cols = slice(i * chunk, (i + 1) * chunk)
                up_keep[:, a] = grad_up[:half, cols]
                up_send[:, a] = grad_up[half:, cols]
                put(3, slice(None), a)
                put(4, slice(None), a)
            part = dot(lifted, down_c)
            back = dot_nt(grad_before, up_c)
            if turn == 0:
                res_ref[...] = part
                gh_ref[...] = back
            else:
                res_ref[...] += part
                gh_ref[...] += back
        block_out[...] = (mid_ref[...] + (res_ref[...] + as_row(get(10)))).astype(BF)
        put(0)
        cot32 = cot_ref[...].astype(F32)
        grad = gh_ref[...]
        normed = norm_ref[...]
        vec_out[0:1, :] = jnp.sum(cot32, 0, keepdims=True)
        vec_out[1:2, :] = jnp.sum(grad * normed, 0, keepdims=True)
        vec_out[2:3, :] = jnp.sum(grad, 0, keepdims=True)
        scaled = grad * as_row(get(4))
        grad_middle = cot32 + inverse * (
            scaled
            - jnp.mean(scaled, -1, keepdims=True)
            - normed * jnp.mean(scaled * normed, -1, keepdims=True)
        )
        gmid_out[...] = grad_middle
        put(8)
        branch = grad_middle.astype(BF)
        vec_out[3:4, :] = jnp.sum(branch.astype(F32), 0, keepdims=True)
        vec_out[4:8, :] = jnp.zeros((4, width), F32)
        att_t = dot_nt(perm_ref[...], att_ref[...]).astype(BF)
        grad_out = dot(att_t, branch).astype(BF)
        cols = pl.ds(hidden, width)
        up_keep[:, cols] = grad_out[:half]
        up_send[:, cols] = grad_out[half:]
        put(3, slice(None), cols)
        put(4, slice(None), cols)
        grad_att = dot_nt(branch, get(1)[...]).astype(BF)
        da_out[...] = grad_att
        put(5)
        grad_att_t = grad_att.astype(F32).T
        dat_out[...] = grad_att_t.astype(BF)
        put(6)
        product = grad_att_t * attt_ref[...]
        for head in range(HEADS):
            spread = jnp.sum(product[head * HD : (head + 1) * HD], 0, keepdims=True)
            place = slice((head % 2) * rows, (head % 2 + 1) * rows)
            negd_out[head // 2 : head // 2 + 1, place] = -spread

    estimate = cost(12 * rows * width * hidden + 6 * rows * width * width, 30 * 2**20, 0)
    return staged(body, "middle", [ids], ins, outs, estimate, scratch)


def three_parts(row):
    high = row.astype(BF)
    rest = row - high.astype(F32)
    mid = rest.astype(BF)
    low = (rest - mid.astype(F32)).astype(BF)
    return high.astype(F32), mid.astype(F32), low.astype(F32)


def extra_rows(row, with_mask):
    n = row.shape[1]
    high, mid, low = three_parts(row)
    place = lax.broadcasted_iota(jnp.int32, (128, n), 0)
    out = jnp.where(place == 0, 1.0 if with_mask else 0.0, 0.0)
    out = jnp.where(place == 1, high, out)
    out = jnp.where(place == 2, mid, out)
    out = jnp.where(place == 3, low, out)
    return out.astype(BF)


def backward_step(ids, distances, q, qt, da, dat, negl, negd, keys, values, toks, w, state, last, deps, arrived=None, through=None):
    rows, width = q.shape
    blocks = len(keys)
    first = state is None
    ins = [qt, negl, dat, negd, q, da]
    for k, v in zip(keys, values):
        ins += [k, v]
    base_w = len(ins)
    ins += [w, *toks]
    base_state = len(ins)
    if not first:
        ins += list(state)
    at_extra = len(ins)
    ins += [x for x in (arrived, through) if x is not None]
    outs = []
    for i in range(blocks):
        outs += [shaped((rows, 2 * width)), shaped((rows, width), F32 if last and i == blocks - 1 else BF)]
    outs += [shaped((8, width), F32), shaped((rows, width)) if last else shaped((width, rows), F32)]
    if through is not None:
        outs.append(shaped(through.shape, through.dtype))

    def body(scalars, get, out, put, scratch):
        (dqt,) = scratch
        vec_out, end_out = out[2 * blocks : 2 * blocks + 2]
        lane = lax.broadcasted_iota(jnp.int32, (rows, 128), 1)
        zero = jnp.zeros((rows, 128), BF)
        value_bias = gain = shift = jnp.zeros((1, width), F32)
        query_bias = jnp.zeros((1, width), F32)
        for i in range(blocks):
            dkv_out, g_out = out[2 * i], out[2 * i + 1]
            extra_keys = extra_lanes(scalars[0], distances[i], rows, 3)
            qt_ref, negl_ref, dat_ref, negd_ref = get(0), get(1), get(2), get(3)
            k_ref, v_ref = get(6 + 2 * i), get(7 + 2 * i)
            keys_t = k_ref[...].astype(F32).T.astype(BF)
            for pair in range(PAIRS):
                lanes = pair_lanes(pair)
                key = jnp.concatenate([k_ref[:, lanes], extra_keys], 1)
                scores = dot(key, two_heads(qt_ref[lanes, :], extra_rows(negl_ref[pair : pair + 1, :], True)))
                softmaxed = jnp.exp2(scores * TO_EXP2)
                value = jnp.concatenate([v_ref[:, lanes], extra_keys], 1)
                centred = dot(value, two_heads(dat_ref[lanes, :], extra_rows(negd_ref[pair : pair + 1, :], False)))
                grad_scores = (softmaxed * centred).astype(BF)
                weights = softmaxed.astype(BF)
                q_pair = get(4)[:, lanes]
                da_pair = get(5)[:, lanes]
                q_both = jnp.concatenate([jnp.where(lane < HD, q_pair, zero), jnp.where(lane < HD, zero, q_pair)], 0)
                da_both = jnp.concatenate([jnp.where(lane < HD, da_pair, zero), jnp.where(lane < HD, zero, da_pair)], 0)
                dkv_out[:, lanes] = (dot(grad_scores, q_both) * SCALE).astype(BF)
                dkv_out[:, slice(width + lanes.start, width + lanes.stop)] = dot(weights, da_both).astype(BF)
                both = dot(keys_t[lanes, :], grad_scores)
                for head in range(2):
                    own = slice(lanes.start + head * HD, lanes.start + (head + 1) * HD)
                    part = both[head * HD : (head + 1) * HD, head * rows : (head + 1) * rows]
                    if i > 0:
                        part = part + dqt[own, :]
                    elif not first:
                        part = part + get(base_state)[own, :]
                    dqt[own, :] = part
            put(2 * i)
            w_ref = get(base_w)
            grad = dot_nt(dkv_out[...], w_ref[:, width:])
            if last and i == blocks - 1:
                dq = (dqt[...].T * SCALE).astype(BF)
                end_out[...] = dq
                put(2 * blocks + 1)
                query_bias = jnp.sum(dq.astype(F32), 0, keepdims=True)
                grad = grad + dot_nt(dq, w_ref[:, :width])
            if arrived is not None and i == 0:
                g_out[...] = (grad + get(at_extra)[...].astype(F32)).astype(g_out.dtype)
            else:
                g_out[...] = grad.astype(g_out.dtype)
            put(2 * i + 1)
            normed, _ = normalize(get(base_w + 1 + i)[...].astype(F32))
            value_bias = value_bias + jnp.sum(dkv_out[:, width:].astype(F32), 0, keepdims=True)
            gain = gain + jnp.sum(grad * normed, 0, keepdims=True)
            shift = shift + jnp.sum(grad, 0, keepdims=True)
        if not last:
            end_out[...] = dqt[...]
        if through is not None:
            out[2 * blocks + 2][...] = get(len(ins) - 1)[...]
        if not first:
            vec_ref = get(base_state + 1)
            value_bias = value_bias + vec_ref[1:2, :]
            gain = gain + vec_ref[2:3, :]
            shift = shift + vec_ref[3:4, :]
        vec_out[0:1, :] = query_bias
        vec_out[1:2, :] = value_bias
        vec_out[2:3, :] = gain
        vec_out[3:4, :] = shift
        vec_out[4:8, :] = jnp.zeros((4, width), F32)

    flops = blocks * (2 * rows * width * width * 3 + 10 * rows * rows * width * 4)
    estimate = cost(flops, 20 * 2**20, blocks * HEADS * rows * rows)
    return staged(
        body, "attend_back", [ids], ins, outs, estimate, [pltpu.VMEM((width, rows), F32)], deps
    )


def projection_step(ids, perm, dq, hiddens, dkvs, vec_mid, vec_up, vec_back, deps):
    rows, width = dq.shape
    count = len(hiddens)
    part = width // 4
    given = not isinstance(perm, tuple)
    ins = [*hiddens, dq, vec_mid, vec_up, vec_back, *dkvs] + ([perm] if given else [])
    outs = [shaped((n, 3 * width)) for n in (part, part, part + 16, part)] + [shaped((8, 3 * width), F32)]
    at = count

    def body(scalars, get, out, put, scratch):
        ht_ref, perm_ref = scratch
        if given:
            perm_ref[...] = get(len(ins) - 1)[...]
        else:
            make_perm(perm_ref, scalars[0][0], *perm)
        keep_a, keep_b, send_a, send_b, vec_ref = out
        for i in range(count):
            ht_ref[:, i * rows : (i + 1) * rows] = dot_nt(perm_ref[...], get(i)[...]).astype(BF)
        vec_ref[0:4, :width] = get(at + 1)[0:4, :]
        vec_ref[0:4, width : 2 * width] = get(at + 3)[0:4, :]
        up = jnp.concatenate([get(at + 2)[i : i + 1, :] for i in range(get(at + 2).shape[0])], 1)
        for i in range(4):
            vec_ref[i : i + 1, 2 * width :] = up[:, i * width : (i + 1) * width]
        vec_ref[4:8, :] = jnp.zeros((4, 3 * width), F32)
        send_a[part:, :] = split_high(vec_ref[...])
        put(4)
        for third in range(3):
            if third == 0:
                grad = dot(ht_ref[:, :rows], get(at)[...])
            else:
                own = slice((third - 1) * width, third * width)
                grad = dot(ht_ref[...], jnp.concatenate([get(at + 4 + i)[:, own] for i in range(count)], 0))
            grad = grad.astype(BF)
            cols = pl.ds(third * width, width)
            send_a[:part, cols] = grad[2 * part : 3 * part]
            put(2, slice(None), cols)
            send_b[:, cols] = grad[3 * part :]
            put(3, slice(None), cols)
            keep_a[:, cols] = grad[:part]
            put(0, slice(None), cols)
            keep_b[:, cols] = grad[part : 2 * part]
            put(1, slice(None), cols)

    estimate = cost(2 * rows * width * width * (1 + 2 * count), 12 * 2**20, 0)
    return staged(
        body,
        "projection_grad",
        [ids],
        ins,
        outs,
        estimate,
        [pltpu.VMEM((width, count * rows), BF), pltpu.VMEM((width, width), BF)],
        deps,
    )


def final_step(tok, gain, gmid, g, pieces, block_out, deps=()):
    def body(scalars, get, out, put, scratch):
        normed, inverse = normalize(get(0)[...].astype(F32))
        total = get(3)[...]
        for i in range(len(pieces)):
            total = total + get(4 + i)[...].astype(F32)
        scaled = total * as_row(get(1))
        out[0][...] = (
            get(2)[...]
            + inverse
            * (
                scaled
                - jnp.mean(scaled, -1, keepdims=True)
                - normed * jnp.mean(scaled * normed, -1, keepdims=True)
            )
        ).astype(BF)
        put(0)
        out[1][...] = get(len(ins) - 1)[...]

    estimate = pl.CostEstimate(flops=10**11, transcendentals=0, bytes_accessed=10**8)
    ins = [tok, gain, gmid, g, *pieces, block_out]
    return staged(body, "norm_back", [], ins, [shaped(tok.shape)] * 2, estimate, deps=deps)


def flip(count, distance):
    return [(i, i ^ distance) for i in range(count)]


def tree_place(bits):
    n = len(bits)
    return np.array([sum(((p >> (n - 1 - i)) & 1) << bit for i, bit in enumerate(bits)) for p in range(1 << n)])


def split_high(values):
    high = values.astype(BF)
    return jnp.concatenate([high.astype(F32), values - high.astype(F32)], 0).astype(BF)


def joined(both):
    both = both.astype(F32)
    return both[:8] + both[8:]


class Part:
    def __init__(self, keep, recv):
        self.terms, self.rows, self.cols = [keep, recv], keep.shape[0], keep.shape[1]

    def inputs(self, start):
        return [(x, slice(start, self.rows), slice(0, self.cols)) for x in self.terms]

    def total(self):
        return sum(x[: self.rows].astype(F32) for x in self.terms)


def add_up(refs):
    total = refs[0][...].astype(F32)
    for ref in refs[1:]:
        total = total + ref[...].astype(F32)
    return total


def halve(parts, name, vectors=None, deps=(), through=None):
    halves = [p.rows // 2 for p in parts]
    if any(h % 16 for h in halves):
        sends = [p.total()[h:].astype(BF) for p, h in zip(parts, halves)]
        if vectors is not None:
            vectors = vectors + joined(parts[0].terms[-1][parts[0].rows :])
            sends[0] = jnp.concatenate([sends[0], split_high(vectors)], 0)
        vectors = through if vectors is None else vectors
    else:
        ins, counts = [], []
        for p, h in zip(parts, halves):
            ins += p.inputs(h)
            counts.append(len(p.terms))
        outs = [shaped((h, p.cols)) for p, h in zip(parts, halves)]
        if vectors is not None:
            sent, rows = parts[0].terms[-1], parts[0].rows
            ins += [vectors, (sent, slice(rows, rows + 16), slice(0, parts[0].cols))]
            outs[0] = shaped((halves[0] + 16, parts[0].cols))
            outs.append(shaped(vectors.shape, F32))
        if through is not None:
            ins.append(through)
            outs.append(shaped(through.shape, through.dtype))

        def body(scalars, get, out, put, scratch):
            at = 0
            for i, (n, h) in enumerate(zip(counts, halves)):
                out[i][:h, :] = add_up([get(at + j) for j in range(n)]).astype(BF)
                at += n
                if vectors is not None and i == 0:
                    total = get(len(ins) - 2)[...] + joined(get(len(ins) - 1)[...])
                    out[len(outs) - 1][...] = total
                    out[0][h:, :] = split_high(total)
                put(i)
            if through is not None:
                out[len(outs) - 1][...] = get(len(ins) - 1)[...]

        size = sum(h * p.cols for p, h in zip(parts, halves))
        made = staged(body, name, [], ins, outs, cost(size, 6 * size), deps=deps)
        sends = made[: len(parts)]
        vectors = made[-1] if len(made) > len(parts) else None
    for p, h in zip(parts, halves):
        p.rows = h
    return sends, vectors


def pack(me, parts, columns, count, name, vectors=None, deps=()):
    rows = min(p.rows for p in parts)
    widths = [c[2] // count for c in columns]
    ahead = 0 if vectors is None else 16 * vectors.shape[1] // (2 * rows)
    wide = ahead + sum(parts[c[0]].rows // rows * w for c, w in zip(columns, widths))
    ins, counts = [], []
    for p in parts:
        ins += p.inputs(0)
        counts.append(len(p.terms))
    outs = [shaped((2 * rows, wide)), shaped((2 * rows, wide), F32)]
    if vectors is not None:
        sent = parts[0].terms[-1]
        ins += [vectors, (sent, slice(parts[0].rows, parts[0].rows + 16), slice(0, parts[0].cols))]
        outs.append(shaped(vectors.shape, F32))

    def body(scalars, get, out, put, scratch):
        (me_ref,) = scalars
        sums, at = [], 0
        for n in counts:
            sums.append(add_up([get(at + j) for j in range(n)]))
            at += n
        if vectors is not None:
            vec = get(len(ins) - 2)[...] + joined(get(len(ins) - 1)[...])
            out[2][...] = vec
            put(2)
            store_vectors(out[0], vec, 2 * rows, ahead)
        for place, (ref, turn) in enumerate([(out[0], 0), (out[0], 1), (out[1], 0), (out[1], 1)]):
            distance = (1, 3, 0, 2)[place]
            for owner in range(count):

                @pl.when((me_ref[0] ^ distance) == owner)
                def _(ref=ref, owner=owner, turn=turn):
                    at = ahead
                    for (which, start, _), w in zip(columns, widths):
                        piece = sums[which][:, start + owner * w : start + (owner + 1) * w].astype(ref.dtype)
                        for j in range(piece.shape[0] // rows):
                            ref[turn * rows : (turn + 1) * rows, at : at + w] = piece[j * rows : (j + 1) * rows]
                            at += w

            if turn == 1:
                put(place // 2)

    size = sum(p.rows * p.cols for p in parts)
    long = pl.CostEstimate(flops=10**11, transcendentals=0, bytes_accessed=10**8)
    estimate = cost(2 * size, 6 * size) if vectors is not None else long
    return staged(body, name, [me], ins, outs, estimate, deps=deps)


def store_vectors(ref, vec, rows, ahead):
    both = split_high(vec)
    for i in range(rows // 16):
        ref[16 * i : 16 * (i + 1), :ahead] = both[:, i * ahead : (i + 1) * ahead]


def load_vectors(ref, rows, ahead):
    return joined(jnp.concatenate([ref[16 * i : 16 * (i + 1), :ahead] for i in range(rows // 16)], 1))


def pack_far(own, recv, name, vectors=None, deps=()):
    rows, wide = own.shape[0] // 2, own.shape[1]
    before = 0 if vectors is None else 16 * vectors.shape[1] // (2 * rows)
    ahead = 2 * before
    far = slice(rows, 2 * rows)
    ins = [(own, far, slice(0, wide)), (recv, far, slice(0, wide))]
    outs = [shaped((rows, wide + before))]
    if vectors is not None:
        ins += [vectors, (recv, slice(0, 2 * rows), slice(0, before))]
        outs.append(shaped(vectors.shape, F32))

    def body(scalars, get, out, put, scratch):
        out[0][:, ahead:] = (get(0)[:, before:] + get(1)[:, before:].astype(F32)).astype(BF)
        if vectors is not None:
            vec = get(2)[...] + load_vectors(get(3), 2 * rows, before)
            out[1][...] = vec
            store_vectors(out[0], vec, rows, ahead)

    size = rows * wide
    return staged(body, name, [], ins, outs, cost(size, 10 * size), deps=deps)


def narrow(vec):
    half = vec.shape[1] // 2
    return jnp.concatenate([vec[:4, :half], vec[:4, half:]], 0)


def pack_all(me, parts, columns, count, name, vectors, deps=()):
    rows = min(p.rows for p in parts)
    widths = [c[2] // count for c in columns]
    ahead = 8 * vectors.shape[1] // rows
    wide = ahead + sum(parts[c[0]].rows // rows * w for c, w in zip(columns, widths))
    ins, counts = [], []
    for p in parts:
        ins += p.inputs(0)
        counts.append(len(p.terms))
    sent = parts[0].terms[-1]
    ins += [vectors, (sent, slice(parts[0].rows, parts[0].rows + 16), slice(0, parts[0].cols))]
    outs = [shaped((rows, wide))] * (count - 1) + [shaped((rows, wide), F32), shaped(vectors.shape, F32)]

    def body(scalars, get, out, put, scratch):
        (me_ref,) = scalars
        sums, at = [], 0
        for n in counts:
            sums.append(add_up([get(at + j) for j in range(n)]))
            at += n
        vec = get(len(ins) - 2)[...] + joined(get(len(ins) - 1)[...])
        out[count][...] = vec
        put(count)
        for distance in (2, 3, 1, 0):
            ref = out[(distance - 1) % count]
            if distance:
                store_vectors(ref, narrow(vec), rows, ahead)
            for owner in range(count):

                @pl.when((me_ref[0] ^ distance) == owner)
                def _(ref=ref, owner=owner):
                    at = ahead
                    for (which, start, _), w in zip(columns, widths):
                        piece = sums[which][:, start + owner * w : start + (owner + 1) * w].astype(ref.dtype)
                        for j in range(piece.shape[0] // rows):
                            ref[:, at : at + w] = piece[j * rows : (j + 1) * rows]
                            at += w

            put((distance - 1) % count)

    size = sum(p.rows * p.cols for p in parts)
    made = staged(body, name, [me], ins, outs, cost(2 * size, 6 * size), deps=deps)
    return made[: count - 1], made[count - 1], made[count]


def unpack_all(own, messages, shape, name, vectors, deps=()):
    rows, wide = own.shape
    ahead = 8 * vectors.shape[1] // rows
    width = vectors.shape[1] // 3
    ins = [own, *messages, vectors]
    outs = [shaped(shape, F32)] + [shaped((width,), F32)] * 8 + [shaped((4 * width,), F32)]

    def body(scalars, get, out, put, scratch):
        total = get(0)[:, ahead:]
        both = jnp.zeros((8, vectors.shape[1] // 2), F32)
        for i in range(len(messages)):
            total = total + get(1 + i)[:, ahead:].astype(F32)
            both = both + load_vectors(get(1 + i), rows, ahead)
        for j in range(shape[0] // rows):
            out[0][j * rows : (j + 1) * rows, :] = total[:, j * shape[1] : (j + 1) * shape[1]]
        put(0)
        vec = get(1 + len(messages))[0:4, :] + jnp.concatenate([both[:4], both[4:]], 1)
        for i in range(2):
            for j in range(4):
                out[1 + 4 * i + j][...] = vec[j : j + 1, i * width : (i + 1) * width].reshape(width)
        for j in range(4):
            out[9][j * width : (j + 1) * width] = vec[j : j + 1, 2 * width :].reshape(width)

    return staged(body, name, [], ins, outs, cost(rows * wide, 20 * rows * wide), deps=deps)


def unpack(own, near, far, shapes, name, vectors=None, deps=(), tall=None, through=None):
    rows, wide = far.shape[0], own.shape[1]
    this, all_cols = slice(0, rows), slice(0, wide)
    ins = [(own, this, all_cols), (near, this, all_cols), far]
    outs = [shaped(shape[::-1] if i == tall else shape, F32) for i, shape in enumerate(shapes)]
    ahead = 0
    if through is not None:
        ins.append(through)
        outs.append(shaped(through.shape, F32))
    if vectors is not None:
        ahead = 16 * vectors.shape[1] // rows
        width = vectors.shape[1] // 3
        ins.append(vectors)
        outs += [shaped((width,), F32)] * 8 + [shaped((4 * width,), F32)]

    def body(scalars, get, out, put, scratch):
        before = ahead // 2
        total = get(0)[:, before:] + get(1)[:, before:].astype(F32) + get(2)[:, ahead:].astype(F32)
        at = 0
        for i, (height, width) in enumerate(shapes):
            if i == tall:
                turns = range(height // rows)
                whole = jnp.concatenate([total[:, at + j * width : at + (j + 1) * width] for j in turns], 0)
                out[i][...] = whole.T
                at += len(turns) * width
            else:
                for j in range(height // rows):
                    out[i][j * rows : (j + 1) * rows, :] = total[:, at : at + width]
                    at += width
            put(i)
        if through is not None:
            out[len(shapes)][...] = get(3)[...].astype(F32)
        if vectors is not None:
            vec = get(3)[...] + load_vectors(get(2), rows, ahead)
            wide = vec.shape[1] // 3
            base = len(shapes)
            for i in range(2):
                for j in range(4):
                    out[base + 4 * i + j][...] = vec[j : j + 1, i * wide : (i + 1) * wide].reshape(wide)
            for j in range(4):
                out[base + 8][j * wide : (j + 1) * wide] = vec[j : j + 1, 2 * wide :].reshape(wide)

    size = rows * wide
    return staged(body, name, [], ins, outs, cost(size, 12 * size), deps=deps)


def spec_sum(part, me, count):
    cols = part.shape[1] // count

    def mine(distance):
        return lax.dynamic_slice_in_dim(part, (me ^ distance) * cols, cols, 1)

    got = [lax.ppermute(mine(d).astype(BF), "spec", flip(count, d)) for d in range(1, count)]
    total = mine(0)
    for piece in got:
        total = total + piece.astype(F32)
    return total


def local(
    tokens,
    cotangent,
    lengths,
    projection,
    query_bias,
    value_bias,
    output_weight,
    output_bias,
    up_weight,
    up_bias,
    down_weight,
    down_bias,
    first_gain,
    first_shift,
    second_gain,
    second_shift,
):
    _, rows, width = tokens.shape
    hidden = up_weight.shape[1]
    cubes, count = lax.axis_size("cube"), lax.axis_size("spec")
    cube, spec = lax.axis_index("cube"), lax.axis_index("spec")
    tok = tokens.reshape(rows, width)
    cot = cotangent.reshape(rows, width)

    assert count == 4
    half_way = count // 2

    def partner(c, s):
        return (c ^ 1, s ^ half_way) if (c & 1) != (s // half_way) else (c, s)

    places = [(c, s) for c in range(cubes) for s in range(count)]

    def both_axes(move):
        return [(c * count + s, move(c, s)[0] * count + move(c, s)[1]) for c, s in places]

    exchange = both_axes(partner)
    pair = flip(cubes, 1)
    near = flip(count, 1)
    axes = ("cube", "spec")

    own_tok = tok
    tok = lax.ppermute(own_tok, axes, exchange)
    away = (cube & 1) != (spec // half_way)
    length = jnp.where(away, lax.ppermute(lengths, "cube", pair), lengths)[0].astype(jnp.int32)
    my_block = jnp.where(away, spec ^ half_way, spec).astype(jnp.int32)
    next_tok = lax.ppermute(tok, "spec", near)
    blocks = [tok, lax.ppermute(tok, "cube", pair), next_tok, lax.ppermute(next_tok, "cube", pair)]
    distances = [0, half_way, 1, half_way + 1]
    ids = jnp.stack([cube.astype(jnp.int32), my_block, length])

    bits = cubes.bit_length() - 1
    order_a = list(range(bits))
    order_b = [0] + list(range(bits - 1, 0, -1))
    place_a, place_b = tree_place(order_a), tree_place(order_b)
    split = cubes // 2

    def source_rows(place, offset, size, block):
        start = (jnp.asarray(place, jnp.int32) ^ cube) * block + offset
        return (start[:, None] + jnp.arange(size, dtype=jnp.int32)[None, :]).reshape(-1)

    def one_hot(source):
        return (source[:, None] == jnp.arange(width, dtype=jnp.int32)[None, :]).astype(BF)

    block = width // cubes
    part = block // 2
    chunks = 8
    lists = [list(map(int, place)) for place in (place_a, place_b)]
    perm_b = (lists[1], [0] * cubes, block, block)
    perm_mixed = (
        lists[0][:split] + lists[1][:split] + lists[0][split:] + lists[1][split:],
        ([0] * split + [part] * split) * 2,
        part,
        block,
    )
    if part % 16:
        perm_b, perm_mixed = (
            one_hot(jnp.concatenate([source_rows([r], f, size, block) for r, f in zip(relative, first)]))
            for relative, first, size, _ in (perm_b, perm_mixed)
        )
    places = lists[0] if cubes == chunks else None

    up_bias_row = up_bias.reshape(chunks, -1)
    hiddens, keys, values = [], [], []
    state = None
    for which in ((0, 1), (2,), (3,)):
        made = forward_step(
            which[-1] == count - 1,
            ids,
            [distances[i] for i in which],
            [blocks[i] for i in which],
            first_gain,
            first_shift,
            projection,
            query_bias,
            value_bias,
            state,
            cot,
            (up_bias_row,) if state is None else (),
        )
        for i in range(len(which)):
            hiddens.append(made[3 + 3 * i])
            keys.append(made[4 + 3 * i])
            values.append(made[5 + 3 * i])
        if state is None:
            q, qt, cot = made[3 + 3 * len(which) :]
            cot = lax.ppermute(cot, axes, exchange)
        state = (qt,) + tuple(made[:3])
    negl, attt = state[1], state[3]

    (
        block_out,
        down_keep,
        down_send,
        up_keep,
        up_send,
        da,
        dat,
        negd,
        gmid,
        vec_mid,
        grad_up_bias,
    ) = middle_step(
        ids,
        places,
        tok,
        cot,
        attt,
        output_weight,
        output_bias,
        second_gain,
        second_shift,
        up_weight,
        up_bias_row,
        down_weight,
        down_bias,
        perm_b,
    )
    if cubes != chunks:
        whole = jnp.concatenate([down_keep, down_send], 0).reshape(cubes, hidden // cubes, width)
        whole = jnp.take(whole, jnp.asarray(place_a, jnp.int32) ^ cube, axis=0)
        down_keep = whole[:split].reshape(hidden // 2, width)
        down_send = whole[split:].reshape(hidden // 2, width)

    down_recv = lax.ppermute(down_send, "cube", pair)
    up_recv = lax.ppermute(up_send, "cube", pair)

    common = (q, qt, da, dat, negl, negd)

    def back(which, state, last, deps, arrived=None, through=None):
        def pick(things):
            return [things[i] for i in which]

        some = (pick(keys), pick(values), pick(blocks))
        return backward_step(
            ids, pick(distances), *common, *some, projection, state, last, deps, arrived, through
        )

    dkv_3, g_3, vec_back, dqt, block_out = back((3,), None, False, (), None, block_out)
    block_out = lax.ppermute(block_out, axes, exchange)
    g_3 = lax.ppermute(g_3, "cube", pair)

    def hop(parts, sends, level):
        for p, send, order in zip(parts, sends, (order_a, order_b)):
            p.terms.append(lax.ppermute(send, "cube", flip(cubes, 1 << order[level])))

    levels = len(order_a)
    me = spec.astype(jnp.int32).reshape(1)
    ff = [Part(down_keep, down_recv), Part(up_keep, up_recv)]
    last = dqt
    if levels > 1:
        sends, _ = halve(ff, "sum_ff", None, (last, g_3))
        last = sends[0]
        hop(ff, sends, 1)
    dkv_2, g_2, dkv_1, g_1, dkv_0, g_0, vec_back, dq = back((2, 1, 0), (dqt, vec_back), True, (last,), g_3)
    g_2 = lax.ppermute(g_2, "spec", near)
    g_1 = lax.ppermute(g_1, "cube", pair)
    last = dq
    for level in range(2, levels):
        sends, _ = halve(ff, "sum_ff", None, (last, block_out))
        last = sends[0]
        hop(ff, sends, level)

    proj_a, proj_b, send_a, send_b, vectors = projection_step(
        ids, perm_mixed, dq, hiddens, [dkv_0, dkv_1, dkv_2, dkv_3], vec_mid, grad_up_bias, vec_back, (g_1, last)
    )
    proj = [
        Part(proj_a, lax.ppermute(send_a, "cube", pair)),
        Part(proj_b, lax.ppermute(send_b, "cube", pair)),
    ]
    aligned = width // cubes % 32 == 0
    far = flip(count, 2)
    last = vectors
    if aligned:
        columns = [(1, 0, hidden), (1, hidden, width), (0, 0, width)]
        ff_send, ff_own = pack(me, ff, columns, count, "pack_ff", None, (last,))
        last = ff_own
        ff_near = lax.ppermute(ff_send, "spec", near)
    for level in range(1, levels):
        sends, vectors = halve(proj, "sum_proj", vectors, (last,))
        last = sends[0]
        hop(proj, sends, level)
        if level == 1:
            grad_tokens, block_out = final_step(tok, first_gain, gmid, g_0, [g_1, g_2], block_out, (last,))
            last = grad_tokens
            grad_tokens = lax.ppermute(grad_tokens, axes, exchange)
    if aligned:
        (last,) = pack_far(ff_own, ff_near, "pack_ff_far", None, (last,))
        ff_far = lax.ppermute(last, "spec", far)
        pr_msgs, pr_own, vectors = pack_all(
            me, proj, [(0, 0, 3 * width), (1, 0, 3 * width)], count, "pack_proj", vectors, (last, grad_tokens)
        )
        pr_msgs = [lax.ppermute(m, "spec", flip(count, d + 1)) for d, m in enumerate(pr_msgs)]
        grad_up, grad_out, grad_down, grad_tokens = unpack(
            ff_own,
            ff_near,
            ff_far,
            [(width // cubes, hidden // count), (width // cubes, width // count), (hidden // cubes, width // count)],
            "unpack_ff",
            None,
            (pr_own,),
            2,
            grad_tokens,
        )
        grad_down = grad_down.T
        shape = (width // cubes, 3 * width // count)
        grad_proj, *vectors = unpack_all(pr_own, pr_msgs, shape, "unpack_proj", vectors, (grad_out,))
    else:
        grad_tokens = grad_tokens.astype(F32)
        vectors = vectors + joined(proj[0].terms[-1][-16:])
        vectors = sum([lax.ppermute(vectors, "spec", flip(count, d)) for d in range(1, count)], vectors)
        grad_up_out = ff[1].total()
        grad_up = spec_sum(grad_up_out[:, :hidden], spec, count)
        grad_out = spec_sum(grad_up_out[:, hidden:], spec, count)
        grad_down = spec_sum(ff[0].total(), spec, count)
        grad_proj = spec_sum(jnp.concatenate([p.total() for p in proj], 0), spec, count)
        vectors = [vectors[j, i * width : (i + 1) * width] for i in range(2) for j in range(4)] + [
            vectors[:4, 2 * width :].reshape(-1)
        ]

    return (
        block_out.reshape(tokens.shape),
        grad_tokens.reshape(tokens.shape),
        grad_proj,
        vectors[4],
        vectors[5],
        grad_out,
        vectors[3],
        grad_up,
        vectors[8],
        grad_down,
        vectors[0],
        vectors[6],
        vectors[7],
        vectors[1],
        vectors[2],
    )


def solution(mesh):
    return jax.shard_map(
        local,
        mesh=mesh,
        in_specs=(
            P("cube", "spec", None),
            P("cube", "spec", None),
            P("cube"),
        )
        + (P(),) * 13,
        out_specs=(
            P("cube", "spec", None),
            P("cube", "spec", None),
            P("cube", "spec"),
            P(),
            P(),
            P("cube", "spec"),
            P(),
            P("cube", "spec"),
            P(),
            P("cube", "spec"),
            P(),
            P(),
            P(),
            P(),
            P(),
        ),
        check_vma=False,
    )
```

```python
import math
from functools import partial

import jax
import jax.numpy as jnp
import numpy as np
from jax import lax
from jax.experimental import pallas as pl
from jax.experimental.pallas import tpu as pltpu
from jax.sharding import PartitionSpec as P

HEADS = 12
HD = 64
PAIRS = HEADS // 2
EPS = 1e-06
SCALE = HD ** (-0.5)
TO_EXP2 = SCALE * math.log2(math.e)
MASKED = -1e30

BF = jnp.bfloat16
F32 = jnp.float32


def dot(left, right):
    return jnp.dot(left, right, preferred_element_type=F32)


def dot_nt(left, right):
    return lax.dot_general(left, right, (((1,), (1,)), ((), ())), preferred_element_type=F32)


def dot_tn(left, right):
    return lax.dot_general(left, right, (((0,), (0,)), ((), ())), preferred_element_type=F32)


def normalize(values):
    average = jnp.mean(values, -1, keepdims=True)
    centred = values - average
    inverse = lax.rsqrt(jnp.mean(centred * centred, -1, keepdims=True) + EPS)
    return centred * inverse, inverse


def params(megabytes=64):
    return pltpu.CompilerParams(vmem_limit_bytes=megabytes * 2**20)


def cost(flops, nbytes, trans=0):
    return pl.CostEstimate(flops=flops // 1000, bytes_accessed=nbytes // 1000, transcendentals=trans // 1000)


def extra_lanes(ids_ref, distance, rows, ones):
    slot = lax.broadcasted_iota(jnp.int32, (rows, 128), 0) + (ids_ref[1] ^ distance) * rows
    lane = lax.broadcasted_iota(jnp.int32, (rows, 128), 1)
    masked = jnp.where(slot < ids_ref[2], 0.0, MASKED)
    rest = jnp.where(lane <= ones, 1.0, 0.0)
    return jnp.where(lane == 0, masked, rest).astype(BF)


def two_heads(part, extra):
    n = part.shape[1]
    zero = jnp.zeros((HD, n), part.dtype)
    left = jnp.concatenate([part[:HD], zero], 0)
    right = jnp.concatenate([zero, part[HD:]], 0)
    return jnp.concatenate([jnp.concatenate([left, right], 1), extra], 0)


def as_row(ref):
    return ref[...].reshape(1, -1)


def pair_lanes(pair):
    return slice(pair * 2 * HD, (pair + 1) * 2 * HD)


ANY = pl.BlockSpec(memory_space=pl.ANY)
SMEM = pl.BlockSpec(memory_space=pltpu.SMEM)


def staged(body, name, scalars, ins, outs, estimate, scratch=(), deps=()):
    parts = [x if isinstance(x, tuple) else (x, slice(0, x.shape[0]), slice(0, x.shape[-1])) for x in ins]
    shapes = []
    for x, rows, cols in parts:
        shapes.append((rows.stop - rows.start,) if x.ndim == 1 else (rows.stop - rows.start, cols.stop - cols.start))
    arrays = []
    for x, _, _ in parts:
        if not any(x is y for y in arrays):
            arrays.append(x)
    index = [[i for i, y in enumerate(arrays) if y is x][0] for x, _, _ in parts]
    n_s, n_a, n_i, n_o, n_x = len(scalars), len(arrays), len(ins), len(outs), len(scratch)

    def kernel(*refs):
        at = 0
        groups = []
        for n in (n_s, n_a, len(deps), n_o, n_x, n_i, n_o):
            groups.append(refs[at : at + n])
            at += n
        s_refs, a_ref, _, o_to, x_refs, i_ref, o_ref = groups
        i_sem, o_sem = refs[at:]
        loads = []
        for i, (x, rows, cols) in enumerate(parts):
            source = a_ref[index[i]]
            if shapes[i] != x.shape:
                source = source.at[rows, cols]
            loads.append(pltpu.make_async_copy(source, i_ref[i], i_sem.at[i]))
        stores = [pltpu.make_async_copy(o_ref[i], o_to[i], o_sem.at[i]) for i in range(n_o)]
        for load in loads:
            load.start()
        waited = set()
        sent = set()

        def get(i):
            if i not in waited:
                waited.add(i)
                loads[i].wait()
            return i_ref[i]

        def put(i, *where):
            sent.add(i)
            if where:
                pltpu.make_async_copy(o_ref[i].at[where], o_to[i].at[where], o_sem.at[i]).start()
            else:
                stores[i].start()

        body(s_refs, get, o_ref, put, x_refs)
        for i in range(n_i):
            get(i)
        for i in range(n_o):
            if i not in sent:
                put(i)
        for store in stores:
            store.wait()

    return pl.pallas_call(
        kernel,
        out_shape=list(outs),
        in_specs=[SMEM] * n_s + [ANY] * (n_a + len(deps)),
        out_specs=[ANY] * n_o,
        scratch_shapes=list(scratch)
        + [pltpu.VMEM(shape, x.dtype) for shape, (x, _, _) in zip(shapes, parts)]
        + [pltpu.VMEM(x.shape, x.dtype) for x in outs]
        + [pltpu.SemaphoreType.DMA((n_i,)), pltpu.SemaphoreType.DMA((n_o,))],
        compiler_params=params(),
        cost_estimate=estimate,
        name=name,
    )(*scalars, *arrays, *deps)


def shaped(shape, dtype=BF):
    return jax.ShapeDtypeStruct(shape, dtype)


def forward_step(last, ids, distances, toks, gain, shift, w, qb, vb, state, through, deps=()):
    first = state is None
    count = len(toks)
    rows, width = toks[0].shape
    block = shaped((rows, width))
    outs = [shaped((8, 2 * rows), F32), shaped((8, 2 * rows), F32), shaped((width, rows), F32)]
    outs += [block, block, block] * count
    full = slice(0, width)
    ins = [toks[0], gain, shift, vb, (w, full, slice(width, 2 * width)), (w, full, slice(2 * width, 3 * width))]
    if first:
        ins += [(w, full, full), qb]
        outs += [block, shaped((width, rows)), block]
    else:
        ins += list(state)
    at_tok = len(ins) - 1
    ins += toks[1:]
    if first:
        ins.append(through)

    def body(scalars, get, out, put, scratch):
        m_out, l_out, acc_out = out[:3]
        ones_row = (lax.broadcasted_iota(jnp.int32, (128, 2 * rows), 0) == 0).astype(BF)
        for i in range(count):
            h_out, k_out, v_out = out[3 + 3 * i : 6 + 3 * i]
            normed, _ = normalize(get(at_tok + i if i > 0 else 0)[...].astype(F32))
            hidden = (normed * as_row(get(1)) + as_row(get(2))).astype(BF)
            h_out[...] = hidden
            put(3 + 3 * i)
            k_out[...] = dot(hidden, get(4)[...]).astype(BF)
            put(4 + 3 * i)
            values = dot(hidden, get(5)[...]) + as_row(get(3))
            v_out[...] = values.astype(BF)
            put(5 + 3 * i)
            values_t = v_out[...].astype(F32).T.astype(BF)
            if first:
                at = 3 + 3 * count
                q_out, qt_out, through_out = out[at:]
                if i == 0:
                    q_out[...] = (dot(hidden, get(6)[...]) + as_row(get(7))).astype(BF)
                    put(at)
                    qt_out[...] = q_out[...].astype(F32).T.astype(BF)
                    put(at + 1)
                if i == count - 1:
                    through_out[...] = get(len(ins) - 1)[...]
                    put(at + 2)
                qt_ref = qt_out
            else:
                qt_ref = get(6)
            extra_keys = extra_lanes(scalars[0], distances[i], rows, 0)
            start = first and i == 0
            end = last and i == count - 1
            for pair in range(PAIRS):
                lanes = pair_lanes(pair)
                this = slice(pair, pair + 1)
                keys = jnp.concatenate([k_out[:, lanes], extra_keys], 1)
                scores = dot(keys, two_heads(qt_ref[lanes, :], ones_row))
                top = jnp.max(scores, 0, keepdims=True)
                if not start:
                    m_ref, l_ref, acc_ref = (get(7 + j) for j in range(3)) if i == 0 else (m_out, l_out, acc_out)
                    before = m_ref[this, :]
                    top = jnp.maximum(top, before)
                    fade = jnp.exp2((before - top) * TO_EXP2)
                weights = jnp.exp2((scores - top) * TO_EXP2)
                total = jnp.sum(weights, 0, keepdims=True)
                if not start:
                    total = total + l_ref[this, :] * fade
                both = dot(values_t[lanes, :], weights.astype(BF))
                for head in range(2):
                    own = slice(lanes.start + head * HD, lanes.start + (head + 1) * HD)
                    cols = slice(head * rows, (head + 1) * rows)
                    part = both[head * HD : (head + 1) * HD, cols]
                    if not start:
                        part = part + acc_ref[own, :] * fade[:, cols]
                    if end:
                        part = part / total[:, cols]
                    acc_out[own, :] = part
                m_out[this, :] = -(top + jnp.log2(total) * (1.0 / TO_EXP2)) if end else top
                l_out[this, :] = total
                if i == count - 1:
                    put(2, lanes)

    estimate = pl.CostEstimate(flops=count * 10**10, bytes_accessed=24 * 2**20, transcendentals=0)
    return staged(body, "attend", [ids], ins, outs, estimate, deps=deps)


def make_perm(ref, me, blocks, firsts, size, block):
    here = lax.broadcasted_iota(jnp.int32, (size, ref.shape[1]), 0)
    there = lax.broadcasted_iota(jnp.int32, (size, ref.shape[1]), 1)
    for i, (relative, first) in enumerate(zip(blocks, firsts)):
        start = (me ^ relative) * block + first
        ref[i * size : (i + 1) * size, :] = (here + start == there).astype(F32).astype(BF)


def middle_step(ids, places, tok, cot, attt, wo, ob, gain, shift, up, ub, down, db, perm):
    rows, width = tok.shape
    hidden = up.shape[1]
    chunks = 8
    chunk = hidden // chunks
    half = width // 2
    given = not isinstance(perm, tuple)
    ins = [attt, wo, ob, tok, gain, shift, up, ub, cot, down, db] + ([perm] if given else [])
    outs = [
        shaped((rows, width)),
        shaped((hidden // 2, width)),
        shaped((hidden // 2, width)),
        shaped((half, hidden + width)),
        shaped((half, hidden + width)),
        shaped((rows, width)),
        shaped((width, rows)),
        shaped((8, 2 * rows), F32),
        shaped((rows, width), F32),
        shaped((8, width), F32),
        shaped((8, chunk), F32),
    ]
    scratch = [
        pltpu.VMEM((rows, width), F32),
        pltpu.VMEM((rows, width), F32),
        pltpu.VMEM((rows, width), BF),
        pltpu.VMEM((width, rows), BF),
        pltpu.VMEM((rows, width), BF),
        pltpu.VMEM((rows, width), F32),
        pltpu.VMEM((rows, width), F32),
        pltpu.VMEM((width, width), BF),
    ]

    def body(scalars, get, out, put, scratch):
        (ids_ref,) = scalars
        block_out, down_keep, down_send, up_keep, up_send, da_out, dat_out, negd_out, gmid_out, vec_out, ubg_out = out
        mid_ref, norm_ref, h2_ref, h2t_ref, att_ref, res_ref, gh_ref, perm_ref = scratch
        if given:
            perm_ref[...] = get(11)[...]
        else:
            make_perm(perm_ref, ids_ref[0], *perm)
        attt_ref = get(0)
        att_ref[...] = attt_ref[...].T.astype(BF)
        projected = dot(att_ref[...], get(1)[...]) + as_row(get(2))
        middle = get(3)[...].astype(F32) + projected
        mid_ref[...] = middle
        normed, inverse = normalize(middle)
        norm_ref[...] = normed
        h2_ref[...] = (normed * as_row(get(4)) + as_row(get(5))).astype(BF)
        h2t_ref[...] = dot_nt(perm_ref[...], h2_ref[...]).astype(BF)
        up_ref, ub_ref, cot_ref, down_ref = get(6), get(7), get(8), get(9)
        for turn in range(chunks // 2):
            p = (2 * turn + chunks // 2) % chunks
            own = [p, p + 1] if places is None else [places[p] ^ ids_ref[0], places[p + 1] ^ ids_ref[0]]
            at = [pl.ds(pl.multiple_of(place * chunk, 128), chunk) for place in own]
            up_c = jnp.concatenate([up_ref[:, a] for a in at], 1)
            down_c = jnp.concatenate([down_ref[a, :] for a in at], 0)
            bias = jnp.concatenate([ub_ref[pl.ds(place, 1), :] for place in own], 1)
            before = dot(h2_ref[...], up_c) + bias
            cdf = 0.5 * (1.0 + lax.erf(before * math.sqrt(0.5)))
            slope = cdf + before * (jnp.exp(-0.5 * before * before) * (1.0 / math.sqrt(2.0 * math.pi)))
            lifted = (before * cdf).astype(BF)
            grad_lifted = dot_nt(cot_ref[...], down_c)
            grad_down = dot_tn(lifted, cot_ref[...]).astype(BF)
            to, first = (down_keep, p) if p < chunks // 2 else (down_send, p - chunks // 2)
            rows_to = pl.ds(first * chunk, 2 * chunk)
            to[rows_to, :] = grad_down
            put(1 if p < chunks // 2 else 2, rows_to)
            grad_before = (grad_lifted * slope).astype(BF)
            bias_grad = jnp.sum(grad_before.astype(F32), 0, keepdims=True)
            for i, place in enumerate(own):
                ubg_out[pl.ds(place, 1), :] = bias_grad[:, i * chunk : (i + 1) * chunk]
            grad_up = dot(h2t_ref[...], grad_before).astype(BF)
            for i, a in enumerate(at):
                cols = slice(i * chunk, (i + 1) * chunk)
                up_keep[:, a] = grad_up[:half, cols]
                up_send[:, a] = grad_up[half:, cols]
                put(3, slice(None), a)
                put(4, slice(None), a)
            part = dot(lifted, down_c)
            back = dot_nt(grad_before, up_c)
            if turn == 0:
                res_ref[...] = part
                gh_ref[...] = back
            else:
                res_ref[...] += part
                gh_ref[...] += back
        block_out[...] = (mid_ref[...] + (res_ref[...] + as_row(get(10)))).astype(BF)
        put(0)
        cot32 = cot_ref[...].astype(F32)
        grad = gh_ref[...]
        normed = norm_ref[...]
        vec_out[0:1, :] = jnp.sum(cot32, 0, keepdims=True)
        vec_out[1:2, :] = jnp.sum(grad * normed, 0, keepdims=True)
        vec_out[2:3, :] = jnp.sum(grad, 0, keepdims=True)
        scaled = grad * as_row(get(4))
        grad_middle = cot32 + inverse * (
            scaled
            - jnp.mean(scaled, -1, keepdims=True)
            - normed * jnp.mean(scaled * normed, -1, keepdims=True)
        )
        gmid_out[...] = grad_middle
        put(8)
        branch = grad_middle.astype(BF)
        vec_out[3:4, :] = jnp.sum(branch.astype(F32), 0, keepdims=True)
        vec_out[4:8, :] = jnp.zeros((4, width), F32)
        att_t = dot_nt(perm_ref[...], att_ref[...]).astype(BF)
        grad_out = dot(att_t, branch).astype(BF)
        cols = pl.ds(hidden, width)
        up_keep[:, cols] = grad_out[:half]
        up_send[:, cols] = grad_out[half:]
        put(3, slice(None), cols)
        put(4, slice(None), cols)
        grad_att = dot_nt(branch, get(1)[...]).astype(BF)
        da_out[...] = grad_att
        put(5)
        grad_att_t = grad_att.astype(F32).T
        dat_out[...] = grad_att_t.astype(BF)
        put(6)
        product = grad_att_t * attt_ref[...]
        for head in range(HEADS):
            spread = jnp.sum(product[head * HD : (head + 1) * HD], 0, keepdims=True)
            place = slice((head % 2) * rows, (head % 2 + 1) * rows)
            negd_out[head // 2 : head // 2 + 1, place] = -spread

    estimate = cost(12 * rows * width * hidden + 6 * rows * width * width, 30 * 2**20, 0)
    return staged(body, "middle", [ids], ins, outs, estimate, scratch)


def three_parts(row):
    high = row.astype(BF)
    rest = row - high.astype(F32)
    mid = rest.astype(BF)
    low = (rest - mid.astype(F32)).astype(BF)
    return high.astype(F32), mid.astype(F32), low.astype(F32)


def extra_rows(row, with_mask):
    n = row.shape[1]
    high, mid, low = three_parts(row)
    place = lax.broadcasted_iota(jnp.int32, (128, n), 0)
    out = jnp.where(place == 0, 1.0 if with_mask else 0.0, 0.0)
    out = jnp.where(place == 1, high, out)
    out = jnp.where(place == 2, mid, out)
    out = jnp.where(place == 3, low, out)
    return out.astype(BF)


def backward_step(ids, distances, q, qt, da, dat, negl, negd, keys, values, toks, w, state, last, deps, arrived=None, through=None):
    rows, width = q.shape
    blocks = len(keys)
    first = state is None
    ins = [qt, negl, dat, negd, q, da]
    for k, v in zip(keys, values):
        ins += [k, v]
    base_w = len(ins)
    ins += [w, *toks]
    base_state = len(ins)
    if not first:
        ins += list(state)
    at_extra = len(ins)
    ins += [x for x in (arrived, through) if x is not None]
    outs = []
    for i in range(blocks):
        outs += [shaped((rows, 2 * width)), shaped((rows, width), F32 if last and i == blocks - 1 else BF)]
    outs += [shaped((8, width), F32), shaped((rows, width)) if last else shaped((width, rows), F32)]
    if through is not None:
        outs.append(shaped(through.shape, through.dtype))

    def body(scalars, get, out, put, scratch):
        (dqt,) = scratch
        vec_out, end_out = out[2 * blocks : 2 * blocks + 2]
        lane = lax.broadcasted_iota(jnp.int32, (rows, 128), 1)
        zero = jnp.zeros((rows, 128), BF)
        value_bias = gain = shift = jnp.zeros((1, width), F32)
        query_bias = jnp.zeros((1, width), F32)
        for i in range(blocks):
            dkv_out, g_out = out[2 * i], out[2 * i + 1]
            extra_keys = extra_lanes(scalars[0], distances[i], rows, 3)
            qt_ref, negl_ref, dat_ref, negd_ref = get(0), get(1), get(2), get(3)
            k_ref, v_ref = get(6 + 2 * i), get(7 + 2 * i)
            keys_t = k_ref[...].astype(F32).T.astype(BF)
            for pair in range(PAIRS):
                lanes = pair_lanes(pair)
                key = jnp.concatenate([k_ref[:, lanes], extra_keys], 1)
                scores = dot(key, two_heads(qt_ref[lanes, :], extra_rows(negl_ref[pair : pair + 1, :], True)))
                softmaxed = jnp.exp2(scores * TO_EXP2)
                value = jnp.concatenate([v_ref[:, lanes], extra_keys], 1)
                centred = dot(value, two_heads(dat_ref[lanes, :], extra_rows(negd_ref[pair : pair + 1, :], False)))
                grad_scores = (softmaxed * centred).astype(BF)
                weights = softmaxed.astype(BF)
                q_pair = get(4)[:, lanes]
                da_pair = get(5)[:, lanes]
                q_both = jnp.concatenate([jnp.where(lane < HD, q_pair, zero), jnp.where(lane < HD, zero, q_pair)], 0)
                da_both = jnp.concatenate([jnp.where(lane < HD, da_pair, zero), jnp.where(lane < HD, zero, da_pair)], 0)
                dkv_out[:, lanes] = (dot(grad_scores, q_both) * SCALE).astype(BF)
                dkv_out[:, slice(width + lanes.start, width + lanes.stop)] = dot(weights, da_both).astype(BF)
                both = dot(keys_t[lanes, :], grad_scores)
                for head in range(2):
                    own = slice(lanes.start + head * HD, lanes.start + (head + 1) * HD)
                    part = both[head * HD : (head + 1) * HD, head * rows : (head + 1) * rows]
                    if i > 0:
                        part = part + dqt[own, :]
                    elif not first:
                        part = part + get(base_state)[own, :]
                    dqt[own, :] = part
            put(2 * i)
            w_ref = get(base_w)
            grad = dot_nt(dkv_out[...], w_ref[:, width:])
            if last and i == blocks - 1:
                dq = (dqt[...].T * SCALE).astype(BF)
                end_out[...] = dq
                put(2 * blocks + 1)
                query_bias = jnp.sum(dq.astype(F32), 0, keepdims=True)
                grad = grad + dot_nt(dq, w_ref[:, :width])
            if arrived is not None and i == 0:
                g_out[...] = (grad + get(at_extra)[...].astype(F32)).astype(g_out.dtype)
            else:
                g_out[...] = grad.astype(g_out.dtype)
            put(2 * i + 1)
            normed, _ = normalize(get(base_w + 1 + i)[...].astype(F32))
            value_bias = value_bias + jnp.sum(dkv_out[:, width:].astype(F32), 0, keepdims=True)
            gain = gain + jnp.sum(grad * normed, 0, keepdims=True)
            shift = shift + jnp.sum(grad, 0, keepdims=True)
        if not last:
            end_out[...] = dqt[...]
        if through is not None:
            out[2 * blocks + 2][...] = get(len(ins) - 1)[...]
        if not first:
            vec_ref = get(base_state + 1)
            value_bias = value_bias + vec_ref[1:2, :]
            gain = gain + vec_ref[2:3, :]
            shift = shift + vec_ref[3:4, :]
        vec_out[0:1, :] = query_bias
        vec_out[1:2, :] = value_bias
        vec_out[2:3, :] = gain
        vec_out[3:4, :] = shift
        vec_out[4:8, :] = jnp.zeros((4, width), F32)

    flops = blocks * (2 * rows * width * width * 3 + 10 * rows * rows * width * 4)
    estimate = cost(flops, 20 * 2**20, blocks * HEADS * rows * rows)
    return staged(
        body, "attend_back", [ids], ins, outs, estimate, [pltpu.VMEM((width, rows), F32)], deps
    )


def projection_step(ids, perm, dq, hiddens, dkvs, vec_mid, vec_up, vec_back, deps):
    rows, width = dq.shape
    count = len(hiddens)
    part = width // 4
    given = not isinstance(perm, tuple)
    ins = [*hiddens, dq, vec_mid, vec_up, vec_back, *dkvs] + ([perm] if given else [])
    outs = [shaped((n, 3 * width)) for n in (part, part, part + 16, part)] + [shaped((8, 3 * width), F32)]
    at = count

    def body(scalars, get, out, put, scratch):
        ht_ref, perm_ref = scratch
        if given:
            perm_ref[...] = get(len(ins) - 1)[...]
        else:
            make_perm(perm_ref, scalars[0][0], *perm)
        keep_a, keep_b, send_a, send_b, vec_ref = out
        for i in range(count):
            ht_ref[:, i * rows : (i + 1) * rows] = dot_nt(perm_ref[...], get(i)[...]).astype(BF)
        vec_ref[0:4, :width] = get(at + 1)[0:4, :]
        vec_ref[0:4, width : 2 * width] = get(at + 3)[0:4, :]
        up = jnp.concatenate([get(at + 2)[i : i + 1, :] for i in range(get(at + 2).shape[0])], 1)
        for i in range(4):
            vec_ref[i : i + 1, 2 * width :] = up[:, i * width : (i + 1) * width]
        vec_ref[4:8, :] = jnp.zeros((4, 3 * width), F32)
        send_a[part:, :] = split_high(vec_ref[...])
        put(4)
        for third in range(3):
            if third == 0:
                grad = dot(ht_ref[:, :rows], get(at)[...])
            else:
                own = slice((third - 1) * width, third * width)
                grad = dot(ht_ref[...], jnp.concatenate([get(at + 4 + i)[:, own] for i in range(count)], 0))
            grad = grad.astype(BF)
            cols = pl.ds(third * width, width)
            send_a[:part, cols] = grad[2 * part : 3 * part]
            put(2, slice(None), cols)
            send_b[:, cols] = grad[3 * part :]
            put(3, slice(None), cols)
            keep_a[:, cols] = grad[:part]
            put(0, slice(None), cols)
            keep_b[:, cols] = grad[part : 2 * part]
            put(1, slice(None), cols)

    estimate = cost(2 * rows * width * width * (1 + 2 * count), 12 * 2**20, 0)
    return staged(
        body,
        "projection_grad",
        [ids],
        ins,
        outs,
        estimate,
        [pltpu.VMEM((width, count * rows), BF), pltpu.VMEM((width, width), BF)],
        deps,
    )


def final_step(tok, gain, gmid, g, pieces, block_out, deps=()):
    def body(scalars, get, out, put, scratch):
        normed, inverse = normalize(get(0)[...].astype(F32))
        total = get(3)[...]
        for i in range(len(pieces)):
            total = total + get(4 + i)[...].astype(F32)
        scaled = total * as_row(get(1))
        out[0][...] = (
            get(2)[...]
            + inverse
            * (
                scaled
                - jnp.mean(scaled, -1, keepdims=True)
                - normed * jnp.mean(scaled * normed, -1, keepdims=True)
            )
        ).astype(BF)
        put(0)
        out[1][...] = get(len(ins) - 1)[...]

    estimate = pl.CostEstimate(flops=10**11, transcendentals=0, bytes_accessed=10**8)
    ins = [tok, gain, gmid, g, *pieces, block_out]
    return staged(body, "norm_back", [], ins, [shaped(tok.shape)] * 2, estimate, deps=deps)


def flip(count, distance):
    return [(i, i ^ distance) for i in range(count)]


def tree_place(bits):
    n = len(bits)
    return np.array([sum(((p >> (n - 1 - i)) & 1) << bit for i, bit in enumerate(bits)) for p in range(1 << n)])


def split_high(values):
    high = values.astype(BF)
    return jnp.concatenate([high.astype(F32), values - high.astype(F32)], 0).astype(BF)


def joined(both):
    both = both.astype(F32)
    return both[:8] + both[8:]


class Part:
    def __init__(self, keep, recv):
        self.terms, self.rows, self.cols = [keep, recv], keep.shape[0], keep.shape[1]

    def inputs(self, start):
        return [(x, slice(start, self.rows), slice(0, self.cols)) for x in self.terms]

    def total(self):
        return sum(x[: self.rows].astype(F32) for x in self.terms)


def add_up(refs):
    total = refs[0][...].astype(F32)
    for ref in refs[1:]:
        total = total + ref[...].astype(F32)
    return total


def halve(parts, name, vectors=None, deps=(), through=None):
    halves = [p.rows // 2 for p in parts]
    if any(h % 16 for h in halves):
        sends = [p.total()[h:].astype(BF) for p, h in zip(parts, halves)]
        if vectors is not None:
            vectors = vectors + joined(parts[0].terms[-1][parts[0].rows :])
            sends[0] = jnp.concatenate([sends[0], split_high(vectors)], 0)
        vectors = through if vectors is None else vectors
    else:
        ins, counts = [], []
        for p, h in zip(parts, halves):
            ins += p.inputs(h)
            counts.append(len(p.terms))
        outs = [shaped((h, p.cols)) for p, h in zip(parts, halves)]
        if vectors is not None:
            sent, rows = parts[0].terms[-1], parts[0].rows
            ins += [vectors, (sent, slice(rows, rows + 16), slice(0, parts[0].cols))]
            outs[0] = shaped((halves[0] + 16, parts[0].cols))
            outs.append(shaped(vectors.shape, F32))
        if through is not None:
            ins.append(through)
            outs.append(shaped(through.shape, through.dtype))

        def body(scalars, get, out, put, scratch):
            at = 0
            for i, (n, h) in enumerate(zip(counts, halves)):
                out[i][:h, :] = add_up([get(at + j) for j in range(n)]).astype(BF)
                at += n
                if vectors is not None and i == 0:
                    total = get(len(ins) - 2)[...] + joined(get(len(ins) - 1)[...])
                    out[len(outs) - 1][...] = total
                    out[0][h:, :] = split_high(total)
                put(i)
            if through is not None:
                out[len(outs) - 1][...] = get(len(ins) - 1)[...]

        size = sum(h * p.cols for p, h in zip(parts, halves))
        made = staged(body, name, [], ins, outs, cost(size, 6 * size), deps=deps)
        sends = made[: len(parts)]
        vectors = made[-1] if len(made) > len(parts) else None
    for p, h in zip(parts, halves):
        p.rows = h
    return sends, vectors


def pack(me, parts, columns, count, name, vectors=None, deps=()):
    rows = min(p.rows for p in parts)
    widths = [c[2] // count for c in columns]
    ahead = 0 if vectors is None else 16 * vectors.shape[1] // (2 * rows)
    wide = ahead + sum(parts[c[0]].rows // rows * w for c, w in zip(columns, widths))
    ins, counts = [], []
    for p in parts:
        ins += p.inputs(0)
        counts.append(len(p.terms))
    outs = [shaped((2 * rows, wide)), shaped((2 * rows, wide), F32)]
    if vectors is not None:
        sent = parts[0].terms[-1]
        ins += [vectors, (sent, slice(parts[0].rows, parts[0].rows + 16), slice(0, parts[0].cols))]
        outs.append(shaped(vectors.shape, F32))

    def body(scalars, get, out, put, scratch):
        (me_ref,) = scalars
        sums, at = [], 0
        for n in counts:
            sums.append(add_up([get(at + j) for j in range(n)]))
            at += n
        if vectors is not None:
            vec = get(len(ins) - 2)[...] + joined(get(len(ins) - 1)[...])
            out[2][...] = vec
            put(2)
            store_vectors(out[0], vec, 2 * rows, ahead)
        for place, (ref, turn) in enumerate([(out[0], 0), (out[0], 1), (out[1], 0), (out[1], 1)]):
            distance = (1, 3, 0, 2)[place]
            for owner in range(count):

                @pl.when((me_ref[0] ^ distance) == owner)
                def _(ref=ref, owner=owner, turn=turn):
                    at = ahead
                    for (which, start, _), w in zip(columns, widths):
                        piece = sums[which][:, start + owner * w : start + (owner + 1) * w].astype(ref.dtype)
                        for j in range(piece.shape[0] // rows):
                            ref[turn * rows : (turn + 1) * rows, at : at + w] = piece[j * rows : (j + 1) * rows]
                            at += w

            if turn == 1:
                put(place // 2)

    size = sum(p.rows * p.cols for p in parts)
    long = pl.CostEstimate(flops=10**11, transcendentals=0, bytes_accessed=10**8)
    estimate = cost(2 * size, 6 * size) if vectors is not None else long
    return staged(body, name, [me], ins, outs, estimate, deps=deps)


def store_vectors(ref, vec, rows, ahead):
    both = split_high(vec)
    for i in range(rows // 16):
        ref[16 * i : 16 * (i + 1), :ahead] = both[:, i * ahead : (i + 1) * ahead]


def load_vectors(ref, rows, ahead):
    return joined(jnp.concatenate([ref[16 * i : 16 * (i + 1), :ahead] for i in range(rows // 16)], 1))


def pack_far(own, recv, name, vectors=None, deps=()):
    rows, wide = own.shape[0] // 2, own.shape[1]
    before = 0 if vectors is None else 16 * vectors.shape[1] // (2 * rows)
    ahead = 2 * before
    far = slice(rows, 2 * rows)
    ins = [(own, far, slice(0, wide)), (recv, far, slice(0, wide))]
    outs = [shaped((rows, wide + before))]
    if vectors is not None:
        ins += [vectors, (recv, slice(0, 2 * rows), slice(0, before))]
        outs.append(shaped(vectors.shape, F32))

    def body(scalars, get, out, put, scratch):
        out[0][:, ahead:] = (get(0)[:, before:] + get(1)[:, before:].astype(F32)).astype(BF)
        if vectors is not None:
            vec = get(2)[...] + load_vectors(get(3), 2 * rows, before)
            out[1][...] = vec
            store_vectors(out[0], vec, rows, ahead)

    size = rows * wide
    return staged(body, name, [], ins, outs, cost(size, 10 * size), deps=deps)


def narrow(vec):
    half = vec.shape[1] // 2
    return jnp.concatenate([vec[:4, :half], vec[:4, half:]], 0)


def pack_all(me, parts, columns, count, name, vectors, deps=()):
    rows = min(p.rows for p in parts)
    widths = [c[2] // count for c in columns]
    ahead = 8 * vectors.shape[1] // rows
    wide = ahead + sum(parts[c[0]].rows // rows * w for c, w in zip(columns, widths))
    ins, counts = [], []
    for p in parts:
        ins += p.inputs(0)
        counts.append(len(p.terms))
    sent = parts[0].terms[-1]
    ins += [vectors, (sent, slice(parts[0].rows, parts[0].rows + 16), slice(0, parts[0].cols))]
    outs = [shaped((rows, wide))] * (count - 1) + [shaped((rows, wide), F32), shaped(vectors.shape, F32)]

    def body(scalars, get, out, put, scratch):
        (me_ref,) = scalars
        sums, at = [], 0
        for n in counts:
            sums.append(add_up([get(at + j) for j in range(n)]))
            at += n
        vec = get(len(ins) - 2)[...] + joined(get(len(ins) - 1)[...])
        out[count][...] = vec
        put(count)
        for distance in (2, 3, 1, 0):
            ref = out[(distance - 1) % count]
            if distance:
                store_vectors(ref, narrow(vec), rows, ahead)
            for owner in range(count):

                @pl.when((me_ref[0] ^ distance) == owner)
                def _(ref=ref, owner=owner):
                    at = ahead
                    for (which, start, _), w in zip(columns, widths):
                        piece = sums[which][:, start + owner * w : start + (owner + 1) * w].astype(ref.dtype)
                        for j in range(piece.shape[0] // rows):
                            ref[:, at : at + w] = piece[j * rows : (j + 1) * rows]
                            at += w

            put((distance - 1) % count)

    size = sum(p.rows * p.cols for p in parts)
    made = staged(body, name, [me], ins, outs, cost(2 * size, 6 * size), deps=deps)
    return made[: count - 1], made[count - 1], made[count]


def unpack_all(own, messages, shape, name, vectors, deps=()):
    rows, wide = own.shape
    ahead = 8 * vectors.shape[1] // rows
    width = vectors.shape[1] // 3
    ins = [own, *messages, vectors]
    outs = [shaped(shape, F32)] + [shaped((width,), F32)] * 8 + [shaped((4 * width,), F32)]

    def body(scalars, get, out, put, scratch):
        total = get(0)[:, ahead:]
        both = jnp.zeros((8, vectors.shape[1] // 2), F32)
        for i in range(len(messages)):
            total = total + get(1 + i)[:, ahead:].astype(F32)
            both = both + load_vectors(get(1 + i), rows, ahead)
        for j in range(shape[0] // rows):
            out[0][j * rows : (j + 1) * rows, :] = total[:, j * shape[1] : (j + 1) * shape[1]]
        put(0)
        vec = get(1 + len(messages))[0:4, :] + jnp.concatenate([both[:4], both[4:]], 1)
        for i in range(2):
            for j in range(4):
                out[1 + 4 * i + j][...] = vec[j : j + 1, i * width : (i + 1) * width].reshape(width)
        for j in range(4):
            out[9][j * width : (j + 1) * width] = vec[j : j + 1, 2 * width :].reshape(width)

    return staged(body, name, [], ins, outs, cost(rows * wide, 20 * rows * wide), deps=deps)


def unpack(own, near, far, shapes, name, vectors=None, deps=(), tall=None, through=None):
    rows, wide = far.shape[0], own.shape[1]
    this, all_cols = slice(0, rows), slice(0, wide)
    ins = [(own, this, all_cols), (near, this, all_cols), far]
    outs = [shaped(shape[::-1] if i == tall else shape, F32) for i, shape in enumerate(shapes)]
    ahead = 0
    if through is not None:
        ins.append(through)
        outs.append(shaped(through.shape, F32))
    if vectors is not None:
        ahead = 16 * vectors.shape[1] // rows
        width = vectors.shape[1] // 3
        ins.append(vectors)
        outs += [shaped((width,), F32)] * 8 + [shaped((4 * width,), F32)]

    def body(scalars, get, out, put, scratch):
        before = ahead // 2
        total = get(0)[:, before:] + get(1)[:, before:].astype(F32) + get(2)[:, ahead:].astype(F32)
        at = 0
        for i, (height, width) in enumerate(shapes):
            if i == tall:
                turns = range(height // rows)
                whole = jnp.concatenate([total[:, at + j * width : at + (j + 1) * width] for j in turns], 0)
                out[i][...] = whole.T
                at += len(turns) * width
            else:
                for j in range(height // rows):
                    out[i][j * rows : (j + 1) * rows, :] = total[:, at : at + width]
                    at += width
            put(i)
        if through is not None:
            out[len(shapes)][...] = get(3)[...].astype(F32)
        if vectors is not None:
            vec = get(3)[...] + load_vectors(get(2), rows, ahead)
            wide = vec.shape[1] // 3
            base = len(shapes)
            for i in range(2):
                for j in range(4):
                    out[base + 4 * i + j][...] = vec[j : j + 1, i * wide : (i + 1) * wide].reshape(wide)
            for j in range(4):
                out[base + 8][j * wide : (j + 1) * wide] = vec[j : j + 1, 2 * wide :].reshape(wide)

    size = rows * wide
    return staged(body, name, [], ins, outs, cost(size, 12 * size), deps=deps)


def spec_sum(part, me, count):
    cols = part.shape[1] // count

    def mine(distance):
        return lax.dynamic_slice_in_dim(part, (me ^ distance) * cols, cols, 1)

    got = [lax.ppermute(mine(d).astype(BF), "spec", flip(count, d)) for d in range(1, count)]
    total = mine(0)
    for piece in got:
        total = total + piece.astype(F32)
    return total


def local(
    tokens,
    cotangent,
    lengths,
    projection,
    query_bias,
    value_bias,
    output_weight,
    output_bias,
    up_weight,
    up_bias,
    down_weight,
    down_bias,
    first_gain,
    first_shift,
    second_gain,
    second_shift,
):
    _, rows, width = tokens.shape
    hidden = up_weight.shape[1]
    cubes, count = lax.axis_size("cube"), lax.axis_size("spec")
    cube, spec = lax.axis_index("cube"), lax.axis_index("spec")
    tok = tokens.reshape(rows, width)
    cot = cotangent.reshape(rows, width)

    assert count == 4
    half_way = count // 2

    def partner(c, s):
        return (c ^ 1, s ^ half_way) if (c & 1) != (s // half_way) else (c, s)

    places = [(c, s) for c in range(cubes) for s in range(count)]

    def both_axes(move):
        return [(c * count + s, move(c, s)[0] * count + move(c, s)[1]) for c, s in places]

    exchange = both_axes(partner)
    pair = flip(cubes, 1)
    near = flip(count, 1)
    axes = ("cube", "spec")

    own_tok = tok
    tok = lax.ppermute(own_tok, axes, exchange)
    away = (cube & 1) != (spec // half_way)
    length = jnp.where(away, lax.ppermute(lengths, "cube", pair), lengths)[0].astype(jnp.int32)
    my_block = jnp.where(away, spec ^ half_way, spec).astype(jnp.int32)
    next_tok = lax.ppermute(tok, "spec", near)
    blocks = [tok, lax.ppermute(tok, "cube", pair), next_tok, lax.ppermute(next_tok, "cube", pair)]
    distances = [0, half_way, 1, half_way + 1]
    ids = jnp.stack([cube.astype(jnp.int32), my_block, length])

    bits = cubes.bit_length() - 1
    order_a = list(range(bits))
    order_b = [0] + list(range(bits - 1, 0, -1))
    place_a, place_b = tree_place(order_a), tree_place(order_b)
    split = cubes // 2

    def source_rows(place, offset, size, block):
        start = (jnp.asarray(place, jnp.int32) ^ cube) * block + offset
        return (start[:, None] + jnp.arange(size, dtype=jnp.int32)[None, :]).reshape(-1)

    def one_hot(source):
        return (source[:, None] == jnp.arange(width, dtype=jnp.int32)[None, :]).astype(BF)

    block = width // cubes
    part = block // 2
    chunks = 8
    lists = [list(map(int, place)) for place in (place_a, place_b)]
    perm_b = (lists[1], [0] * cubes, block, block)
    perm_mixed = (
        lists[0][:split] + lists[1][:split] + lists[0][split:] + lists[1][split:],
        ([0] * split + [part] * split) * 2,
        part,
        block,
    )
    if part % 16:
        perm_b, perm_mixed = (
            one_hot(jnp.concatenate([source_rows([r], f, size, block) for r, f in zip(relative, first)]))
            for relative, first, size, _ in (perm_b, perm_mixed)
        )
    places = lists[0] if cubes == chunks else None

    up_bias_row = up_bias.reshape(chunks, -1)
    hiddens, keys, values = [], [], []
    state = None
    for which in ((0, 1), (2,), (3,)):
        made = forward_step(
            which[-1] == count - 1,
            ids,
            [distances[i] for i in which],
            [blocks[i] for i in which],
            first_gain,
            first_shift,
            projection,
            query_bias,
            value_bias,
            state,
            cot,
            (up_bias_row,) if state is None else (),
        )
        for i in range(len(which)):
            hiddens.append(made[3 + 3 * i])
            keys.append(made[4 + 3 * i])
            values.append(made[5 + 3 * i])
        if state is None:
            q, qt, cot = made[3 + 3 * len(which) :]
            cot = lax.ppermute(cot, axes, exchange)
        state = (qt,) + tuple(made[:3])
    negl, attt = state[1], state[3]

    (
        block_out,
        down_keep,
        down_send,
        up_keep,
        up_send,
        da,
        dat,
        negd,
        gmid,
        vec_mid,
        grad_up_bias,
    ) = middle_step(
        ids,
        places,
        tok,
        cot,
        attt,
        output_weight,
        output_bias,
        second_gain,
        second_shift,
        up_weight,
        up_bias_row,
        down_weight,
        down_bias,
        perm_b,
    )
    if cubes != chunks:
        whole = jnp.concatenate([down_keep, down_send], 0).reshape(cubes, hidden // cubes, width)
        whole = jnp.take(whole, jnp.asarray(place_a, jnp.int32) ^ cube, axis=0)
        down_keep = whole[:split].reshape(hidden // 2, width)
        down_send = whole[split:].reshape(hidden // 2, width)

    down_recv = lax.ppermute(down_send, "cube", pair)
    up_recv = lax.ppermute(up_send, "cube", pair)

    common = (q, qt, da, dat, negl, negd)

    def back(which, state, last, deps, arrived=None, through=None):
        def pick(things):
            return [things[i] for i in which]

        some = (pick(keys), pick(values), pick(blocks))
        return backward_step(
            ids, pick(distances), *common, *some, projection, state, last, deps, arrived, through
        )

    dkv_3, g_3, vec_back, dqt, block_out = back((3,), None, False, (), None, block_out)
    block_out = lax.ppermute(block_out, axes, exchange)
    g_3 = lax.ppermute(g_3, "cube", pair)

    def hop(parts, sends, level):
        for p, send, order in zip(parts, sends, (order_a, order_b)):
            p.terms.append(lax.ppermute(send, "cube", flip(cubes, 1 << order[level])))

    levels = len(order_a)
    me = spec.astype(jnp.int32).reshape(1)
    ff = [Part(down_keep, down_recv), Part(up_keep, up_recv)]
    last = dqt
    if levels > 1:
        sends, _ = halve(ff, "sum_ff", None, (last, g_3))
        last = sends[0]
        hop(ff, sends, 1)
    dkv_2, g_2, dkv_1, g_1, dkv_0, g_0, vec_back, dq = back((2, 1, 0), (dqt, vec_back), True, (last,), g_3)
    g_2 = lax.ppermute(g_2, "spec", near)
    g_1 = lax.ppermute(g_1, "cube", pair)
    last = dq
    for level in range(2, levels):
        sends, _ = halve(ff, "sum_ff", None, (last, block_out))
        last = sends[0]
        hop(ff, sends, level)

    proj_a, proj_b, send_a, send_b, vectors = projection_step(
        ids, perm_mixed, dq, hiddens, [dkv_0, dkv_1, dkv_2, dkv_3], vec_mid, grad_up_bias, vec_back, (g_1, last)
    )
    proj = [
        Part(proj_a, lax.ppermute(send_a, "cube", pair)),
        Part(proj_b, lax.ppermute(send_b, "cube", pair)),
    ]
    aligned = width // cubes % 32 == 0
    far = flip(count, 2)
    last = vectors
    if aligned:
        columns = [(1, 0, hidden), (1, hidden, width), (0, 0, width)]
        ff_send, ff_own = pack(me, ff, columns, count, "pack_ff", None, (last,))
        last = ff_own
        ff_near = lax.ppermute(ff_send, "spec", near)
    for level in range(1, levels):
        sends, vectors = halve(proj, "sum_proj", vectors, (last,))
        last = sends[0]
        hop(proj, sends, level)
        if level == 1:
            grad_tokens, block_out = final_step(tok, first_gain, gmid, g_0, [g_1, g_2], block_out, (last,))
            last = grad_tokens
            grad_tokens = lax.ppermute(grad_tokens, axes, exchange)
    if aligned:
        (last,) = pack_far(ff_own, ff_near, "pack_ff_far", None, (last,))
        ff_far = lax.ppermute(last, "spec", far)
        pr_msgs, pr_own, vectors = pack_all(
            me, proj, [(0, 0, 3 * width), (1, 0, 3 * width)], count, "pack_proj", vectors, (last,)
        )
        pr_msgs = [lax.ppermute(m, "spec", flip(count, d + 1)) for d, m in enumerate(pr_msgs)]
        grad_up, grad_out, grad_down, grad_tokens = unpack(
            ff_own,
            ff_near,
            ff_far,
            [(width // cubes, hidden // count), (width // cubes, width // count), (hidden // cubes, width // count)],
            "unpack_ff",
            None,
            (pr_own,),
            2,
            grad_tokens,
        )
        grad_down = grad_down.T
        shape = (width // cubes, 3 * width // count)
        grad_proj, *vectors = unpack_all(pr_own, pr_msgs, shape, "unpack_proj", vectors, (grad_out,))
    else:
        grad_tokens = grad_tokens.astype(F32)
        vectors = vectors + joined(proj[0].terms[-1][-16:])
        vectors = sum([lax.ppermute(vectors, "spec", flip(count, d)) for d in range(1, count)], vectors)
        grad_up_out = ff[1].total()
        grad_up = spec_sum(grad_up_out[:, :hidden], spec, count)
        grad_out = spec_sum(grad_up_out[:, hidden:], spec, count)
        grad_down = spec_sum(ff[0].total(), spec, count)
        grad_proj = spec_sum(jnp.concatenate([p.total() for p in proj], 0), spec, count)
        vectors = [vectors[j, i * width : (i + 1) * width] for i in range(2) for j in range(4)] + [
            vectors[:4, 2 * width :].reshape(-1)
        ]

    return (
        block_out.reshape(tokens.shape),
        grad_tokens.reshape(tokens.shape),
        grad_proj,
        vectors[4],
        vectors[5],
        grad_out,
        vectors[3],
        grad_up,
        vectors[8],
        grad_down,
        vectors[0],
        vectors[6],
        vectors[7],
        vectors[1],
        vectors[2],
    )


def solution(mesh):
    return jax.shard_map(
        local,
        mesh=mesh,
        in_specs=(
            P("cube", "spec", None),
            P("cube", "spec", None),
            P("cube"),
        )
        + (P(),) * 13,
        out_specs=(
            P("cube", "spec", None),
            P("cube", "spec", None),
            P("cube", "spec"),
            P(),
            P(),
            P("cube", "spec"),
            P(),
            P("cube", "spec"),
            P(),
            P("cube", "spec"),
            P(),
            P(),
            P(),
            P(),
            P(),
        ),
        check_vma=False,
    )
```

```python
import math
from functools import partial

import jax
import jax.numpy as jnp
import numpy as np
from jax import lax
from jax.experimental import pallas as pl
from jax.experimental.pallas import tpu as pltpu
from jax.sharding import PartitionSpec as P

HEADS = 12
HD = 64
PAIRS = HEADS // 2
EPS = 1e-06
SCALE = HD ** (-0.5)
TO_EXP2 = SCALE * math.log2(math.e)
MASKED = -1e30

BF = jnp.bfloat16
F32 = jnp.float32


def dot(left, right):
    return jnp.dot(left, right, preferred_element_type=F32)


def dot_nt(left, right):
    return lax.dot_general(left, right, (((1,), (1,)), ((), ())), preferred_element_type=F32)


def dot_tn(left, right):
    return lax.dot_general(left, right, (((0,), (0,)), ((), ())), preferred_element_type=F32)


def normalize(values):
    average = jnp.mean(values, -1, keepdims=True)
    centred = values - average
    inverse = lax.rsqrt(jnp.mean(centred * centred, -1, keepdims=True) + EPS)
    return centred * inverse, inverse


def params(megabytes=64):
    return pltpu.CompilerParams(vmem_limit_bytes=megabytes * 2**20)


def cost(flops, nbytes, trans=0):
    return pl.CostEstimate(flops=flops // 1000, bytes_accessed=nbytes // 1000, transcendentals=trans // 1000)


def extra_lanes(ids_ref, distance, rows, ones):
    slot = lax.broadcasted_iota(jnp.int32, (rows, 128), 0) + (ids_ref[1] ^ distance) * rows
    lane = lax.broadcasted_iota(jnp.int32, (rows, 128), 1)
    masked = jnp.where(slot < ids_ref[2], 0.0, MASKED)
    rest = jnp.where(lane <= ones, 1.0, 0.0)
    return jnp.where(lane == 0, masked, rest).astype(BF)


def two_heads(part, extra):
    n = part.shape[1]
    zero = jnp.zeros((HD, n), part.dtype)
    left = jnp.concatenate([part[:HD], zero], 0)
    right = jnp.concatenate([zero, part[HD:]], 0)
    return jnp.concatenate([jnp.concatenate([left, right], 1), extra], 0)


def as_row(ref):
    return ref[...].reshape(1, -1)


def pair_lanes(pair):
    return slice(pair * 2 * HD, (pair + 1) * 2 * HD)


ANY = pl.BlockSpec(memory_space=pl.ANY)
SMEM = pl.BlockSpec(memory_space=pltpu.SMEM)


def staged(body, name, scalars, ins, outs, estimate, scratch=(), deps=()):
    parts = [x if isinstance(x, tuple) else (x, slice(0, x.shape[0]), slice(0, x.shape[-1])) for x in ins]
    shapes = []
    for x, rows, cols in parts:
        shapes.append((rows.stop - rows.start,) if x.ndim == 1 else (rows.stop - rows.start, cols.stop - cols.start))
    arrays = []
    for x, _, _ in parts:
        if not any(x is y for y in arrays):
            arrays.append(x)
    index = [[i for i, y in enumerate(arrays) if y is x][0] for x, _, _ in parts]
    n_s, n_a, n_i, n_o, n_x = len(scalars), len(arrays), len(ins), len(outs), len(scratch)

    def kernel(*refs):
        at = 0
        groups = []
        for n in (n_s, n_a, len(deps), n_o, n_x, n_i, n_o):
            groups.append(refs[at : at + n])
            at += n
        s_refs, a_ref, _, o_to, x_refs, i_ref, o_ref = groups
        i_sem, o_sem = refs[at:]
        loads = []
        for i, (x, rows, cols) in enumerate(parts):
            source = a_ref[index[i]]
            if shapes[i] != x.shape:
                source = source.at[rows, cols]
            loads.append(pltpu.make_async_copy(source, i_ref[i], i_sem.at[i]))
        stores = [pltpu.make_async_copy(o_ref[i], o_to[i], o_sem.at[i]) for i in range(n_o)]
        for load in loads:
            load.start()
        waited = set()
        sent = set()

        def get(i):
            if i not in waited:
                waited.add(i)
                loads[i].wait()
            return i_ref[i]

        def put(i, *where):
            sent.add(i)
            if where:
                pltpu.make_async_copy(o_ref[i].at[where], o_to[i].at[where], o_sem.at[i]).start()
            else:
                stores[i].start()

        body(s_refs, get, o_ref, put, x_refs)
        for i in range(n_i):
            get(i)
        for i in range(n_o):
            if i not in sent:
                put(i)
        for store in stores:
            store.wait()

    return pl.pallas_call(
        kernel,
        out_shape=list(outs),
        in_specs=[SMEM] * n_s + [ANY] * (n_a + len(deps)),
        out_specs=[ANY] * n_o,
        scratch_shapes=list(scratch)
        + [pltpu.VMEM(shape, x.dtype) for shape, (x, _, _) in zip(shapes, parts)]
        + [pltpu.VMEM(x.shape, x.dtype) for x in outs]
        + [pltpu.SemaphoreType.DMA((n_i,)), pltpu.SemaphoreType.DMA((n_o,))],
        compiler_params=params(),
        cost_estimate=estimate,
        name=name,
    )(*scalars, *arrays, *deps)


def shaped(shape, dtype=BF):
    return jax.ShapeDtypeStruct(shape, dtype)


def forward_step(last, ids, distances, toks, gain, shift, w, qb, vb, state, through, deps=()):
    first = state is None
    count = len(toks)
    rows, width = toks[0].shape
    block = shaped((rows, width))
    outs = [shaped((8, 2 * rows), F32), shaped((8, 2 * rows), F32), shaped((width, rows), F32)]
    outs += [block, block, block] * count
    full = slice(0, width)
    ins = [toks[0], gain, shift, vb, (w, full, slice(width, 2 * width)), (w, full, slice(2 * width, 3 * width))]
    if first:
        ins += [(w, full, full), qb]
        outs += [block, shaped((width, rows)), block]
    else:
        ins += list(state)
    at_tok = len(ins) - 1
    ins += toks[1:]
    if first:
        ins.append(through)

    def body(scalars, get, out, put, scratch):
        m_out, l_out, acc_out = out[:3]
        ones_row = (lax.broadcasted_iota(jnp.int32, (128, 2 * rows), 0) == 0).astype(BF)
        for i in range(count):
            h_out, k_out, v_out = out[3 + 3 * i : 6 + 3 * i]
            normed, _ = normalize(get(at_tok + i if i > 0 else 0)[...].astype(F32))
            hidden = (normed * as_row(get(1)) + as_row(get(2))).astype(BF)
            h_out[...] = hidden
            put(3 + 3 * i)
            k_out[...] = dot(hidden, get(4)[...]).astype(BF)
            put(4 + 3 * i)
            values = dot(hidden, get(5)[...]) + as_row(get(3))
            v_out[...] = values.astype(BF)
            put(5 + 3 * i)
            values_t = v_out[...].astype(F32).T.astype(BF)
            if first:
                at = 3 + 3 * count
                q_out, qt_out, through_out = out[at:]
                if i == 0:
                    q_out[...] = (dot(hidden, get(6)[...]) + as_row(get(7))).astype(BF)
                    put(at)
                    qt_out[...] = q_out[...].astype(F32).T.astype(BF)
                    put(at + 1)
                if i == count - 1:
                    through_out[...] = get(len(ins) - 1)[...]
                    put(at + 2)
                qt_ref = qt_out
            else:
                qt_ref = get(6)
            extra_keys = extra_lanes(scalars[0], distances[i], rows, 0)
            start = first and i == 0
            end = last and i == count - 1
            for pair in range(PAIRS):
                lanes = pair_lanes(pair)
                this = slice(pair, pair + 1)
                keys = jnp.concatenate([k_out[:, lanes], extra_keys], 1)
                scores = dot(keys, two_heads(qt_ref[lanes, :], ones_row))
                top = jnp.max(scores, 0, keepdims=True)
                if not start:
                    m_ref, l_ref, acc_ref = (get(7 + j) for j in range(3)) if i == 0 else (m_out, l_out, acc_out)
                    before = m_ref[this, :]
                    top = jnp.maximum(top, before)
                    fade = jnp.exp2((before - top) * TO_EXP2)
                weights = jnp.exp2((scores - top) * TO_EXP2)
                total = jnp.sum(weights, 0, keepdims=True)
                if not start:
                    total = total + l_ref[this, :] * fade
                both = dot(values_t[lanes, :], weights.astype(BF))
                for head in range(2):
                    own = slice(lanes.start + head * HD, lanes.start + (head + 1) * HD)
                    cols = slice(head * rows, (head + 1) * rows)
                    part = both[head * HD : (head + 1) * HD, cols]
                    if not start:
                        part = part + acc_ref[own, :] * fade[:, cols]
                    if end:
                        part = part / total[:, cols]
                    acc_out[own, :] = part
                m_out[this, :] = -(top + jnp.log2(total) * (1.0 / TO_EXP2)) if end else top
                l_out[this, :] = total
                if i == count - 1:
                    put(2, lanes)

    estimate = pl.CostEstimate(flops=count * 10**10, bytes_accessed=24 * 2**20, transcendentals=0)
    return staged(body, "attend", [ids], ins, outs, estimate, deps=deps)


def make_perm(ref, me, blocks, firsts, size, block):
    here = lax.broadcasted_iota(jnp.int32, (size, ref.shape[1]), 0)
    there = lax.broadcasted_iota(jnp.int32, (size, ref.shape[1]), 1)
    for i, (relative, first) in enumerate(zip(blocks, firsts)):
        start = (me ^ relative) * block + first
        ref[i * size : (i + 1) * size, :] = (here + start == there).astype(F32).astype(BF)


def middle_step(ids, places, tok, cot, attt, wo, ob, gain, shift, up, ub, down, db, perm):
    rows, width = tok.shape
    hidden = up.shape[1]
    chunks = 8
    chunk = hidden // chunks
    half = width // 2
    given = not isinstance(perm, tuple)
    ins = [attt, wo, ob, tok, gain, shift, up, ub, cot, down, db] + ([perm] if given else [])
    outs = [
        shaped((rows, width)),
        shaped((hidden // 2, width)),
        shaped((hidden // 2, width)),
        shaped((half, hidden + width)),
        shaped((half, hidden + width)),
        shaped((rows, width)),
        shaped((width, rows)),
        shaped((8, 2 * rows), F32),
        shaped((rows, width), F32),
        shaped((8, width), F32),
        shaped((8, chunk), F32),
    ]
    scratch = [
        pltpu.VMEM((rows, width), F32),
        pltpu.VMEM((rows, width), F32),
        pltpu.VMEM((rows, width), BF),
        pltpu.VMEM((width, rows), BF),
        pltpu.VMEM((rows, width), BF),
        pltpu.VMEM((rows, width), F32),
        pltpu.VMEM((rows, width), F32),
        pltpu.VMEM((width, width), BF),
        pltpu.VMEM((chunks, chunk), F32),
    ]

    def body(scalars, get, out, put, scratch):
        (ids_ref,) = scalars
        block_out, down_keep, down_send, up_keep, up_send, da_out, dat_out, negd_out, gmid_out, vec_out, ubg_out = out
        mid_ref, norm_ref, h2_ref, h2t_ref, att_ref, res_ref, gh_ref, perm_ref = scratch[:8]
        if given:
            perm_ref[...] = get(11)[...]
        else:
            make_perm(perm_ref, ids_ref[0], *perm)
        attt_ref = get(0)
        att_ref[...] = attt_ref[...].T.astype(BF)
        projected = dot(att_ref[...], get(1)[...]) + as_row(get(2))
        middle = get(3)[...].astype(F32) + projected
        mid_ref[...] = middle
        normed, inverse = normalize(middle)
        norm_ref[...] = normed
        h2_ref[...] = (normed * as_row(get(4)) + as_row(get(5))).astype(BF)
        h2t_ref[...] = dot_nt(perm_ref[...], h2_ref[...]).astype(BF)
        up_ref, cot_ref, down_ref = get(6), get(8), get(9)
        ub_ref = scratch[8]
        for i in range(chunks):
            ub_ref[i : i + 1, :] = get(7)[i * chunk : (i + 1) * chunk].reshape(1, chunk)
        for turn in range(chunks // 2):
            p = (2 * turn + chunks // 2) % chunks
            own = [p, p + 1] if places is None else [places[p] ^ ids_ref[0], places[p + 1] ^ ids_ref[0]]
            at = [pl.ds(pl.multiple_of(place * chunk, 128), chunk) for place in own]
            up_c = jnp.concatenate([up_ref[:, a] for a in at], 1)
            down_c = jnp.concatenate([down_ref[a, :] for a in at], 0)
            bias = jnp.concatenate([ub_ref[pl.ds(place, 1), :] for place in own], 1)
            before = dot(h2_ref[...], up_c) + bias
            cdf = 0.5 * (1.0 + lax.erf(before * math.sqrt(0.5)))
            slope = cdf + before * (jnp.exp(-0.5 * before * before) * (1.0 / math.sqrt(2.0 * math.pi)))
            lifted = (before * cdf).astype(BF)
            grad_lifted = dot_nt(cot_ref[...], down_c)
            grad_down = dot_tn(lifted, cot_ref[...]).astype(BF)
            to, first = (down_keep, p) if p < chunks // 2 else (down_send, p - chunks // 2)
            rows_to = pl.ds(first * chunk, 2 * chunk)
            to[rows_to, :] = grad_down
            put(1 if p < chunks // 2 else 2, rows_to)
            grad_before = (grad_lifted * slope).astype(BF)
            bias_grad = jnp.sum(grad_before.astype(F32), 0, keepdims=True)
            for i, place in enumerate(own):
                ubg_out[pl.ds(place, 1), :] = bias_grad[:, i * chunk : (i + 1) * chunk]
            grad_up = dot(h2t_ref[...], grad_before).astype(BF)
            for i, a in enumerate(at):
                cols = slice(i * chunk, (i + 1) * chunk)
                up_keep[:, a] = grad_up[:half, cols]
                up_send[:, a] = grad_up[half:, cols]
                put(3, slice(None), a)
                put(4, slice(None), a)
            part = dot(lifted, down_c)
            back = dot_nt(grad_before, up_c)
            if turn == 0:
                res_ref[...] = part
                gh_ref[...] = back
            else:
                res_ref[...] += part
                gh_ref[...] += back
        block_out[...] = (mid_ref[...] + (res_ref[...] + as_row(get(10)))).astype(BF)
        put(0)
        cot32 = cot_ref[...].astype(F32)
        grad = gh_ref[...]
        normed = norm_ref[...]
        vec_out[0:1, :] = jnp.sum(cot32, 0, keepdims=True)
        vec_out[1:2, :] = jnp.sum(grad * normed, 0, keepdims=True)
        vec_out[2:3, :] = jnp.sum(grad, 0, keepdims=True)
        scaled = grad * as_row(get(4))
        grad_middle = cot32 + inverse * (
            scaled
            - jnp.mean(scaled, -1, keepdims=True)
            - normed * jnp.mean(scaled * normed, -1, keepdims=True)
        )
        gmid_out[...] = grad_middle
        put(8)
        branch = grad_middle.astype(BF)
        vec_out[3:4, :] = jnp.sum(branch.astype(F32), 0, keepdims=True)
        vec_out[4:8, :] = jnp.zeros((4, width), F32)
        att_t = dot_nt(perm_ref[...], att_ref[...]).astype(BF)
        grad_out = dot(att_t, branch).astype(BF)
        cols = pl.ds(hidden, width)
        up_keep[:, cols] = grad_out[:half]
        up_send[:, cols] = grad_out[half:]
        put(3, slice(None), cols)
        put(4, slice(None), cols)
        grad_att = dot_nt(branch, get(1)[...]).astype(BF)
        da_out[...] = grad_att
        put(5)
        grad_att_t = grad_att.astype(F32).T
        dat_out[...] = grad_att_t.astype(BF)
        put(6)
        product = grad_att_t * attt_ref[...]
        for head in range(HEADS):
            spread = jnp.sum(product[head * HD : (head + 1) * HD], 0, keepdims=True)
            place = slice((head % 2) * rows, (head % 2 + 1) * rows)
            negd_out[head // 2 : head // 2 + 1, place] = -spread

    estimate = cost(12 * rows * width * hidden + 6 * rows * width * width, 30 * 2**20, 0)
    return staged(body, "middle", [ids], ins, outs, estimate, scratch)


def three_parts(row):
    high = row.astype(BF)
    rest = row - high.astype(F32)
    mid = rest.astype(BF)
    low = (rest - mid.astype(F32)).astype(BF)
    return high.astype(F32), mid.astype(F32), low.astype(F32)


def extra_rows(row, with_mask):
    n = row.shape[1]
    high, mid, low = three_parts(row)
    place = lax.broadcasted_iota(jnp.int32, (128, n), 0)
    out = jnp.where(place == 0, 1.0 if with_mask else 0.0, 0.0)
    out = jnp.where(place == 1, high, out)
    out = jnp.where(place == 2, mid, out)
    out = jnp.where(place == 3, low, out)
    return out.astype(BF)


def backward_step(ids, distances, q, qt, da, dat, negl, negd, keys, values, toks, w, state, last, deps, arrived=None, through=None):
    rows, width = q.shape
    blocks = len(keys)
    first = state is None
    ins = [qt, negl, dat, negd, q, da]
    for k, v in zip(keys, values):
        ins += [k, v]
    base_w = len(ins)
    ins += [w, *toks]
    base_state = len(ins)
    if not first:
        ins += list(state)
    at_extra = len(ins)
    ins += [x for x in (arrived, through) if x is not None]
    outs = []
    for i in range(blocks):
        outs += [shaped((rows, 2 * width)), shaped((rows, width), F32 if last and i == blocks - 1 else BF)]
    outs += [shaped((8, width), F32), shaped((rows, width)) if last else shaped((width, rows), F32)]
    if through is not None:
        outs.append(shaped(through.shape, through.dtype))

    def body(scalars, get, out, put, scratch):
        (dqt,) = scratch
        vec_out, end_out = out[2 * blocks : 2 * blocks + 2]
        lane = lax.broadcasted_iota(jnp.int32, (rows, 128), 1)
        zero = jnp.zeros((rows, 128), BF)
        value_bias = gain = shift = jnp.zeros((1, width), F32)
        query_bias = jnp.zeros((1, width), F32)
        for i in range(blocks):
            dkv_out, g_out = out[2 * i], out[2 * i + 1]
            extra_keys = extra_lanes(scalars[0], distances[i], rows, 3)
            qt_ref, negl_ref, dat_ref, negd_ref = get(0), get(1), get(2), get(3)
            k_ref, v_ref = get(6 + 2 * i), get(7 + 2 * i)
            keys_t = k_ref[...].astype(F32).T.astype(BF)
            for pair in range(PAIRS):
                lanes = pair_lanes(pair)
                key = jnp.concatenate([k_ref[:, lanes], extra_keys], 1)
                scores = dot(key, two_heads(qt_ref[lanes, :], extra_rows(negl_ref[pair : pair + 1, :], True)))
                softmaxed = jnp.exp2(scores * TO_EXP2)
                value = jnp.concatenate([v_ref[:, lanes], extra_keys], 1)
                centred = dot(value, two_heads(dat_ref[lanes, :], extra_rows(negd_ref[pair : pair + 1, :], False)))
                grad_scores = (softmaxed * centred).astype(BF)
                weights = softmaxed.astype(BF)
                q_pair = get(4)[:, lanes]
                da_pair = get(5)[:, lanes]
                q_both = jnp.concatenate([jnp.where(lane < HD, q_pair, zero), jnp.where(lane < HD, zero, q_pair)], 0)
                da_both = jnp.concatenate([jnp.where(lane < HD, da_pair, zero), jnp.where(lane < HD, zero, da_pair)], 0)
                dkv_out[:, lanes] = (dot(grad_scores, q_both) * SCALE).astype(BF)
                dkv_out[:, slice(width + lanes.start, width + lanes.stop)] = dot(weights, da_both).astype(BF)
                both = dot(keys_t[lanes, :], grad_scores)
                for head in range(2):
                    own = slice(lanes.start + head * HD, lanes.start + (head + 1) * HD)
                    part = both[head * HD : (head + 1) * HD, head * rows : (head + 1) * rows]
                    if i > 0:
                        part = part + dqt[own, :]
                    elif not first:
                        part = part + get(base_state)[own, :]
                    dqt[own, :] = part
            put(2 * i)
            w_ref = get(base_w)
            grad = dot_nt(dkv_out[...], w_ref[:, width:])
            if last and i == blocks - 1:
                dq = (dqt[...].T * SCALE).astype(BF)
                end_out[...] = dq
                put(2 * blocks + 1)
                query_bias = jnp.sum(dq.astype(F32), 0, keepdims=True)
                grad = grad + dot_nt(dq, w_ref[:, :width])
            if arrived is not None and i == 0:
                g_out[...] = (grad + get(at_extra)[...].astype(F32)).astype(g_out.dtype)
            else:
                g_out[...] = grad.astype(g_out.dtype)
            put(2 * i + 1)
            normed, _ = normalize(get(base_w + 1 + i)[...].astype(F32))
            value_bias = value_bias + jnp.sum(dkv_out[:, width:].astype(F32), 0, keepdims=True)
            gain = gain + jnp.sum(grad * normed, 0, keepdims=True)
            shift = shift + jnp.sum(grad, 0, keepdims=True)
        if not last:
            end_out[...] = dqt[...]
        if through is not None:
            out[2 * blocks + 2][...] = get(len(ins) - 1)[...]
        if not first:
            vec_ref = get(base_state + 1)
            value_bias = value_bias + vec_ref[1:2, :]
            gain = gain + vec_ref[2:3, :]
            shift = shift + vec_ref[3:4, :]
        vec_out[0:1, :] = query_bias
        vec_out[1:2, :] = value_bias
        vec_out[2:3, :] = gain
        vec_out[3:4, :] = shift
        vec_out[4:8, :] = jnp.zeros((4, width), F32)

    flops = blocks * (2 * rows * width * width * 3 + 10 * rows * rows * width * 4)
    estimate = cost(flops, 20 * 2**20, blocks * HEADS * rows * rows)
    return staged(
        body, "attend_back", [ids], ins, outs, estimate, [pltpu.VMEM((width, rows), F32)], deps
    )


def projection_step(ids, perm, dq, hiddens, dkvs, vec_mid, vec_up, vec_back, deps):
    rows, width = dq.shape
    count = len(hiddens)
    part = width // 4
    given = not isinstance(perm, tuple)
    ins = [*hiddens, dq, vec_mid, vec_up, vec_back, *dkvs] + ([perm] if given else [])
    outs = [shaped((n, 3 * width)) for n in (part, part, part + 16, part)] + [shaped((8, 3 * width), F32)]
    at = count

    def body(scalars, get, out, put, scratch):
        ht_ref, perm_ref = scratch
        if given:
            perm_ref[...] = get(len(ins) - 1)[...]
        else:
            make_perm(perm_ref, scalars[0][0], *perm)
        keep_a, keep_b, send_a, send_b, vec_ref = out
        for i in range(count):
            ht_ref[:, i * rows : (i + 1) * rows] = dot_nt(perm_ref[...], get(i)[...]).astype(BF)
        vec_ref[0:4, :width] = get(at + 1)[0:4, :]
        vec_ref[0:4, width : 2 * width] = get(at + 3)[0:4, :]
        up = jnp.concatenate([get(at + 2)[i : i + 1, :] for i in range(get(at + 2).shape[0])], 1)
        for i in range(4):
            vec_ref[i : i + 1, 2 * width :] = up[:, i * width : (i + 1) * width]
        vec_ref[4:8, :] = jnp.zeros((4, 3 * width), F32)
        send_a[part:, :] = split_high(vec_ref[...])
        put(4)
        for third in range(3):
            if third == 0:
                grad = dot(ht_ref[:, :rows], get(at)[...])
            else:
                own = slice((third - 1) * width, third * width)
                grad = dot(ht_ref[...], jnp.concatenate([get(at + 4 + i)[:, own] for i in range(count)], 0))
            grad = grad.astype(BF)
            cols = pl.ds(third * width, width)
            send_a[:part, cols] = grad[2 * part : 3 * part]
            put(2, slice(None), cols)
            send_b[:, cols] = grad[3 * part :]
            put(3, slice(None), cols)
            keep_a[:, cols] = grad[:part]
            put(0, slice(None), cols)
            keep_b[:, cols] = grad[part : 2 * part]
            put(1, slice(None), cols)

    estimate = cost(2 * rows * width * width * (1 + 2 * count), 12 * 2**20, 0)
    return staged(
        body,
        "projection_grad",
        [ids],
        ins,
        outs,
        estimate,
        [pltpu.VMEM((width, count * rows), BF), pltpu.VMEM((width, width), BF)],
        deps,
    )


def final_step(tok, gain, gmid, g, pieces, block_out, deps=()):
    def body(scalars, get, out, put, scratch):
        normed, inverse = normalize(get(0)[...].astype(F32))
        total = get(3)[...]
        for i in range(len(pieces)):
            total = total + get(4 + i)[...].astype(F32)
        scaled = total * as_row(get(1))
        out[0][...] = (
            get(2)[...]
            + inverse
            * (
                scaled
                - jnp.mean(scaled, -1, keepdims=True)
                - normed * jnp.mean(scaled * normed, -1, keepdims=True)
            )
        ).astype(BF)
        put(0)
        out[1][...] = get(len(ins) - 1)[...]

    estimate = pl.CostEstimate(flops=10**11, transcendentals=0, bytes_accessed=10**8)
    ins = [tok, gain, gmid, g, *pieces, block_out]
    return staged(body, "norm_back", [], ins, [shaped(tok.shape)] * 2, estimate, deps=deps)


def flip(count, distance):
    return [(i, i ^ distance) for i in range(count)]


def tree_place(bits):
    n = len(bits)
    return np.array([sum(((p >> (n - 1 - i)) & 1) << bit for i, bit in enumerate(bits)) for p in range(1 << n)])


def split_high(values):
    high = values.astype(BF)
    return jnp.concatenate([high.astype(F32), values - high.astype(F32)], 0).astype(BF)


def joined(both):
    both = both.astype(F32)
    return both[:8] + both[8:]


class Part:
    def __init__(self, keep, recv):
        self.terms, self.rows, self.cols = [keep, recv], keep.shape[0], keep.shape[1]

    def inputs(self, start):
        return [(x, slice(start, self.rows), slice(0, self.cols)) for x in self.terms]

    def total(self):
        return sum(x[: self.rows].astype(F32) for x in self.terms)


def add_up(refs):
    total = refs[0][...].astype(F32)
    for ref in refs[1:]:
        total = total + ref[...].astype(F32)
    return total


def halve(parts, name, vectors=None, deps=(), through=None):
    halves = [p.rows // 2 for p in parts]
    if any(h % 16 for h in halves):
        sends = [p.total()[h:].astype(BF) for p, h in zip(parts, halves)]
        if vectors is not None:
            vectors = vectors + joined(parts[0].terms[-1][parts[0].rows :])
            sends[0] = jnp.concatenate([sends[0], split_high(vectors)], 0)
        vectors = through if vectors is None else vectors
    else:
        ins, counts = [], []
        for p, h in zip(parts, halves):
            ins += p.inputs(h)
            counts.append(len(p.terms))
        outs = [shaped((h, p.cols)) for p, h in zip(parts, halves)]
        if vectors is not None:
            sent, rows = parts[0].terms[-1], parts[0].rows
            ins += [vectors, (sent, slice(rows, rows + 16), slice(0, parts[0].cols))]
            outs[0] = shaped((halves[0] + 16, parts[0].cols))
            outs.append(shaped(vectors.shape, F32))
        if through is not None:
            ins.append(through)
            outs.append(shaped(through.shape, through.dtype))

        def body(scalars, get, out, put, scratch):
            at = 0
            for i, (n, h) in enumerate(zip(counts, halves)):
                out[i][:h, :] = add_up([get(at + j) for j in range(n)]).astype(BF)
                at += n
                if vectors is not None and i == 0:
                    total = get(len(ins) - 2)[...] + joined(get(len(ins) - 1)[...])
                    out[len(outs) - 1][...] = total
                    out[0][h:, :] = split_high(total)
                put(i)
            if through is not None:
                out[len(outs) - 1][...] = get(len(ins) - 1)[...]

        size = sum(h * p.cols for p, h in zip(parts, halves))
        made = staged(body, name, [], ins, outs, cost(size, 6 * size), deps=deps)
        sends = made[: len(parts)]
        vectors = made[-1] if len(made) > len(parts) else None
    for p, h in zip(parts, halves):
        p.rows = h
    return sends, vectors


def pack(me, parts, columns, count, name, vectors=None, deps=()):
    rows = min(p.rows for p in parts)
    widths = [c[2] // count for c in columns]
    ahead = 0 if vectors is None else 16 * vectors.shape[1] // (2 * rows)
    wide = ahead + sum(parts[c[0]].rows // rows * w for c, w in zip(columns, widths))
    ins, counts = [], []
    for p in parts:
        ins += p.inputs(0)
        counts.append(len(p.terms))
    outs = [shaped((2 * rows, wide)), shaped((2 * rows, wide), F32)]
    if vectors is not None:
        sent = parts[0].terms[-1]
        ins += [vectors, (sent, slice(parts[0].rows, parts[0].rows + 16), slice(0, parts[0].cols))]
        outs.append(shaped(vectors.shape, F32))

    def body(scalars, get, out, put, scratch):
        (me_ref,) = scalars
        sums, at = [], 0
        for n in counts:
            sums.append(add_up([get(at + j) for j in range(n)]))
            at += n
        if vectors is not None:
            vec = get(len(ins) - 2)[...] + joined(get(len(ins) - 1)[...])
            out[2][...] = vec
            put(2)
            store_vectors(out[0], vec, 2 * rows, ahead)
        for place, (ref, turn) in enumerate([(out[0], 0), (out[0], 1), (out[1], 0), (out[1], 1)]):
            distance = (1, 3, 0, 2)[place]
            for owner in range(count):

                @pl.when((me_ref[0] ^ distance) == owner)
                def _(ref=ref, owner=owner, turn=turn):
                    at = ahead
                    for (which, start, _), w in zip(columns, widths):
                        piece = sums[which][:, start + owner * w : start + (owner + 1) * w].astype(ref.dtype)
                        for j in range(piece.shape[0] // rows):
                            ref[turn * rows : (turn + 1) * rows, at : at + w] = piece[j * rows : (j + 1) * rows]
                            at += w

            if turn == 1:
                put(place // 2)

    size = sum(p.rows * p.cols for p in parts)
    long = pl.CostEstimate(flops=10**11, transcendentals=0, bytes_accessed=10**8)
    estimate = cost(2 * size, 6 * size) if vectors is not None else long
    return staged(body, name, [me], ins, outs, estimate, deps=deps)


def store_vectors(ref, vec, rows, ahead):
    both = split_high(vec)
    for i in range(rows // 16):
        ref[16 * i : 16 * (i + 1), :ahead] = both[:, i * ahead : (i + 1) * ahead]


def load_vectors(ref, rows, ahead):
    return joined(jnp.concatenate([ref[16 * i : 16 * (i + 1), :ahead] for i in range(rows // 16)], 1))


def pack_far(own, recv, name, vectors=None, deps=()):
    rows, wide = own.shape[0] // 2, own.shape[1]
    before = 0 if vectors is None else 16 * vectors.shape[1] // (2 * rows)
    ahead = 2 * before
    far = slice(rows, 2 * rows)
    ins = [(own, far, slice(0, wide)), (recv, far, slice(0, wide))]
    outs = [shaped((rows, wide + before))]
    if vectors is not None:
        ins += [vectors, (recv, slice(0, 2 * rows), slice(0, before))]
        outs.append(shaped(vectors.shape, F32))

    def body(scalars, get, out, put, scratch):
        out[0][:, ahead:] = (get(0)[:, before:] + get(1)[:, before:].astype(F32)).astype(BF)
        if vectors is not None:
            vec = get(2)[...] + load_vectors(get(3), 2 * rows, before)
            out[1][...] = vec
            store_vectors(out[0], vec, rows, ahead)

    size = rows * wide
    return staged(body, name, [], ins, outs, cost(size, 10 * size), deps=deps)


def narrow(vec):
    half = vec.shape[1] // 2
    return jnp.concatenate([vec[:4, :half], vec[:4, half:]], 0)


def pack_all(me, parts, columns, count, name, vectors, deps=()):
    rows = min(p.rows for p in parts)
    widths = [c[2] // count for c in columns]
    ahead = 8 * vectors.shape[1] // rows
    wide = ahead + sum(parts[c[0]].rows // rows * w for c, w in zip(columns, widths))
    ins, counts = [], []
    for p in parts:
        ins += p.inputs(0)
        counts.append(len(p.terms))
    sent = parts[0].terms[-1]
    ins += [vectors, (sent, slice(parts[0].rows, parts[0].rows + 16), slice(0, parts[0].cols))]
    outs = [shaped((rows, wide))] * (count - 1) + [shaped((rows, wide), F32), shaped(vectors.shape, F32)]

    def body(scalars, get, out, put, scratch):
        (me_ref,) = scalars
        sums, at = [], 0
        for n in counts:
            sums.append(add_up([get(at + j) for j in range(n)]))
            at += n
        vec = get(len(ins) - 2)[...] + joined(get(len(ins) - 1)[...])
        out[count][...] = vec
        put(count)
        for distance in (2, 3, 1, 0):
            ref = out[(distance - 1) % count]
            if distance:
                store_vectors(ref, narrow(vec), rows, ahead)
            for owner in range(count):

                @pl.when((me_ref[0] ^ distance) == owner)
                def _(ref=ref, owner=owner):
                    at = ahead
                    for (which, start, _), w in zip(columns, widths):
                        piece = sums[which][:, start + owner * w : start + (owner + 1) * w].astype(ref.dtype)
                        for j in range(piece.shape[0] // rows):
                            ref[:, at : at + w] = piece[j * rows : (j + 1) * rows]
                            at += w

            put((distance - 1) % count)

    size = sum(p.rows * p.cols for p in parts)
    made = staged(body, name, [me], ins, outs, cost(2 * size, 6 * size), deps=deps)
    return made[: count - 1], made[count - 1], made[count]


def unpack_all(own, messages, shape, name, vectors, deps=()):
    rows, wide = own.shape
    ahead = 8 * vectors.shape[1] // rows
    width = vectors.shape[1] // 3
    ins = [own, *messages, vectors]
    outs = [shaped(shape, F32)] + [shaped((width,), F32)] * 8 + [shaped((4 * width,), F32)]

    def body(scalars, get, out, put, scratch):
        total = get(0)[:, ahead:]
        both = jnp.zeros((8, vectors.shape[1] // 2), F32)
        for i in range(len(messages)):
            total = total + get(1 + i)[:, ahead:].astype(F32)
            both = both + load_vectors(get(1 + i), rows, ahead)
        for j in range(shape[0] // rows):
            out[0][j * rows : (j + 1) * rows, :] = total[:, j * shape[1] : (j + 1) * shape[1]]
        put(0)
        vec = get(1 + len(messages))[0:4, :] + jnp.concatenate([both[:4], both[4:]], 1)
        for i in range(2):
            for j in range(4):
                out[1 + 4 * i + j][...] = vec[j : j + 1, i * width : (i + 1) * width].reshape(width)
        for j in range(4):
            out[9][j * width : (j + 1) * width] = vec[j : j + 1, 2 * width :].reshape(width)

    return staged(body, name, [], ins, outs, cost(rows * wide, 20 * rows * wide), deps=deps)


def unpack(own, near, far, shapes, name, vectors=None, deps=(), tall=None, through=None):
    rows, wide = far.shape[0], own.shape[1]
    this, all_cols = slice(0, rows), slice(0, wide)
    ins = [(own, this, all_cols), (near, this, all_cols), far]
    outs = [shaped(shape[::-1] if i == tall else shape, F32) for i, shape in enumerate(shapes)]
    ahead = 0
    if through is not None:
        ins.append(through)
        outs.append(shaped(through.shape, F32))
    if vectors is not None:
        ahead = 16 * vectors.shape[1] // rows
        width = vectors.shape[1] // 3
        ins.append(vectors)
        outs += [shaped((width,), F32)] * 8 + [shaped((4 * width,), F32)]

    def body(scalars, get, out, put, scratch):
        before = ahead // 2
        total = get(0)[:, before:] + get(1)[:, before:].astype(F32) + get(2)[:, ahead:].astype(F32)
        at = 0
        for i, (height, width) in enumerate(shapes):
            if i == tall:
                turns = range(height // rows)
                whole = jnp.concatenate([total[:, at + j * width : at + (j + 1) * width] for j in turns], 0)
                out[i][...] = whole.T
                at += len(turns) * width
            else:
                for j in range(height // rows):
                    out[i][j * rows : (j + 1) * rows, :] = total[:, at : at + width]
                    at += width
            put(i)
        if through is not None:
            out[len(shapes)][...] = get(3)[...].astype(F32)
        if vectors is not None:
            vec = get(3)[...] + load_vectors(get(2), rows, ahead)
            wide = vec.shape[1] // 3
            base = len(shapes)
            for i in range(2):
                for j in range(4):
                    out[base + 4 * i + j][...] = vec[j : j + 1, i * wide : (i + 1) * wide].reshape(wide)
            for j in range(4):
                out[base + 8][j * wide : (j + 1) * wide] = vec[j : j + 1, 2 * wide :].reshape(wide)

    size = rows * wide
    return staged(body, name, [], ins, outs, cost(size, 12 * size), deps=deps)


def spec_sum(part, me, count):
    cols = part.shape[1] // count

    def mine(distance):
        return lax.dynamic_slice_in_dim(part, (me ^ distance) * cols, cols, 1)

    got = [lax.ppermute(mine(d).astype(BF), "spec", flip(count, d)) for d in range(1, count)]
    total = mine(0)
    for piece in got:
        total = total + piece.astype(F32)
    return total


def local(
    tokens,
    cotangent,
    lengths,
    projection,
    query_bias,
    value_bias,
    output_weight,
    output_bias,
    up_weight,
    up_bias,
    down_weight,
    down_bias,
    first_gain,
    first_shift,
    second_gain,
    second_shift,
):
    _, rows, width = tokens.shape
    hidden = up_weight.shape[1]
    cubes, count = lax.axis_size("cube"), lax.axis_size("spec")
    cube, spec = lax.axis_index("cube"), lax.axis_index("spec")
    tok = tokens.reshape(rows, width)
    cot = cotangent.reshape(rows, width)

    assert count == 4
    half_way = count // 2

    def partner(c, s):
        return (c ^ 1, s ^ half_way) if (c & 1) != (s // half_way) else (c, s)

    places = [(c, s) for c in range(cubes) for s in range(count)]

    def both_axes(move):
        return [(c * count + s, move(c, s)[0] * count + move(c, s)[1]) for c, s in places]

    exchange = both_axes(partner)
    pair = flip(cubes, 1)
    near = flip(count, 1)
    axes = ("cube", "spec")

    own_tok = tok
    tok = lax.ppermute(own_tok, axes, exchange)
    away = (cube & 1) != (spec // half_way)
    others = lax.ppermute(jnp.broadcast_to(lengths[:1], (256, 1024)), "cube", pair)
    length = jnp.where(away, others[0, 0], lengths[0]).astype(jnp.int32)
    my_block = jnp.where(away, spec ^ half_way, spec).astype(jnp.int32)
    next_tok = lax.ppermute(tok, "spec", near)
    blocks = [tok, lax.ppermute(tok, "cube", pair), next_tok, lax.ppermute(next_tok, "cube", pair)]
    distances = [0, half_way, 1, half_way + 1]
    ids = jnp.stack([cube.astype(jnp.int32), my_block, length])

    bits = cubes.bit_length() - 1
    order_a = list(range(bits))
    order_b = [0] + list(range(bits - 1, 0, -1))
    place_a, place_b = tree_place(order_a), tree_place(order_b)
    split = cubes // 2

    def source_rows(place, offset, size, block):
        start = (jnp.asarray(place, jnp.int32) ^ cube) * block + offset
        return (start[:, None] + jnp.arange(size, dtype=jnp.int32)[None, :]).reshape(-1)

    def one_hot(source):
        return (source[:, None] == jnp.arange(width, dtype=jnp.int32)[None, :]).astype(BF)

    block = width // cubes
    part = block // 2
    chunks = 8
    lists = [list(map(int, place)) for place in (place_a, place_b)]
    perm_b = (lists[1], [0] * cubes, block, block)
    perm_mixed = (
        lists[0][:split] + lists[1][:split] + lists[0][split:] + lists[1][split:],
        ([0] * split + [part] * split) * 2,
        part,
        block,
    )
    if part % 16:
        perm_b, perm_mixed = (
            one_hot(jnp.concatenate([source_rows([r], f, size, block) for r, f in zip(relative, first)]))
            for relative, first, size, _ in (perm_b, perm_mixed)
        )
    places = lists[0] if cubes == chunks else None

    hiddens, keys, values = [], [], []
    state = None
    for which in ((0, 1), (2,), (3,)):
        made = forward_step(
            which[-1] == count - 1,
            ids,
            [distances[i] for i in which],
            [blocks[i] for i in which],
            first_gain,
            first_shift,
            projection,
            query_bias,
            value_bias,
            state,
            cot,
        )
        for i in range(len(which)):
            hiddens.append(made[3 + 3 * i])
            keys.append(made[4 + 3 * i])
            values.append(made[5 + 3 * i])
        if state is None:
            q, qt, cot = made[3 + 3 * len(which) :]
            cot = lax.ppermute(cot, axes, exchange)
        state = (qt,) + tuple(made[:3])
    negl, attt = state[1], state[3]

    (
        block_out,
        down_keep,
        down_send,
        up_keep,
        up_send,
        da,
        dat,
        negd,
        gmid,
        vec_mid,
        grad_up_bias,
    ) = middle_step(
        ids,
        places,
        tok,
        cot,
        attt,
        output_weight,
        output_bias,
        second_gain,
        second_shift,
        up_weight,
        up_bias,
        down_weight,
        down_bias,
        perm_b,
    )
    if cubes != chunks:
        whole = jnp.concatenate([down_keep, down_send], 0).reshape(cubes, hidden // cubes, width)
        whole = jnp.take(whole, jnp.asarray(place_a, jnp.int32) ^ cube, axis=0)
        down_keep = whole[:split].reshape(hidden // 2, width)
        down_send = whole[split:].reshape(hidden // 2, width)

    down_recv = lax.ppermute(down_send, "cube", pair)
    up_recv = lax.ppermute(up_send, "cube", pair)

    common = (q, qt, da, dat, negl, negd)

    def back(which, state, last, deps, arrived=None, through=None):
        def pick(things):
            return [things[i] for i in which]

        some = (pick(keys), pick(values), pick(blocks))
        return backward_step(
            ids, pick(distances), *common, *some, projection, state, last, deps, arrived, through
        )

    dkv_3, g_3, vec_back, dqt, block_out = back((3,), None, False, (), None, block_out)
    block_out = lax.ppermute(block_out, axes, exchange)
    g_3 = lax.ppermute(g_3, "cube", pair)

    def hop(parts, sends, level):
        for p, send, order in zip(parts, sends, (order_a, order_b)):
            p.terms.append(lax.ppermute(send, "cube", flip(cubes, 1 << order[level])))

    levels = len(order_a)
    me = spec.astype(jnp.int32).reshape(1)
    ff = [Part(down_keep, down_recv), Part(up_keep, up_recv)]
    last = dqt
    if levels > 1:
        sends, _ = halve(ff, "sum_ff", None, (last, g_3))
        last = sends[0]
        hop(ff, sends, 1)
    dkv_2, g_2, dkv_1, g_1, dkv_0, g_0, vec_back, dq = back((2, 1, 0), (dqt, vec_back), True, (last,), g_3)
    g_2 = lax.ppermute(g_2, "spec", near)
    g_1 = lax.ppermute(g_1, "cube", pair)
    last = dq
    for level in range(2, levels):
        sends, _ = halve(ff, "sum_ff", None, (last, block_out))
        last = sends[0]
        hop(ff, sends, level)

    proj_a, proj_b, send_a, send_b, vectors = projection_step(
        ids, perm_mixed, dq, hiddens, [dkv_0, dkv_1, dkv_2, dkv_3], vec_mid, grad_up_bias, vec_back, (g_1, last)
    )
    proj = [
        Part(proj_a, lax.ppermute(send_a, "cube", pair)),
        Part(proj_b, lax.ppermute(send_b, "cube", pair)),
    ]
    aligned = width // cubes % 32 == 0
    far = flip(count, 2)
    last = vectors
    if aligned:
        columns = [(1, 0, hidden), (1, hidden, width), (0, 0, width)]
        ff_send, ff_own = pack(me, ff, columns, count, "pack_ff", None, (last,))
        last = ff_own
        ff_near = lax.ppermute(ff_send, "spec", near)
    for level in range(1, levels):
        sends, vectors = halve(proj, "sum_proj", vectors, (last,))
        last = sends[0]
        hop(proj, sends, level)
        if level == 1:
            grad_tokens, block_out = final_step(tok, first_gain, gmid, g_0, [g_1, g_2], block_out, (last,))
            last = grad_tokens
            grad_tokens = lax.ppermute(grad_tokens, axes, exchange)
    if aligned:
        (last,) = pack_far(ff_own, ff_near, "pack_ff_far", None, (last,))
        ff_far = lax.ppermute(last, "spec", far)
        pr_msgs, pr_own, vectors = pack_all(
            me, proj, [(0, 0, 3 * width), (1, 0, 3 * width)], count, "pack_proj", vectors, (last,)
        )
        pr_msgs = [lax.ppermute(m, "spec", flip(count, d + 1)) for d, m in enumerate(pr_msgs)]
        grad_up, grad_out, grad_down, grad_tokens = unpack(
            ff_own,
            ff_near,
            ff_far,
            [(width // cubes, hidden // count), (width // cubes, width // count), (hidden // cubes, width // count)],
            "unpack_ff",
            None,
            (pr_own,),
            2,
            grad_tokens,
        )
        grad_down = grad_down.T
        shape = (width // cubes, 3 * width // count)
        grad_proj, *vectors = unpack_all(pr_own, pr_msgs, shape, "unpack_proj", vectors, (grad_out,))
    else:
        grad_tokens = grad_tokens.astype(F32)
        vectors = vectors + joined(proj[0].terms[-1][-16:])
        vectors = sum([lax.ppermute(vectors, "spec", flip(count, d)) for d in range(1, count)], vectors)
        grad_up_out = ff[1].total()
        grad_up = spec_sum(grad_up_out[:, :hidden], spec, count)
        grad_out = spec_sum(grad_up_out[:, hidden:], spec, count)
        grad_down = spec_sum(ff[0].total(), spec, count)
        grad_proj = spec_sum(jnp.concatenate([p.total() for p in proj], 0), spec, count)
        vectors = [vectors[j, i * width : (i + 1) * width] for i in range(2) for j in range(4)] + [
            vectors[:4, 2 * width :].reshape(-1)
        ]

    return (
        block_out.reshape(tokens.shape),
        grad_tokens.reshape(tokens.shape),
        grad_proj,
        vectors[4],
        vectors[5],
        grad_out,
        vectors[3],
        grad_up,
        vectors[8],
        grad_down,
        vectors[0],
        vectors[6],
        vectors[7],
        vectors[1],
        vectors[2],
    )


def solution(mesh):
    return jax.shard_map(
        local,
        mesh=mesh,
        in_specs=(
            P("cube", "spec", None),
            P("cube", "spec", None),
            P("cube"),
        )
        + (P(),) * 13,
        out_specs=(
            P("cube", "spec", None),
            P("cube", "spec", None),
            P("cube", "spec"),
            P(),
            P(),
            P("cube", "spec"),
            P(),
            P("cube", "spec"),
            P(),
            P("cube", "spec"),
            P(),
            P(),
            P(),
            P(),
            P(),
        ),
        check_vma=False,
    )
```
